128 devices in a mesh: row: 16 (over x, y), col: 8 (over z, core).
Axes of the slice: x: 4, y: 4, z: 4, core: 2. Of those that a mesh axis runs over, the one named last changes fastest.
Arguments:
- density: bfloat16 [64, 64, 128, 128], P('row', 'col'), as said below
- basis: bfloat16 [384, 4, 256, 1024], P(('row', 'col')), may hold values from -6 to 6
- weights: float32 [384, 256], P(('row', 'col')), may hold values from 0.01 to 0.1
- batch_start: int32 [384], replicated, may hold values from 0 to 56
- batch_count: int32 [128], replicated, may hold values from 1 to 3, as said below
Outputs:
- potential: float32 [64, 64, 128, 128], P('row', 'col')
- energy: float32 [], replicated
The draws below stay inside these ranges and needn't reach their ends.
Inputs may be any that keep to these rules, and one draw needn't show every extreme that they name: Device d holds batch slots d * 3 to d * 3 + 2 and works on the first batch_count[d] of them; some device has 3. Batch k's significant shell blocks are the 8 consecutive blocks starting at batch_start[k]; the basis arrays list their functions in that order. density is symmetric: block (i, j) is the transpose of block (j, i).
All inputs are finite; a program needn't handle non-finite values.
Results may differ from the reference program's by a relative error of at most 0.0021.
Values may be sent and summed in bfloat16 or wider, within the bound.
No kernel may reach another device: no remote copies, remote signals or barrier semaphores. Data moves between devices by JAX's collectives and lax.ppermute only.
A program may use at most 128 MiB of HBM per device.

```python
import math
import jax
import jax.numpy as jnp
from jax import lax

BF = 128
KB = 8
NBLK = 64
G = 256
SLOTS = 3
KF = 1024
NB = 8192
BATCHES = 384
N_ROW = 16
N_COL = 8
DEVICES = 128


def draw_density(key, part):
    key = jax.random.fold_in(key, 11)
    shape = (NBLK, NBLK, BF, BF)
    full = jax.random.normal(key, shape, jnp.float32)
    full = full / (KB * BF)
    natural = 0.5 * (full + full.transpose(1, 0, 3, 2))
    owner = natural.reshape(NBLK // N_ROW, N_ROW, NBLK // N_COL, N_COL, BF, BF).transpose(1, 0, 3, 2, 4, 5)
    return owner.reshape(shape).astype(jnp.bfloat16)


def draw_batch_count(key, part):
    key = jax.random.fold_in(key, 23)
    first, second = jax.random.split(key)
    heavy = jax.random.randint(first, (DEVICES,), 0, 4)
    counts = jnp.where(heavy == 0, SLOTS, 1)
    chosen = jax.random.randint(second, (), 0, DEVICES)
    return counts.at[chosen].set(SLOTS).astype(jnp.int32)


def touch_ends(result, key, least, largest):
    longest = result.shape.index(max(result.shape))
    spots = []
    for shift in (0, 1):
        where = [jax.random.randint(jax.random.fold_in(key, axis), (), 0, length) for axis, length in enumerate(result.shape)]
        where[longest] = (where[longest] + shift) % result.shape[longest]
        spots.append(tuple(where))
    return result.at[spots[0]].set(least).at[spots[1]].set(largest)


def block_scale(key, shape, cuts, smallest, high):
    def one(dim, parts):
        heights = jax.random.uniform(jax.random.fold_in(jax.random.fold_in(key, 6), dim), (parts,), jnp.float32, smallest / len(cuts), high / len(cuts))
        return jnp.repeat(jnp.exp(heights), shape[dim] // parts).reshape((-1,) + (1,) * (len(shape) - dim - 1))

    loudness = one(*cuts[0])
    for cut in cuts[1:]:
        loudness = loudness * one(*cut)
    return loudness


def noise(key, extent, spread, most, cuts=(), kind=jnp.bfloat16):
    loudness = block_scale(key, extent, cuts, -0.22, 0.18) if cuts else 1.0
    drawn = jax.random.normal(key, extent, jnp.float32) * spread * loudness
    return jnp.minimum(jnp.maximum(drawn, -most), most).astype(kind)


def setup_inputs(seed: int = 0) -> dict:
    seeds = jax.random.split(jax.random.key(seed), 6)
    return {
        "density": draw_density(jax.random.fold_in(seeds[5], 71), 0),
        "basis": noise(seeds[1], (BATCHES, 4, G, KF), 1.0, 6.0, ((0, 128),)),
        "weights": jnp.clip(jnp.exp(math.log(0.1) - 2.3025851 * jax.random.uniform(seeds[2], (BATCHES, G), jnp.float32) ** block_scale(seeds[2], (BATCHES, G), ((0, 128),), -0.2, 0.2)), 0.01, 0.1),
        "batch_start": touch_ends(jax.random.randint(seeds[3], (BATCHES,), 0, NBLK - KB + 1), jax.random.fold_in(seeds[3], 1), 0, NBLK - KB).astype(jnp.int32),
        "batch_count": draw_batch_count(jax.random.fold_in(seeds[5], 71), 0),
    }


CX_CONST = 0.7385587663820224
MU_CONST = 0.2195149727645171
KAPPA_CONST = 0.804

def exchange_energy(density_value, gradient_square):
    square = density_value * density_value + 1.0
    scaled = square ** (2.0 / 3.0)
    reduced = gradient_square / square ** (4.0 / 3.0)
    factor = 1.0 + MU_CONST * reduced / (1.0 + MU_CONST * reduced / KAPPA_CONST)
    return -CX_CONST * scaled * factor

def batch_terms(phi_all, quad_weight, sub_matrix):
    values = phi_all[0]
    product = jnp.dot(values, sub_matrix, preferred_element_type=jnp.float32)
    density_value = lax.optimization_barrier(jnp.sum(values * product, axis=1))
    gradient = 2.0 * lax.optimization_barrier(jnp.sum(phi_all[1:4] * product[None], axis=2))
    gradient_square = lax.optimization_barrier(jnp.sum(gradient * gradient, axis=0))
    energy_point, pullback = jax.vjp(exchange_energy, density_value, gradient_square)
    weighted_rho, weighted_sigma = pullback(quad_weight)
    along = lax.optimization_barrier(jnp.sum(gradient[:, :, None] * phi_all[1:4], axis=0))
    kernel = (0.5 * weighted_rho[:, None] * values + 2.0 * weighted_sigma[:, None] * along).astype(jnp.bfloat16)
    half = jnp.dot(values.T, kernel, preferred_element_type=jnp.float32)
    return (half + half.T, jnp.sum(quad_weight * energy_point))

def to_natural(blocks):
    sectioned = blocks.reshape(N_ROW, NBLK // N_ROW, N_COL, NBLK // N_COL, BF, BF)
    return sectioned.transpose(1, 0, 3, 2, 4, 5).reshape(NBLK, NBLK, BF, BF)

def to_owner(blocks):
    sectioned = blocks.reshape(NBLK // N_ROW, N_ROW, NBLK // N_COL, N_COL, BF, BF)
    return sectioned.transpose(1, 0, 3, 2, 4, 5).reshape(NBLK, NBLK, BF, BF)

def reference(density, basis, weights, batch_start, batch_count):
    natural = to_natural(density).transpose(0, 2, 1, 3).reshape(NB, NB)
    width = KB * BF

    def step(index, carry):
        start = (batch_start[index] * BF).astype(jnp.int32)
        live = index % SLOTS < batch_count[index // SLOTS]

        def work(state):
            potential, energy = state
            sub_matrix = lax.dynamic_slice(natural, (start, start), (width, width))
            block, part_energy = batch_terms(basis[index], weights[index], sub_matrix)
            old = lax.dynamic_slice(potential, (start, start), (width, width))
            potential = lax.dynamic_update_slice(potential, old + block, (start, start))
            return (potential, energy + part_energy)

        def keep(state):
            return state
        return lax.cond(live, work, keep, carry)
    start_state = (jnp.zeros((NB, NB), jnp.float32), jnp.zeros((), jnp.float32))
    potential, energy = lax.fori_loop(0, DEVICES * SLOTS, step, start_state)
    blocks = potential.reshape(NBLK, BF, NBLK, BF).transpose(0, 2, 1, 3)
    return (to_owner(blocks), energy / NB)
```

```python
import functools

import jax
import jax.numpy as jnp
import numpy as np
from jax import lax
from jax.experimental import pallas as pl
from jax.experimental.pallas import tpu as pltpu
from jax.sharding import Mesh, PartitionSpec as P

CX = 0.7385587663820224
MU = 0.2195149727645171
KAPPA = 0.804
BF = 128
KB = 8
NBLK = 64
G = 256
SLOTS = 3
KF = 1024
N_ROW = 16
N_COL = 8
HALF = 64
MIB = 1024 * 1024
ROW = ("h", "xl", "y")
COL = ("z", "c")
ALL = ROW + COL
GROUP = ("xl", "y", "z", "c")
ANY = pl.BlockSpec(memory_space=pl.ANY)


def half_band_kernel(where, density, out, sems):
    copies = [
        pltpu.make_async_copy(density.at[a, where[a]], out.at[a], sems.at[a])
        for a in range(NBLK // N_ROW)
    ]
    for copy in copies:
        copy.start()
    for copy in copies:
        copy.wait()


def half_band(density, row_id, col_id):
    turns = jnp.arange(NBLK // N_ROW, dtype=jnp.int32)
    shift = jnp.mod(col_id - row_id, N_COL)
    where = jnp.minimum((row_id + N_ROW * turns + shift) // N_COL, NBLK // N_COL - 1)
    return pl.pallas_call(
        half_band_kernel,
        out_shape=jax.ShapeDtypeStruct((NBLK // N_ROW, BF, BF), jnp.bfloat16),
        grid_spec=pltpu.PrefetchScalarGridSpec(
            num_scalar_prefetch=1,
            grid=(),
            in_specs=[ANY],
            out_specs=ANY,
            scratch_shapes=[pltpu.SemaphoreType.DMA((NBLK // N_ROW,))],
        ),
        name="half_band",
    )(where.astype(jnp.int32), density)


def batch_kernel(
    scal, weights, basis, band, out, energy, phis, upper, mat, pair, stage, sem_b, sem_u, sem_o
):
    count = scal[SLOTS]

    def basis_copy(slot):
        return pltpu.make_async_copy(basis.at[slot], phis.at[slot], sem_b.at[slot])

    def row_copy(slot, o):
        i = scal[slot] + o
        return pltpu.make_async_copy(
            band.at[lax.rem(i, N_ROW), :, i // N_ROW], upper.at[slot, o], sem_u.at[slot, o]
        )

    def out_copy(slot):
        return pltpu.make_async_copy(stage.at[slot], out.at[:, slot], sem_o.at[slot])

    def fetch(slot, carry):
        basis_copy(slot).start()
        for o in range(KB):
            row_copy(slot, o).start()
        return carry

    lax.fori_loop(0, count, fetch, 0)

    def work(slot, total):
        start = scal[slot]
        for o in range(KB):
            row_copy(slot, o).wait()
        for o1 in range(KB):
            for o2 in range(o1, KB):
                block = upper[slot, o1, lax.rem(start + o2, KB)]
                mat[o1 * BF : (o1 + 1) * BF, o2 * BF : (o2 + 1) * BF] = block
                if o2 == o1 + 1 and o1 % 2 == 0:
                    mat[o2 * BF : (o2 + 1) * BF, o1 * BF : (o1 + 1) * BF] = block.T
        basis_copy(slot).wait()
        sums = [jnp.zeros((G, 1), jnp.float32) for _ in range(4)]
        for t in range(4):
            lo, hi = 256 * t, 256 * (t + 1)
            product = jnp.dot(
                phis[slot, 0, :, :hi], mat[:hi, lo:hi], preferred_element_type=jnp.float32
            )
            if hi < KF:
                product += lax.dot_general(
                    phis[slot, 0, :, hi:],
                    mat[lo:hi, hi:],
                    (((1,), (1,)), ((), ())),
                    preferred_element_type=jnp.float32,
                )
            for k in range(4):
                sums[k] += jnp.sum(
                    phis[slot, k, :, lo:hi].astype(jnp.float32) * product, axis=1, keepdims=True
                )
        rho = sums[0]
        grads = [2.0 * x for x in sums[1:]]
        sigma = grads[0] * grads[0] + grads[1] * grads[1] + grads[2] * grads[2]
        quad = weights[slot]
        square = rho * rho + 1.0
        logs = jnp.log(square)
        cube = jnp.exp(logs * (1.0 / 3.0))
        scaled = cube * cube
        reduced = sigma / (scaled * scaled)
        denom = 1.0 + MU * reduced / KAPPA
        factor = 1.0 + MU * reduced / denom
        slope = MU / denom / denom
        point = -CX * scaled * factor
        by_rho = (-CX * 2.0) * rho / cube * ((2.0 / 3.0) * factor - (4.0 / 3.0) * slope * reduced)
        by_sigma = -CX * slope / scaled
        wr = 0.5 * quad * by_rho
        ws = 2.0 * quad * by_sigma
        total = total + jnp.sum(quad * point)
        coeffs = [wr] + [ws * x for x in grads]
        for t in range(4):
            lo, hi = 256 * t, 256 * (t + 1)
            mixed = coeffs[0] * phis[slot, 0, :, lo:hi].astype(jnp.float32)
            for k in range(1, 4):
                mixed += coeffs[k] * phis[slot, k, :, lo:hi].astype(jnp.float32)
            pair[:G, lo:hi] = mixed.astype(jnp.bfloat16)
        pair[G:, :] = phis[slot, 0]
        for t in range(4):
            lo, hi = 256 * t, 256 * (t + 1)
            left = jnp.concatenate([pair[G:, lo:hi], pair[:G, lo:hi]], axis=0)
            rows = lax.dot_general(
                left, pair[...], (((0,), (0,)), ((), ())), preferred_element_type=jnp.float32
            ).astype(jnp.bfloat16)
            for k in range(2):
                a = lax.rem(start + 2 * t + k, KB)
                for o2 in range(KB):
                    b = lax.rem(start + o2, KB)
                    stage[slot, a * KB + b] = rows[
                        k * BF : (k + 1) * BF, o2 * BF : (o2 + 1) * BF
                    ]
        out_copy(slot).start()
        return total

    total = lax.fori_loop(0, count, work, jnp.float32(0.0))
    energy[...] = jnp.full(energy.shape, total, jnp.float32)

    def drain(slot, carry):
        out_copy(slot).wait()
        return carry

    lax.fori_loop(0, count, drain, 0)


def batches(scal, weights, basis, band):
    return pl.pallas_call(
        batch_kernel,
        out_shape=(
            jax.ShapeDtypeStruct((HALF, SLOTS, BF, BF), jnp.bfloat16),
            jax.ShapeDtypeStruct((1, BF), jnp.float32),
        ),
        grid_spec=pltpu.PrefetchScalarGridSpec(
            num_scalar_prefetch=1,
            grid=(),
            in_specs=[pl.BlockSpec(memory_space=pltpu.VMEM), ANY, ANY],
            out_specs=[ANY, pl.BlockSpec(memory_space=pltpu.VMEM)],
            scratch_shapes=[
                pltpu.VMEM((SLOTS, 4, G, KF), jnp.bfloat16),
                pltpu.VMEM((SLOTS, KB, KB, BF, BF), jnp.bfloat16),
                pltpu.VMEM((KF, KF), jnp.bfloat16),
                pltpu.VMEM((2 * G, KF), jnp.bfloat16),
                pltpu.VMEM((SLOTS, HALF, BF, BF), jnp.bfloat16),
                pltpu.SemaphoreType.DMA((SLOTS,)),
                pltpu.SemaphoreType.DMA((SLOTS, KB)),
                pltpu.SemaphoreType.DMA((SLOTS,)),
            ],
        ),
        compiler_params=pltpu.CompilerParams(vmem_limit_bytes=44 * MIB),
        name="batches",
    )(scal, weights, basis, band)


CHUNK = 8


def collect_kernel(scal, arrived, acc):
    step = pl.program_id(0)
    a, b, h = scal[HALF * (SLOTS + 1)], scal[HALF * (SLOTS + 1) + 1], scal[HALF * (SLOTS + 1) + 2]

    @pl.when(step == 0)
    def _():
        acc[...] = jnp.zeros(acc.shape, acc.dtype)

    def source(k, carry):
        peer = step * CHUNK + k

        def one(slot, inner):
            start = scal[peer * SLOTS + slot]
            i = start + lax.rem(a - start + NBLK, KB)
            j = start + lax.rem(b - start + NBLK, KB)
            below = jnp.where(j < i, 1, 0)
            turn = i // KB
            other = jnp.where(lax.rem(turn, 2) == h, 0, 1)
            acc[other, below, turn // 2] += arrived[k, slot].astype(jnp.float32)
            return inner

        lax.fori_loop(0, scal[HALF * SLOTS + peer], one, 0)
        return carry

    lax.fori_loop(0, CHUNK, source, 0)


def collect(scal, arrived):
    shape = (2, 2, NBLK // N_ROW, BF, BF)
    return pl.pallas_call(
        collect_kernel,
        out_shape=jax.ShapeDtypeStruct(shape, jnp.float32),
        grid_spec=pltpu.PrefetchScalarGridSpec(
            num_scalar_prefetch=1,
            grid=(HALF // CHUNK,),
            in_specs=[pl.BlockSpec((CHUNK, SLOTS, BF, BF), lambda s, _: (s, 0, 0, 0))],
            out_specs=pl.BlockSpec(shape, lambda s, _: (0, 0, 0, 0, 0)),
        ),
        compiler_params=pltpu.CompilerParams(vmem_limit_bytes=16 * MIB),
        name="collect",
    )(scal, arrived)


def place_kernel(scal, mine, theirs, out):
    turn = pl.program_id(0)
    row_id, shift = scal[0], scal[1]
    out[...] = jnp.zeros(out.shape, out.dtype)
    at = (row_id + N_ROW * turn + shift) // N_COL

    @pl.when(at < NBLK // N_COL)
    def _():
        out[0, at] = mine[0, 0] + theirs[0, 0]

    @pl.when((at > 0) & (shift > 0))
    def _():
        out[0, at - 1] = mine[1, 0] + theirs[1, 0]


def place(scal, mine, theirs):
    block = pl.BlockSpec((2, 1, BF, BF), lambda t, _: (0, t, 0, 0))
    return pl.pallas_call(
        place_kernel,
        out_shape=jax.ShapeDtypeStruct((NBLK // N_ROW, NBLK // N_COL, BF, BF), jnp.float32),
        grid_spec=pltpu.PrefetchScalarGridSpec(
            num_scalar_prefetch=1,
            grid=(NBLK // N_ROW,),
            in_specs=[block, block],
            out_specs=pl.BlockSpec((1, NBLK // N_COL, BF, BF), lambda t, _: (t, 0, 0, 0)),
        ),
        name="place",
    )(scal, mine, theirs)


def shards(density, basis, weights, batch_start, batch_count):
    row_id = lax.axis_index(ROW).astype(jnp.int32)
    col_id = lax.axis_index(COL).astype(jnp.int32)
    half_id = lax.axis_index("h").astype(jnp.int32)
    self_index = row_id * N_COL + col_id
    shift = jnp.mod(col_id - row_id, N_COL)

    band = lax.all_gather(half_band(density, row_id, col_id), ALL, axis=0, tiled=True)
    band = band.reshape(N_ROW, N_COL, NBLK // N_ROW, BF, BF)

    own_starts = lax.dynamic_slice(batch_start, (self_index * SLOTS,), (SLOTS,))
    own_count = lax.dynamic_slice(batch_count, (self_index,), (1,))
    scal = jnp.concatenate([own_starts, own_count])
    outgoing, energy = batches(scal, weights.reshape(SLOTS, G, 1), basis, band)

    energies = lax.all_gather(energy, ALL, axis=0, tiled=True)
    arrived = lax.all_to_all(outgoing, GROUP, split_axis=0, concat_axis=0, tiled=True)

    half_starts = lax.dynamic_slice(batch_start, (half_id * HALF * SLOTS,), (HALF * SLOTS,))
    half_counts = lax.dynamic_slice(batch_count, (half_id * HALF,), (HALF,))
    ids = jnp.stack([jnp.mod(row_id, KB), col_id, half_id])
    acc = collect(jnp.concatenate([half_starts, half_counts, ids]), arrived)
    theirs = lax.ppermute(acc[1], "h", [(0, 1), (1, 0)])
    potential = place(jnp.stack([row_id, shift]), acc[0], theirs)
    return potential, jnp.sum(energies[:, 0]) / (NBLK * BF)


def solution(mesh):
    fine = Mesh(np.asarray(mesh.devices).reshape(2, 2, 4, 4, 2), ALL)
    in_specs = (P(ROW, COL), P(ALL), P(ALL), P(), P())
    out_specs = (P(ROW, COL), P())
    return jax.shard_map(shards, mesh=fine, in_specs=in_specs, out_specs=out_specs, check_vma=False)
```

```python
import jax
import jax.numpy as jnp
import numpy as np
from jax import lax
from jax.experimental import pallas as pl
from jax.experimental.pallas import tpu as pltpu
from jax.sharding import Mesh, PartitionSpec as P

CX = 0.7385587663820224
MU = 0.2195149727645171
KAPPA = 0.804
BF = 128
KB = 8
NBLK = 64
G = 256
SLOTS = 3
KF = 1024
N_ROW = 16
N_COL = 8
TURNS = NBLK // N_ROW
PEERS = 64
MIB = 1024 * 1024
HB = BF // 2
EXT = SLOTS * HB
ROWS = EXT + 16
BAND = 2 * TURNS * HB
ROW = ("h", "xl", "y")
COL = ("z", "c")
ALL = ROW + COL
GROUP = ("xl", "y", "z", "c")
VMEM = pl.BlockSpec(memory_space=pltpu.VMEM)
HBM = pl.BlockSpec(memory_space=pltpu.HBM)
ANY = pl.BlockSpec(memory_space=pl.ANY)
F32 = jnp.float32
BF16 = jnp.bfloat16


def lanes(shape):
    return lax.broadcasted_iota(jnp.int32, shape, 0), lax.broadcasted_iota(jnp.int32, shape, 1)


def pack_symmetric(full):
    r, c = lanes((HB, BF))
    top, bottom = full[:HB], full[HB:]
    packed = jnp.where((c >= HB) | (r <= c), top, pltpu.roll(bottom, HB, 1))
    row = jnp.sum(jnp.where(c - HB == r, bottom, 0.0), axis=0, keepdims=True)
    return packed, row


def unpack_symmetric(packed, row):
    r, c = lanes((HB, BF))
    flip = jnp.concatenate([packed, packed], axis=0).T
    top = jnp.where((c >= HB) | (r <= c), packed, flip[:HB])
    corner = jnp.where(c - HB < r, pltpu.roll(packed, HB, 1), flip[:HB])
    corner = jnp.where(c - HB == r, row, corner)
    return jnp.concatenate([top, jnp.where(c < HB, flip[HB:], corner)], axis=0)


def pick_row(rows, index):
    r, _ = lanes(rows.shape)
    return jnp.sum(jnp.where(r == index, rows, 0.0), axis=0, keepdims=True)


def entry(scal, peer, slot):
    a, b, h = scal[PEERS * (SLOTS + 1)], scal[PEERS * (SLOTS + 1) + 1], scal[PEERS * (SLOTS + 1) + 2]
    start = scal[peer * SLOTS + slot]
    i = start + lax.rem(a - start + NBLK, KB)
    j = start + lax.rem(b - start + NBLK, KB)
    turn = i // KB
    other = jnp.where(lax.rem(turn, 2) == h, 0, 1)
    below = jnp.where(j < i, TURNS, 0)
    return other, turn // 2, pl.multiple_of((below + turn // 2) * HB, HB)


def share_kernel(scal, density, out):
    row_id, shift = scal[0], scal[1]
    row, _ = lanes((16, BF))
    out[BAND:, :] = jnp.zeros((16, BF), BF16)
    for t in range(TURNS):
        at = (row_id + N_ROW * t + shift) // N_COL
        low = TURNS * HB + t * HB

        @pl.when(shift > 0)
        def _():
            out[t * HB : (t + 1) * HB, :] = density[t, jnp.minimum(at, N_COL - 1), :HB, :]
            flip = density[t, jnp.maximum(at - 1, 0)].astype(F32).T
            out[low : low + HB, :] = flip[HB:].astype(BF16)

        @pl.when(shift == 0)
        def _():
            packed, line = pack_symmetric(density[t, at].astype(F32))
            out[t * HB : (t + 1) * HB, :] = packed.astype(BF16)
            out[low : low + HB, :] = jnp.zeros((HB, BF), BF16)
            old = out[BAND:, :].astype(F32)
            out[BAND:, :] = jnp.where(row == t, line, old).astype(BF16)


def share(scal, density):
    return pl.pallas_call(
        share_kernel,
        out_shape=jax.ShapeDtypeStruct((BAND + 16, BF), BF16),
        grid_spec=pltpu.PrefetchScalarGridSpec(
            num_scalar_prefetch=1, grid=(), in_specs=[VMEM], out_specs=VMEM
        ),
        name="share",
    )(scal, density)


CHUNK = 8


def pack_kernel(scal, mine, theirs, out, table, lines, buf, sems):
    table[0] = mine[:BAND, :]
    table[1] = theirs[:BAND, :]
    lines[0] = mine[BAND:, :].astype(F32)
    lines[1] = theirs[BAND:, :].astype(F32)
    row, _ = lanes((16, BF))

    def send(chunk):
        span = pl.ds(pl.multiple_of(chunk * CHUNK, CHUNK), CHUNK)
        return pltpu.make_async_copy(buf.at[span], out.at[span], sems.at[chunk])

    def one_chunk(chunk, carry):
        def one_peer(k, inner):
            peer = chunk * CHUNK + k

            def one(slot, ext):
                other, turn, at = entry(scal, peer, slot)
                buf[peer, pl.ds(pl.multiple_of(slot * HB, HB), HB), :] = table[
                    other, pl.ds(at, HB), :
                ]
                return jnp.where(row == slot, lines[other, pl.ds(turn, 1), :], ext)

            ext = lax.fori_loop(0, scal[PEERS * SLOTS + peer], one, jnp.zeros((16, BF), F32))
            buf[peer, EXT:, :] = ext.astype(BF16)
            return inner

        lax.fori_loop(0, CHUNK, one_peer, 0)
        send(chunk).start()
        return carry

    lax.fori_loop(0, PEERS // CHUNK, one_chunk, 0)

    def drain(chunk, carry):
        send(chunk).wait()
        return carry

    lax.fori_loop(0, PEERS // CHUNK, drain, 0)


def pack(scal, mine, theirs):
    return pl.pallas_call(
        pack_kernel,
        out_shape=jax.ShapeDtypeStruct((PEERS, ROWS, BF), BF16),
        grid_spec=pltpu.PrefetchScalarGridSpec(
            num_scalar_prefetch=1,
            grid=(),
            in_specs=[VMEM, VMEM],
            out_specs=HBM,
            scratch_shapes=[
                pltpu.VMEM((2, BAND, BF), BF16),
                pltpu.VMEM((2, 16, BF), F32),
                pltpu.VMEM((PEERS, ROWS, BF), BF16),
                pltpu.SemaphoreType.DMA((PEERS // CHUNK,)),
            ],
        ),
        compiler_params=pltpu.CompilerParams(vmem_limit_bytes=16 * MIB),
        name="pack",
    )(scal, mine, theirs)


def batch_kernel(
    scal, weights, basis, window, out,
    phis, win, win_ext, mat, pair, stage, stage_ext, lines, sem_b, sem_w, sem_o, sem_e,
):
    count = scal[SLOTS]
    row, lane = lanes((16, BF))

    def span(slot):
        return pl.ds(pl.multiple_of(slot * HB, HB), HB)

    def basis_copy(slot):
        return pltpu.make_async_copy(basis.at[slot], phis.at[slot], sem_b.at[slot])

    def window_copy(slot):
        return pltpu.make_async_copy(window.at[:, span(slot)], win.at[slot], sem_w.at[slot])

    def out_copy(slot):
        return pltpu.make_async_copy(stage.at[slot], out.at[:, span(slot)], sem_o.at[slot])

    ext_in = pltpu.make_async_copy(window.at[:, pl.ds(EXT, 16)], win_ext, sem_e.at[0])
    ext_out = pltpu.make_async_copy(stage_ext, out.at[:, pl.ds(EXT, 16)], sem_e.at[1])

    def fetch(slot, carry):
        window_copy(slot).start()
        basis_copy(slot).start()
        return carry

    ext_in.start()
    lax.fori_loop(0, count, fetch, 0)
    lines[...] = jnp.zeros(lines.shape, F32)
    ext_in.wait()

    def work(slot, total):
        start = scal[slot]
        cls = [lax.rem(start + o, KB) for o in range(KB)]
        window_copy(slot).wait()
        for o1 in range(KB):
            r1 = o1 * BF
            for o2 in range(o1 + 1, KB):
                top = win[slot, cls[o1] * KB + cls[o2]]
                bottom = win[slot, cls[o2] * KB + cls[o1]]
                mat[r1 : r1 + HB, o2 * BF : (o2 + 1) * BF] = top
                mat[r1 + HB : r1 + BF, o2 * BF : (o2 + 1) * BF] = bottom
                if o2 == o1 + 1 and o1 % 2 == 0:
                    mat[o2 * BF : (o2 + 1) * BF, r1 : r1 + BF] = jnp.concatenate(
                        [top, bottom], axis=0
                    ).T
            line = pick_row(win_ext[cls[o1] * (KB + 1)].astype(F32), slot)
            block = unpack_symmetric(win[slot, cls[o1] * (KB + 1)].astype(F32), line)
            mat[r1 : r1 + BF, r1 : r1 + BF] = block.astype(BF16)
        basis_copy(slot).wait()
        sums = [jnp.zeros((G, 1), F32) for _ in range(4)]
        for t in range(4):
            lo, hi = 256 * t, 256 * (t + 1)
            product = jnp.dot(phis[slot, 0, :, :hi], mat[:hi, lo:hi], preferred_element_type=F32)
            if hi < KF:
                product += lax.dot_general(
                    phis[slot, 0, :, hi:],
                    mat[lo:hi, hi:],
                    (((1,), (1,)), ((), ())),
                    preferred_element_type=F32,
                )
            for k in range(4):
                sums[k] += jnp.sum(
                    phis[slot, k, :, lo:hi].astype(F32) * product, axis=1, keepdims=True
                )
        rho = sums[0]
        grads = [2.0 * x for x in sums[1:]]
        sigma = grads[0] * grads[0] + grads[1] * grads[1] + grads[2] * grads[2]
        quad = weights[slot]
        square = rho * rho + 1.0
        logs = jnp.log(square)
        cube = jnp.exp(logs * (1.0 / 3.0))
        scaled = cube * cube
        reduced = sigma / (scaled * scaled)
        denom = 1.0 + MU * reduced / KAPPA
        factor = 1.0 + MU * reduced / denom
        slope = MU / denom / denom
        point = -CX * scaled * factor
        by_rho = (-CX * 2.0) * rho / cube * ((2.0 / 3.0) * factor - (4.0 / 3.0) * slope * reduced)
        by_sigma = -CX * slope / scaled
        wr = 0.5 * quad * by_rho
        ws = 2.0 * quad * by_sigma
        total = total + jnp.sum(quad * point)
        coeffs = [wr] + [ws * x for x in grads]
        for t in range(4):
            lo, hi = 256 * t, 256 * (t + 1)
            mixed = coeffs[0] * phis[slot, 0, :, lo:hi].astype(F32)
            for k in range(1, 4):
                mixed += coeffs[k] * phis[slot, k, :, lo:hi].astype(F32)
            pair[:G, lo:hi] = mixed.astype(BF16)
        pair[G:, :] = phis[slot, 0]
        for t in range(4):
            lo, hi = 256 * t, 256 * (t + 1)
            left = jnp.concatenate([pair[G:, lo:hi], pair[:G, lo:hi]], axis=0)
            rows = lax.dot_general(
                left, pair[:, lo:], (((0,), (0,)), ((), ())), preferred_element_type=F32
            )
            for k in range(2):
                o1 = 2 * t + k
                for o2 in range(o1, KB):
                    c0 = o2 * BF - lo
                    block = rows[k * BF : (k + 1) * BF, c0 : c0 + BF]
                    if o2 == o1:
                        packed, line = pack_symmetric(block)
                        stage[slot, cls[o1] * (KB + 1)] = packed.astype(BF16)
                        lines[cls[o1]] = jnp.where(row == slot, line, lines[cls[o1]])
                    else:
                        stage[slot, cls[o1] * KB + cls[o2]] = block[:HB].astype(BF16)
                        stage[slot, cls[o2] * KB + cls[o1]] = block[HB:].astype(BF16)
        out_copy(slot).start()
        return total

    total = jnp.full((16, BF), lax.fori_loop(0, count, work, jnp.float32(0.0)), F32)
    first = total.astype(BF16).astype(F32)
    second = (total - first).astype(BF16).astype(F32)
    third = total - first - second
    spread = jnp.where(lane == 0, first, jnp.where(lane == 1, second, third))
    energy = jnp.where((row == 0) & (lane < 3), spread, 0.0)
    for peer in range(PEERS):
        if peer % (KB + 1) == 0:
            stage_ext[peer] = (lines[peer // (KB + 1)] + energy).astype(BF16)
        else:
            stage_ext[peer] = energy.astype(BF16)
    ext_out.start()

    def drain(slot, carry):
        out_copy(slot).wait()
        return carry

    lax.fori_loop(0, count, drain, 0)
    ext_out.wait()


def batches(scal, weights, basis, window):
    return pl.pallas_call(
        batch_kernel,
        out_shape=jax.ShapeDtypeStruct((PEERS, ROWS, BF), BF16),
        grid_spec=pltpu.PrefetchScalarGridSpec(
            num_scalar_prefetch=1,
            grid=(),
            in_specs=[VMEM, ANY, ANY],
            out_specs=HBM,
            scratch_shapes=[
                pltpu.VMEM((SLOTS, 4, G, KF), BF16),
                pltpu.VMEM((SLOTS, PEERS, HB, BF), BF16),
                pltpu.VMEM((PEERS, 16, BF), BF16),
                pltpu.VMEM((KF, KF), BF16),
                pltpu.VMEM((2 * G, KF), BF16),
                pltpu.VMEM((SLOTS, PEERS, HB, BF), BF16),
                pltpu.VMEM((PEERS, 16, BF), BF16),
                pltpu.VMEM((KB, 16, BF), F32),
                pltpu.SemaphoreType.DMA((SLOTS,)),
                pltpu.SemaphoreType.DMA((SLOTS,)),
                pltpu.SemaphoreType.DMA((SLOTS,)),
                pltpu.SemaphoreType.DMA((2,)),
            ],
        ),
        compiler_params=pltpu.CompilerParams(vmem_limit_bytes=40 * MIB),
        name="batches",
    )(scal, weights, basis, window)


def collect_kernel(scal, arrived, mine, other_out, acc, lines, energy):
    step = pl.program_id(0)
    row, lane = lanes((16, BF))
    on_diagonal = scal[PEERS * (SLOTS + 1)] == scal[PEERS * (SLOTS + 1) + 1]

    @pl.when(step == 0)
    def _():
        acc[...] = jnp.zeros(acc.shape, F32)
        lines[...] = jnp.zeros(lines.shape, F32)
        energy[...] = jnp.zeros(energy.shape, F32)

    def source(k, carry):
        peer = step * CHUNK + k
        ext = arrived[k, EXT:, :].astype(F32)
        energy[...] += jnp.where((row == 0) & (lane < 3), ext, 0.0)

        def one(slot, inner):
            other, turn, at = entry(scal, peer, slot)
            part = arrived[k, pl.ds(pl.multiple_of(slot * HB, HB), HB), :]
            acc[other, pl.ds(at, HB), :] += part.astype(F32)

            @pl.when(on_diagonal)
            def _():
                line = jnp.where((row == slot) & (lane >= HB), ext, 0.0)
                lines[other, pl.ds(turn, 1), :] += jnp.sum(line, axis=0, keepdims=True)

            return inner

        lax.fori_loop(0, scal[PEERS * SLOTS + peer], one, 0)
        return carry

    lax.fori_loop(0, CHUNK, source, 0)

    @pl.when(step == PEERS // CHUNK - 1)
    def _():
        total = jnp.sum(jnp.sum(energy[...], axis=0, keepdims=True), axis=1, keepdims=True)
        eight, _ = lanes((8, BF))
        mine[:BAND, :] = acc[0]
        other_out[:BAND, :] = acc[1]
        mine[BAND:, :] = jnp.where(eight == TURNS, total, lines[0])
        other_out[BAND:, :] = jnp.where(eight == TURNS, total, lines[1])


def collect(scal, arrived):
    shape = (BAND + 8, BF)
    return pl.pallas_call(
        collect_kernel,
        out_shape=[jax.ShapeDtypeStruct(shape, F32)] * 2,
        grid_spec=pltpu.PrefetchScalarGridSpec(
            num_scalar_prefetch=1,
            grid=(PEERS // CHUNK,),
            in_specs=[pl.BlockSpec((CHUNK, ROWS, BF), lambda s, _: (s, 0, 0))],
            out_specs=[pl.BlockSpec(shape, lambda s, _: (0, 0))] * 2,
            scratch_shapes=[
                pltpu.VMEM((2, BAND, BF), F32),
                pltpu.VMEM((2, 8, BF), F32),
                pltpu.VMEM((16, BF), F32),
            ],
        ),
        compiler_params=pltpu.CompilerParams(vmem_limit_bytes=16 * MIB),
        name="collect",
    )(scal, arrived)


def merge_kernel(mine, theirs, upper, lower, rest):
    upper[...] = mine[: TURNS * HB, :] + theirs[: TURNS * HB, :]
    lower[...] = mine[TURNS * HB : BAND, :] + theirs[TURNS * HB : BAND, :]
    rest[...] = mine[BAND:, :] + theirs[BAND:, :]


def merge(mine, theirs):
    half = jax.ShapeDtypeStruct((TURNS * HB, BF), F32)
    return pl.pallas_call(
        merge_kernel,
        out_shape=[half, half, jax.ShapeDtypeStruct((8, BF), F32)],
        in_specs=[VMEM, VMEM],
        out_specs=[VMEM, VMEM, VMEM],
        name="merge",
    )(mine, theirs)


def place_kernel(scal, upper, lower, rest, got_upper, got_lower, out):
    t = pl.program_id(0)
    row_id, shift = scal[0], scal[1]
    out[...] = jnp.zeros(out.shape, F32)
    at = (row_id + N_ROW * t + shift) // N_COL

    def part(ref, turn):
        return ref[pl.ds(pl.multiple_of(turn * HB, HB), HB), :]

    @pl.when((shift > 0) & (at < N_COL))
    def _():
        turn = t + jnp.where(row_id + shift >= N_ROW, 1, 0)
        out[0, at, :HB, :] = part(upper, t)
        out[0, at, HB:, :] = part(got_lower, jnp.minimum(turn, TURNS - 1))

    @pl.when((shift > 0) & (at > 0))
    def _():
        turn = t - jnp.where(row_id + shift < N_COL, 1, 0)
        both = jnp.concatenate([part(got_upper, jnp.maximum(turn, 0)), part(lower, t)], axis=0)
        out[0, at - 1] = both.T

    @pl.when(shift == 0)
    def _():
        out[0, at] = unpack_symmetric(part(upper, t), rest[pl.ds(t, 1), :])


def place(scal, upper, lower, rest, got_upper, got_lower):
    return pl.pallas_call(
        place_kernel,
        out_shape=jax.ShapeDtypeStruct((TURNS, N_COL, BF, BF), F32),
        grid_spec=pltpu.PrefetchScalarGridSpec(
            num_scalar_prefetch=1,
            grid=(TURNS,),
            in_specs=[VMEM] * 5,
            out_specs=pl.BlockSpec((1, N_COL, BF, BF), lambda t, _: (t, 0, 0, 0)),
        ),
        name="place",
    )(scal, upper, lower, rest, got_upper, got_lower)


def mirror_pairs():
    pairs = []
    for row in range(N_ROW):
        for col in range(N_COL):
            shift = (col - row) % N_COL
            pairs.append((row * N_COL + col, (row + shift) % N_ROW * N_COL + row % N_COL))
    return pairs


def shards(density, basis, weights, batch_start, batch_count):
    row_id = lax.axis_index(ROW).astype(jnp.int32)
    col_id = lax.axis_index(COL).astype(jnp.int32)
    half_id = lax.axis_index("h").astype(jnp.int32)
    self_index = row_id * N_COL + col_id
    where = jnp.stack([row_id, jnp.mod(col_id - row_id, N_COL)])
    half_starts = lax.dynamic_slice(batch_start, (half_id * PEERS * SLOTS,), (PEERS * SLOTS,))
    half_counts = lax.dynamic_slice(batch_count, (half_id * PEERS,), (PEERS,))
    ids = jnp.stack([jnp.mod(row_id, KB), col_id, half_id])
    plan = jnp.concatenate([half_starts, half_counts, ids])
    own_starts = lax.dynamic_slice(batch_start, (self_index * SLOTS,), (SLOTS,))
    own_count = lax.dynamic_slice(batch_count, (self_index,), (1,))
    scal = jnp.concatenate([own_starts, own_count])
    swap = [(0, 1), (1, 0)]

    held = share(where, density)
    packed = pack(plan, held, lax.ppermute(held, "h", swap))
    window = lax.all_to_all(packed, GROUP, split_axis=0, concat_axis=0, tiled=True)

    outgoing = batches(scal, weights.reshape(SLOTS, G, 1), basis, window)
    arrived = lax.all_to_all(outgoing, GROUP, split_axis=0, concat_axis=0, tiled=True)

    mine, other = collect(plan, arrived)
    upper, lower, rest = merge(mine, lax.ppermute(other, "h", swap))
    there = mirror_pairs()
    got_upper = lax.ppermute(upper, ALL, there)
    got_lower = lax.ppermute(lower, ALL, [(d, s) for s, d in there])
    potential = place(where, upper, lower, rest, got_upper, got_lower)
    return potential, rest[TURNS, 0] / (NBLK * BF)


def solution(mesh):
    fine = Mesh(np.asarray(mesh.devices).reshape(2, 2, 4, 4, 2), ALL)
    in_specs = (P(ROW, COL), P(ALL), P(ALL), P(), P())
    out_specs = (P(ROW, COL), P())
    return jax.shard_map(shards, mesh=fine, in_specs=in_specs, out_specs=out_specs, check_vma=False)
```

```python
import functools

import jax
import jax.numpy as jnp
import numpy as np
from jax import lax
from jax.experimental import pallas as pl
from jax.experimental.pallas import tpu as pltpu
from jax.sharding import Mesh, PartitionSpec as P

CX = 0.7385587663820224
MU = 0.2195149727645171
KAPPA = 0.804
BF = 128
KB = 8
NBLK = 64
G = 256
SLOTS = 3
KF = 1024
N_ROW = 16
N_COL = 8
TURNS = NBLK // N_ROW
PEERS = 64
MIB = 1024 * 1024
HB = BF // 2
EXT = SLOTS * HB
ROWS = EXT + 16
BAND = 2 * TURNS * HB
ROW = ("h", "xl", "y")
COL = ("z", "c")
ALL = ROW + COL
GROUP = ("xl", "y", "z", "c")
VMEM = pl.BlockSpec(memory_space=pltpu.VMEM)
HBM = pl.BlockSpec(memory_space=pltpu.HBM)
F32 = jnp.float32
BF16 = jnp.bfloat16


def lanes(shape):
    return lax.broadcasted_iota(jnp.int32, shape, 0), lax.broadcasted_iota(jnp.int32, shape, 1)


def pack_symmetric(full):
    r, c = lanes((HB, BF))
    top, bottom = full[:HB], full[HB:]
    packed = jnp.where((c >= HB) | (r <= c), top, pltpu.roll(bottom, HB, 1))
    row = jnp.sum(jnp.where(c - HB == r, bottom, 0.0), axis=0, keepdims=True)
    return packed, row


def unpack_symmetric(packed, row):
    r, c = lanes((HB, BF))
    flip = jnp.concatenate([packed, packed], axis=0).T
    top = jnp.where((c >= HB) | (r <= c), packed, flip[:HB])
    corner = jnp.where(c - HB < r, pltpu.roll(packed, HB, 1), flip[:HB])
    corner = jnp.where(c - HB == r, row, corner)
    return jnp.concatenate([top, jnp.where(c < HB, flip[HB:], corner)], axis=0)


def pick_row(rows, index):
    r, _ = lanes(rows.shape)
    return jnp.sum(jnp.where(r == index, rows, 0.0), axis=0, keepdims=True)


def position():
    h = lax.axis_index("h")
    row_id = (h * 2 + lax.axis_index("xl")) * 4 + lax.axis_index("y")
    return row_id, lax.axis_index("z") * 2 + lax.axis_index("c"), h


def entry(starts, peer, slot, where):
    row_id, col_id, h = where
    start = starts[(h * PEERS + peer) * SLOTS + slot]
    i = start + ((row_id - start) & (KB - 1))
    j = start + ((col_id - start) & (KB - 1))
    other = ((i >> 3) & 1) ^ h
    turn = i >> 4
    below = jnp.where(j < i, TURNS, 0)
    return other, turn, pl.multiple_of((below + turn) * HB, HB)


def scalars(count, in_specs, out_specs, scratch_shapes=()):
    return pltpu.PrefetchScalarGridSpec(
        num_scalar_prefetch=count,
        grid=(),
        in_specs=in_specs,
        out_specs=out_specs,
        scratch_shapes=list(scratch_shapes),
    )


def limit(mib):
    return pltpu.CompilerParams(vmem_limit_bytes=mib * MIB)


def share_kernel(density, out, copy, ups, lows, sems):
    row_id, col_id, _ = position()
    shift = (col_id - row_id) & (N_COL - 1)
    row, _ = lanes((16, BF))
    loads = []
    for t in range(TURNS):
        at = (row_id + N_ROW * t + shift) >> 3
        up = density.at[t, jnp.minimum(at, N_COL - 1)]
        low = density.at[t, jnp.maximum(at - 1, 0)]
        loads.append(pltpu.make_async_copy(up, ups.at[t], sems.at[t]))
        loads.append(pltpu.make_async_copy(low, lows.at[t], sems.at[TURNS + t]))
    for load in loads:
        load.start()
    for load in loads:
        load.wait()

    @pl.when(shift > 0)
    def _():
        for t in range(TURNS):
            low = TURNS * HB + t * HB
            out[t * HB : (t + 1) * HB, :] = ups[t, :HB, :]
            out[low : low + HB, :] = lows[t].astype(F32).T[HB:].astype(BF16)
        out[BAND:, :] = jnp.zeros((16, BF), BF16)

    @pl.when(shift == 0)
    def _():
        ext = jnp.zeros((16, BF), F32)
        for t in range(TURNS):
            packed, line = pack_symmetric(ups[t].astype(F32))
            out[t * HB : (t + 1) * HB, :] = packed.astype(BF16)
            ext = jnp.where(row == t, line, ext)
        out[TURNS * HB : BAND, :] = jnp.zeros((TURNS * HB, BF), BF16)
        out[BAND:, :] = ext.astype(BF16)

    copy[...] = out[...]


def share(density):
    held = jax.ShapeDtypeStruct((BAND + 16, BF), BF16)
    return pl.pallas_call(
        share_kernel,
        out_shape=[held, held],
        in_specs=[HBM],
        out_specs=[VMEM, VMEM],
        scratch_shapes=[
            pltpu.VMEM((TURNS, BF, BF), BF16),
            pltpu.VMEM((TURNS, BF, BF), BF16),
            pltpu.SemaphoreType.DMA((2 * TURNS,)),
        ],
        compiler_params=limit(4),
        name="share",
    )(density)


CHUNK = 8


def pack_kernel(starts, counts, mine, theirs, out, table, lines, buf, sems):
    where = position()
    on_diagonal = ((where[1] - where[0]) & (KB - 1)) == 0
    table[0] = mine[:BAND, :]
    table[1] = theirs[:BAND, :]
    lines[0] = mine[BAND:, :].astype(F32)
    lines[1] = theirs[BAND:, :].astype(F32)
    row, _ = lanes((16, BF))

    def send(chunk):
        span = pl.ds(pl.multiple_of(chunk * CHUNK, CHUNK), CHUNK)
        return pltpu.make_async_copy(buf.at[span], out.at[span], sems.at[chunk])

    def one_chunk(chunk, carry):
        for k in range(CHUNK):
            peer = chunk * CHUNK + k
            count = counts[where[2] * PEERS + peer]

            def one(slot):
                other, _, at = entry(starts, peer, slot, where)
                buf[peer, slot * HB : (slot + 1) * HB, :] = table[other, pl.ds(at, HB), :]

            one(0)
            for slot in range(1, SLOTS):
                pl.when(slot < count)(lambda slot=slot: one(slot))

            @pl.when(on_diagonal)
            def _():
                ext = jnp.zeros((16, BF), F32)
                for slot in range(SLOTS):
                    other, turn, _ = entry(starts, peer, slot, where)
                    ext = jnp.where(row == slot, lines[other, pl.ds(turn, 1), :], ext)
                buf[peer, EXT:, :] = ext.astype(BF16)

        send(chunk).start()
        return carry

    lax.fori_loop(0, PEERS // CHUNK, one_chunk, 0)

    def drain(chunk, carry):
        send(chunk).wait()
        return carry

    lax.fori_loop(0, PEERS // CHUNK, drain, 0)


def pack(starts, counts, mine, theirs):
    return pl.pallas_call(
        pack_kernel,
        out_shape=jax.ShapeDtypeStruct((PEERS, ROWS, BF), BF16),
        grid_spec=scalars(
            2,
            [VMEM, VMEM],
            HBM,
            [
                pltpu.VMEM((2, BAND, BF), BF16),
                pltpu.VMEM((2, 16, BF), F32),
                pltpu.VMEM((PEERS, ROWS, BF), BF16),
                pltpu.SemaphoreType.DMA((PEERS // CHUNK,)),
            ],
        ),
        compiler_params=limit(8),
        name="pack",
    )(starts, counts, mine, theirs)


def batch_kernel(
    starts, counts, weights, basis, window, out, quads, phis, mat, pair, lines, sem_w, sem_b
):
    row_id, col_id, _ = position()
    me = row_id * N_COL + col_id
    count = counts[me]
    row, lane = lanes((16, BF))
    weights_copy = pltpu.make_async_copy(weights, quads, sem_w)

    def basis_copy(slot):
        return pltpu.make_async_copy(basis.at[slot], phis.at[slot], sem_b.at[slot])

    def fetch(slot, carry):
        basis_copy(slot).start()
        return carry

    weights_copy.start()
    lax.fori_loop(0, count, fetch, 0)
    lines[...] = jnp.zeros(lines.shape, F32)
    weights_copy.wait()

    def work(slot, total):
        start = starts[me * SLOTS + slot]
        cls = [(start + o) & (KB - 1) for o in range(KB)]
        span = pl.ds(pl.multiple_of(slot * HB, HB), HB)
        for o1 in range(KB):
            r1 = o1 * BF
            for o2 in range(o1 + 1, KB):
                top = window[cls[o1] * KB + cls[o2], span, :]
                bottom = window[cls[o2] * KB + cls[o1], span, :]
                mat[r1 : r1 + HB, o2 * BF : (o2 + 1) * BF] = top
                mat[r1 + HB : r1 + BF, o2 * BF : (o2 + 1) * BF] = bottom
                if o2 == o1 + 1 and o1 % 2 == 0:
                    mat[o2 * BF : (o2 + 1) * BF, r1 : r1 + BF] = jnp.concatenate(
                        [top, bottom], axis=0
                    ).T
            diagonal = cls[o1] * (KB + 1)
            line = pick_row(window[diagonal, EXT:, :].astype(F32), slot)
            block = unpack_symmetric(window[diagonal, span, :].astype(F32), line)
            mat[r1 : r1 + BF, r1 : r1 + BF] = block.astype(BF16)
        basis_copy(slot).wait()
        sums = [jnp.zeros((G, 1), F32) for _ in range(4)]
        for t in range(4):
            lo, hi = 256 * t, 256 * (t + 1)
            product = jnp.dot(phis[slot, 0, :, :hi], mat[:hi, lo:hi], preferred_element_type=F32)
            if hi < KF:
                product += lax.dot_general(
                    phis[slot, 0, :, hi:],
                    mat[lo:hi, hi:],
                    (((1,), (1,)), ((), ())),
                    preferred_element_type=F32,
                )
            for k in range(4):
                sums[k] += jnp.sum(
                    phis[slot, k, :, lo:hi].astype(F32) * product, axis=1, keepdims=True
                )
        rho = sums[0]
        grads = [2.0 * x for x in sums[1:]]
        sigma = grads[0] * grads[0] + grads[1] * grads[1] + grads[2] * grads[2]
        quad = quads[slot]
        square = rho * rho + 1.0
        logs = jnp.log(square)
        cube = jnp.exp(logs * (1.0 / 3.0))
        scaled = cube * cube
        reduced = sigma / (scaled * scaled)
        denom = 1.0 + MU * reduced / KAPPA
        factor = 1.0 + MU * reduced / denom
        slope = MU / denom / denom
        point = -CX * scaled * factor
        by_rho = (-CX * 2.0) * rho / cube * ((2.0 / 3.0) * factor - (4.0 / 3.0) * slope * reduced)
        by_sigma = -CX * slope / scaled
        wr = 0.5 * quad * by_rho
        ws = 2.0 * quad * by_sigma
        total = total + jnp.sum(quad * point)
        coeffs = [wr] + [ws * x for x in grads]
        for t in range(4):
            lo, hi = 256 * t, 256 * (t + 1)
            mixed = coeffs[0] * phis[slot, 0, :, lo:hi].astype(F32)
            for k in range(1, 4):
                mixed += coeffs[k] * phis[slot, k, :, lo:hi].astype(F32)
            pair[:G, lo:hi] = mixed.astype(BF16)
        pair[G:, :] = phis[slot, 0]
        for t in range(4):
            lo, hi = 256 * t, 256 * (t + 1)
            left = jnp.concatenate([pair[G:, lo:hi], pair[:G, lo:hi]], axis=0)
            rows = lax.dot_general(
                left, pair[:, lo:], (((0,), (0,)), ((), ())), preferred_element_type=F32
            )
            for k in range(2):
                o1 = 2 * t + k
                for o2 in range(o1, KB):
                    c0 = o2 * BF - lo
                    block = rows[k * BF : (k + 1) * BF, c0 : c0 + BF]
                    if o2 == o1:
                        packed, line = pack_symmetric(block)
                        out[cls[o1] * (KB + 1), span, :] = packed.astype(BF16)
                        lines[cls[o1]] = jnp.where(row == slot, line, lines[cls[o1]])
                    else:
                        out[cls[o1] * KB + cls[o2], span, :] = block[:HB].astype(BF16)
                        out[cls[o2] * KB + cls[o1], span, :] = block[HB:].astype(BF16)
        return total

    total = jnp.full((16, BF), lax.fori_loop(0, count, work, jnp.float32(0.0)), F32)
    first = total.astype(BF16).astype(F32)
    second = (total - first).astype(BF16).astype(F32)
    third = total - first - second
    spread = jnp.where(lane == 0, first, jnp.where(lane == 1, second, third))
    energy = jnp.where((row == 0) & (lane < 3), spread, 0.0)
    for peer in range(PEERS):
        if peer % (KB + 1) == 0:
            out[peer, EXT:, :] = (lines[peer // (KB + 1)] + energy).astype(BF16)
        else:
            out[peer, EXT:, :] = energy.astype(BF16)


def batches(starts, counts, weights, basis, window):
    return pl.pallas_call(
        batch_kernel,
        out_shape=jax.ShapeDtypeStruct((PEERS, ROWS, BF), BF16),
        grid_spec=scalars(
            2,
            [HBM, HBM, VMEM],
            VMEM,
            [
                pltpu.VMEM((SLOTS, G, 1), F32),
                pltpu.VMEM((SLOTS, 4, G, KF), BF16),
                pltpu.VMEM((KF, KF), BF16),
                pltpu.VMEM((2 * G, KF), BF16),
                pltpu.VMEM((KB, 16, BF), F32),
                pltpu.SemaphoreType.DMA,
                pltpu.SemaphoreType.DMA((SLOTS,)),
            ],
        ),
        compiler_params=limit(32),
        name="batches",
    )(starts, counts, weights, basis, window)


def collect_kernel(which, starts, counts, arrived, out, energy):
    where = position()
    on_diagonal = ((where[1] - where[0]) & (KB - 1)) == 0
    row, lane = lanes((16, BF))
    eight, _ = lanes((8, BF))
    out[...] = jnp.zeros(out.shape, F32)
    energy[...] = jnp.zeros(energy.shape, F32)

    def one_chunk(chunk, carry):
        for k in range(CHUNK):
            peer = chunk * CHUNK + k
            count = counts[where[2] * PEERS + peer]
            if which:
                energy[...] += arrived[peer, EXT:, :].astype(F32)

            def one(slot, live):
                other, turn, at = entry(starts, peer, slot, where)
                wanted = other == which

                @pl.when(wanted if live is None else wanted & live)
                def _():
                    part = arrived[peer, slot * HB : (slot + 1) * HB, :]
                    out[pl.ds(at, HB), :] += part.astype(F32)

                    @pl.when(on_diagonal)
                    def _():
                        ext = arrived[peer, EXT:, :].astype(F32)
                        line = jnp.where((row == slot) & (lane >= HB), ext, 0.0)
                        line = jnp.sum(line, axis=0, keepdims=True)
                        out[BAND:, :] += jnp.where(eight == turn, line, 0.0)

            one(0, None)
            for slot in range(1, SLOTS):
                one(slot, slot < count)
        return carry

    lax.fori_loop(0, PEERS // CHUNK, one_chunk, 0)
    if which:
        total = jnp.where((row == 0) & (lane < 3), energy[...], 0.0)
        total = jnp.sum(jnp.sum(total, axis=0, keepdims=True), axis=1, keepdims=True)
        out[BAND:, :] = jnp.where(eight == TURNS, total, out[BAND:, :])


def collect(which, starts, counts, arrived):
    return pl.pallas_call(
        functools.partial(collect_kernel, which),
        out_shape=jax.ShapeDtypeStruct((BAND + 8, BF), F32),
        grid_spec=scalars(2, [VMEM], VMEM, [pltpu.VMEM((16, BF), F32)]),
        compiler_params=limit(8),
        cost_estimate=pl.CostEstimate(flops=10**6, bytes_accessed=4 * MIB, transcendentals=0),
        name=("collect_own", "collect_other")[which],
    )(starts, counts, arrived)


def merge_kernel(mine, sent, theirs, upper, lower, rest):
    eight, _ = lanes((8, BF))
    upper[...] = mine[: TURNS * HB, :] + theirs[: TURNS * HB, :]
    lower[...] = mine[TURNS * HB : BAND, :] + theirs[TURNS * HB : BAND, :]
    half = jnp.where(eight == TURNS, sent[BAND:, :], mine[BAND:, :])
    rest[...] = half + theirs[BAND:, :]


def merge(mine, sent, theirs):
    half = jax.ShapeDtypeStruct((TURNS * HB, BF), F32)
    return pl.pallas_call(
        merge_kernel,
        out_shape=[half, half, jax.ShapeDtypeStruct((8, BF), F32)],
        in_specs=[VMEM] * 3,
        out_specs=[VMEM] * 3,
        compiler_params=limit(4),
        name="merge",
    )(mine, sent, theirs)


def place_kernel(upper, lower, rest, got_upper, got_lower, blank, out, blocks, sems):
    del blank
    row_id, col_id, _ = position()
    shift = (col_id - row_id) & (N_COL - 1)

    def part(ref, turn):
        return ref[pl.ds(pl.multiple_of(turn * HB, HB), HB), :]

    def write(t, low, at):
        slot = TURNS * low + t
        return pltpu.make_async_copy(blocks.at[slot], out.at[t, at], sems.at[slot])

    for finish in (False, True):
        for t in range(TURNS):
            at = (row_id + N_ROW * t + shift) >> 3

            @pl.when((shift > 0) & (at < N_COL))
            def _():
                if finish:
                    write(t, 0, at).wait()
                else:
                    turn = t + jnp.where(row_id + shift >= N_ROW, 1, 0)
                    blocks[t, :HB, :] = part(upper, t)
                    blocks[t, HB:, :] = part(got_lower, jnp.minimum(turn, TURNS - 1))
                    write(t, 0, at).start()

            @pl.when((shift > 0) & (at > 0))
            def _():
                if finish:
                    write(t, 1, at - 1).wait()
                else:
                    turn = t - jnp.where(row_id + shift < N_COL, 1, 0)
                    top = part(got_upper, jnp.maximum(turn, 0))
                    blocks[TURNS + t] = jnp.concatenate([top, part(lower, t)], axis=0).T
                    write(t, 1, at - 1).start()

            @pl.when(shift == 0)
            def _():
                if finish:
                    write(t, 0, at).wait()
                else:
                    blocks[t] = unpack_symmetric(part(upper, t), rest[t : t + 1, :])
                    write(t, 0, at).start()


def place(upper, lower, rest, got_upper, got_lower, blank):
    return pl.pallas_call(
        place_kernel,
        out_shape=jax.ShapeDtypeStruct((TURNS, N_COL, BF, BF), F32),
        in_specs=[VMEM] * 5 + [HBM],
        out_specs=HBM,
        scratch_shapes=[
            pltpu.VMEM((2 * TURNS, BF, BF), F32),
            pltpu.SemaphoreType.DMA((2 * TURNS,)),
        ],
        input_output_aliases={5: 0},
        compiler_params=limit(4),
        name="place",
    )(upper, lower, rest, got_upper, got_lower, blank)


def mirror_pairs():
    pairs = []
    for row in range(N_ROW):
        for col in range(N_COL):
            shift = (col - row) % N_COL
            pairs.append((row * N_COL + col, (row + shift) % N_ROW * N_COL + row % N_COL))
    return pairs


def shards(density, basis, weights, batch_start, batch_count):
    swap = [(0, 1), (1, 0)]
    there = mirror_pairs()
    held, sent = share(density)
    theirs = lax.ppermute(sent, "h", swap)
    packed = pack(batch_start, batch_count, held, theirs)
    window = lax.all_to_all(packed, GROUP, split_axis=0, concat_axis=0, tiled=True)

    outgoing = batches(batch_start, batch_count, weights.reshape(SLOTS, G, 1), basis, window)
    arrived = lax.all_to_all(outgoing, GROUP, split_axis=0, concat_axis=0, tiled=True)

    other = collect(1, batch_start, batch_count, arrived)
    theirs = lax.ppermute(other, "h", swap)
    mine = collect(0, batch_start, batch_count, arrived)
    upper, lower, rest = merge(mine, other, theirs)
    got_upper = lax.ppermute(upper, ALL, there)
    got_lower = lax.ppermute(lower, ALL, [(d, s) for s, d in there])
    blank = jnp.zeros(density.shape, F32)
    potential = place(upper, lower, rest, got_upper, got_lower, blank)
    return potential, rest[TURNS, 0] / (NBLK * BF)


def solution(mesh):
    fine = Mesh(np.asarray(mesh.devices).reshape(2, 2, 4, 4, 2), ALL)
    in_specs = (P(ROW, COL), P(ALL), P(ALL), P(), P())
    out_specs = (P(ROW, COL), P())
    return jax.shard_map(shards, mesh=fine, in_specs=in_specs, out_specs=out_specs, check_vma=False)
```

```python
import functools
import math

import jax
import jax.numpy as jnp
import numpy as np
from jax import lax
from jax.experimental import pallas as pl
from jax.experimental.pallas import tpu as pltpu
from jax.sharding import Mesh, PartitionSpec as P

CX = 0.7385587663820224
MU = 0.2195149727645171
KAPPA = 0.804
BF = 128
KB = 8
NBLK = 64
G = 256
SLOTS = 3
KF = 1024
N_ROW = 16
N_COL = 8
TURNS = NBLK // N_ROW
PEERS = 64
MIB = 1024 * 1024
HB = BF // 2
EXT = SLOTS * HB
ROWS = EXT + 16
BAND = 2 * TURNS * HB
ROW = ("h", "xl", "y")
COL = ("z", "c")
ALL = ROW + COL
GROUP = ("xl", "y", "z", "c")
VMEM = pl.BlockSpec(memory_space=pltpu.VMEM)
HBM = pl.BlockSpec(memory_space=pltpu.HBM)
F32 = jnp.float32
BF16 = jnp.bfloat16


def lanes(shape):
    return lax.broadcasted_iota(jnp.int32, shape, 0), lax.broadcasted_iota(jnp.int32, shape, 1)


def pack_symmetric(full):
    r, c = lanes((HB, BF))
    top, bottom = full[:HB], full[HB:]
    packed = jnp.where((c >= HB) | (r <= c), top, pltpu.roll(bottom, HB, 1))
    row = jnp.sum(jnp.where(c - HB == r, bottom, 0.0), axis=0, keepdims=True)
    return packed, row


def unpack_symmetric(packed, row):
    r, c = lanes((HB, BF))
    flip = jnp.concatenate([packed, packed], axis=0).T
    top = jnp.where((c >= HB) | (r <= c), packed, flip[:HB])
    corner = jnp.where(c - HB < r, pltpu.roll(packed, HB, 1), flip[:HB])
    corner = jnp.where(c - HB == r, row, corner)
    return jnp.concatenate([top, jnp.where(c < HB, flip[HB:], corner)], axis=0)


def pick_row(rows, index):
    r, _ = lanes(rows.shape)
    return jnp.sum(jnp.where(r == index, rows, 0.0), axis=0, keepdims=True)


def position():
    h = lax.axis_index("h")
    row_id = (h * 2 + lax.axis_index("xl")) * 4 + lax.axis_index("y")
    return row_id, lax.axis_index("z") * 2 + lax.axis_index("c"), h


def live(plan, device):
    return plan[N_ROW * N_COL * SLOTS + device]


def entry(plan, peer, slot, where):
    row_id, col_id, h = where
    start = plan[(h * PEERS + peer) * SLOTS + slot]
    i = start + ((row_id - start) & (KB - 1))
    j = start + ((col_id - start) & (KB - 1))
    other = ((i >> 3) & 1) ^ h
    turn = i >> 4
    below = jnp.where(j < i, TURNS, 0)
    return other, turn, pl.multiple_of((below + turn) * HB, HB)


def scalars(count, in_specs, out_specs, scratch_shapes=()):
    return pltpu.PrefetchScalarGridSpec(
        num_scalar_prefetch=count,
        grid=(),
        in_specs=in_specs,
        out_specs=out_specs,
        scratch_shapes=list(scratch_shapes),
    )


def limit(mib):
    return pltpu.CompilerParams(vmem_limit_bytes=mib * MIB)


def share_kernel(density, out, copy, ups, lows, sems):
    row_id, col_id, _ = position()
    shift = (col_id - row_id) & (N_COL - 1)
    row, _ = lanes((16, BF))
    loads = []
    for t in range(TURNS):
        at = (row_id + N_ROW * t + shift) >> 3
        up = density.at[t, jnp.minimum(at, N_COL - 1)]
        low = density.at[t, jnp.maximum(at - 1, 0)]
        loads.append(pltpu.make_async_copy(up, ups.at[t], sems.at[t]))
        loads.append(pltpu.make_async_copy(low, lows.at[t], sems.at[TURNS + t]))
    for load in loads:
        load.start()
    for load in loads:
        load.wait()

    @pl.when(shift > 0)
    def _():
        for t in range(TURNS):
            low = TURNS * HB + t * HB
            out[t * HB : (t + 1) * HB, :] = ups[t, :HB, :]
            out[low : low + HB, :] = lows[t].astype(F32).T[HB:].astype(BF16)
        out[BAND:, :] = jnp.zeros((16, BF), BF16)

    @pl.when(shift == 0)
    def _():
        ext = jnp.zeros((16, BF), F32)
        for t in range(TURNS):
            packed, line = pack_symmetric(ups[t].astype(F32))
            out[t * HB : (t + 1) * HB, :] = packed.astype(BF16)
            ext = jnp.where(row == t, line, ext)
        out[TURNS * HB : BAND, :] = jnp.zeros((TURNS * HB, BF), BF16)
        out[BAND:, :] = ext.astype(BF16)

    copy[...] = out[...]


def share(density):
    held = jax.ShapeDtypeStruct((BAND + 16, BF), BF16)
    return pl.pallas_call(
        share_kernel,
        out_shape=[held, held],
        in_specs=[HBM],
        out_specs=[VMEM, VMEM],
        scratch_shapes=[
            pltpu.VMEM((TURNS, BF, BF), BF16),
            pltpu.VMEM((TURNS, BF, BF), BF16),
            pltpu.SemaphoreType.DMA((2 * TURNS,)),
        ],
        compiler_params=limit(4),
        name="share",
    )(density)


CHUNK = 8


def pack_kernel(plan, mine, theirs, out, table, lines, buf, sems):
    where = position()
    on_diagonal = ((where[1] - where[0]) & (KB - 1)) == 0
    table[0] = mine[:BAND, :]
    table[1] = theirs[:BAND, :]
    lines[0] = mine[BAND:, :].astype(F32)
    lines[1] = theirs[BAND:, :].astype(F32)
    row, _ = lanes((16, BF))

    def send(chunk):
        span = pl.ds(pl.multiple_of(chunk * CHUNK, CHUNK), CHUNK)
        return pltpu.make_async_copy(buf.at[span], out.at[span], sems.at[chunk])

    def one_chunk(chunk, carry):
        for k in range(CHUNK):
            peer = chunk * CHUNK + k
            count = live(plan, where[2] * PEERS + peer)

            def one(slot):
                other, _, at = entry(plan, peer, slot, where)
                buf[peer, slot * HB : (slot + 1) * HB, :] = table[other, pl.ds(at, HB), :]

            one(0)
            for slot in range(1, SLOTS):
                pl.when(slot < count)(lambda slot=slot: one(slot))

            @pl.when(on_diagonal)
            def _():
                ext = jnp.zeros((16, BF), F32)
                for slot in range(SLOTS):
                    other, turn, _ = entry(plan, peer, slot, where)
                    ext = jnp.where(row == slot, lines[other, pl.ds(turn, 1), :], ext)
                buf[peer, EXT:, :] = ext.astype(BF16)

        send(chunk).start()
        return carry

    lax.fori_loop(0, PEERS // CHUNK, one_chunk, 0)

    def drain(chunk, carry):
        send(chunk).wait()
        return carry

    lax.fori_loop(0, PEERS // CHUNK, drain, 0)


def pack(plan, mine, theirs):
    return pl.pallas_call(
        pack_kernel,
        out_shape=jax.ShapeDtypeStruct((PEERS, ROWS, BF), BF16),
        grid_spec=scalars(
            1,
            [VMEM, VMEM],
            HBM,
            [
                pltpu.VMEM((2, BAND, BF), BF16),
                pltpu.VMEM((2, 16, BF), F32),
                pltpu.VMEM((PEERS, ROWS, BF), BF16),
                pltpu.SemaphoreType.DMA((PEERS // CHUNK,)),
            ],
        ),
        compiler_params=limit(8),
        name="pack",
    )(plan, mine, theirs)


def batch_kernel(
    plan, weights, basis, window, out,
    quads, phis, win, win_ext, mat, pair, lines, sem_e, sem_w, sem_b,
):
    row_id, col_id, _ = position()
    me = row_id * N_COL + col_id
    count = live(plan, me)
    row, lane = lanes((16, BF))
    weights_copy = pltpu.make_async_copy(weights, quads, sem_e.at[0])
    ext_copy = pltpu.make_async_copy(window.at[:, pl.ds(EXT, 16)], win_ext, sem_e.at[1])

    def window_copy(slot):
        span = pl.ds(pl.multiple_of(slot * HB, HB), HB)
        return pltpu.make_async_copy(window.at[:, span], win.at[slot], sem_w.at[slot])

    def basis_copy(slot):
        return pltpu.make_async_copy(basis.at[slot], phis.at[slot], sem_b.at[slot])

    def fetch(slot, carry):
        window_copy(slot).start()
        basis_copy(slot).start()
        return carry

    ext_copy.start()
    weights_copy.start()
    lax.fori_loop(0, count, fetch, 0)
    lines[...] = jnp.zeros(lines.shape, F32)
    ext_copy.wait()
    weights_copy.wait()

    def work(slot, total):
        start = plan[me * SLOTS + slot]
        cls = [(start + o) & (KB - 1) for o in range(KB)]
        span = pl.ds(pl.multiple_of(slot * HB, HB), HB)
        window_copy(slot).wait()
        for o1 in range(KB):
            r1 = o1 * BF
            for o2 in range(o1 + 1, KB):
                top = win[slot, cls[o1] * KB + cls[o2]]
                bottom = win[slot, cls[o2] * KB + cls[o1]]
                mat[r1 : r1 + HB, o2 * BF : (o2 + 1) * BF] = top
                mat[r1 + HB : r1 + BF, o2 * BF : (o2 + 1) * BF] = bottom
                if o2 == o1 + 1 and o1 % 2 == 0:
                    mat[o2 * BF : (o2 + 1) * BF, r1 : r1 + BF] = jnp.concatenate(
                        [top, bottom], axis=0
                    ).T
            diagonal = cls[o1] * (KB + 1)
            line = pick_row(win_ext[diagonal].astype(F32), slot)
            block = unpack_symmetric(win[slot, diagonal].astype(F32), line)
            mat[r1 : r1 + BF, r1 : r1 + BF] = block.astype(BF16)
        basis_copy(slot).wait()
        sums = [jnp.zeros((G, BF), F32) for _ in range(4)]
        for t in range(4):
            lo, hi = 256 * t, 256 * (t + 1)
            product = jnp.dot(phis[slot, 0, :, :hi], mat[:hi, lo:hi], preferred_element_type=F32)
            if hi < KF:
                product += lax.dot_general(
                    phis[slot, 0, :, hi:],
                    mat[lo:hi, hi:],
                    (((1,), (1,)), ((), ())),
                    preferred_element_type=F32,
                )
            for k in range(4):
                terms = phis[slot, k, :, lo:hi].astype(F32) * product
                sums[k] += terms[:, :BF] + terms[:, BF:]
        sums = [jnp.sum(x, axis=1, keepdims=True) for x in sums]
        rho = sums[0]
        grads = [2.0 * x for x in sums[1:]]
        sigma = grads[0] * grads[0] + grads[1] * grads[1] + grads[2] * grads[2]
        quad = quads[slot]
        square = rho * rho + 1.0
        logs = jnp.log(square)
        cube = jnp.exp(logs * (1.0 / 3.0))
        scaled = cube * cube
        reduced = sigma / (scaled * scaled)
        denom = 1.0 + MU * reduced / KAPPA
        factor = 1.0 + MU * reduced / denom
        slope = MU / denom / denom
        point = -CX * scaled * factor
        by_rho = (-CX * 2.0) * rho / cube * ((2.0 / 3.0) * factor - (4.0 / 3.0) * slope * reduced)
        by_sigma = -CX * slope / scaled
        wr = 0.5 * quad * by_rho
        ws = 2.0 * quad * by_sigma
        total = total + jnp.sum(quad * point)
        coeffs = [wr] + [ws * x for x in grads]
        for t in range(4):
            lo, hi = 256 * t, 256 * (t + 1)
            mixed = coeffs[0] * phis[slot, 0, :, lo:hi].astype(F32)
            for k in range(1, 4):
                mixed += coeffs[k] * phis[slot, k, :, lo:hi].astype(F32)
            pair[:G, lo:hi] = mixed.astype(BF16)
        pair[G:, :] = phis[slot, 0]
        for t in range(4):
            lo, hi = 256 * t, 256 * (t + 1)
            left = jnp.concatenate([pair[G:, lo:hi], pair[:G, lo:hi]], axis=0)
            rows = lax.dot_general(
                left, pair[:, lo:], (((0,), (0,)), ((), ())), preferred_element_type=F32
            )
            for k in range(2):
                o1 = 2 * t + k
                for o2 in range(o1, KB):
                    c0 = o2 * BF - lo
                    block = rows[k * BF : (k + 1) * BF, c0 : c0 + BF]
                    if o2 == o1:
                        packed, line = pack_symmetric(block)
                        out[cls[o1] * (KB + 1), span, :] = packed.astype(BF16)
                        lines[cls[o1]] = jnp.where(row == slot, line, lines[cls[o1]])
                    else:
                        out[cls[o1] * KB + cls[o2], span, :] = block[:HB].astype(BF16)
                        out[cls[o2] * KB + cls[o1], span, :] = block[HB:].astype(BF16)
        return total

    total = jnp.full((16, BF), lax.fori_loop(0, count, work, jnp.float32(0.0)), F32)
    first = total.astype(BF16).astype(F32)
    second = (total - first).astype(BF16).astype(F32)
    third = total - first - second
    spread = jnp.where(lane == 0, first, jnp.where(lane == 1, second, third))
    energy = jnp.where((row == 0) & (lane < 3), spread, 0.0)
    for peer in range(PEERS):
        if peer % (KB + 1) == 0:
            out[peer, EXT:, :] = (lines[peer // (KB + 1)] + energy).astype(BF16)
        else:
            out[peer, EXT:, :] = energy.astype(BF16)


def batches(plan, weights, basis, window):
    return pl.pallas_call(
        batch_kernel,
        out_shape=jax.ShapeDtypeStruct((PEERS, ROWS, BF), BF16),
        grid_spec=scalars(
            1,
            [HBM, HBM, HBM],
            VMEM,
            [
                pltpu.VMEM((SLOTS, G, 1), F32),
                pltpu.VMEM((SLOTS, 4, G, KF), BF16),
                pltpu.VMEM((SLOTS, PEERS, HB, BF), BF16),
                pltpu.VMEM((PEERS, 16, BF), BF16),
                pltpu.VMEM((KF, KF), BF16),
                pltpu.VMEM((2 * G, KF), BF16),
                pltpu.VMEM((KB, 16, BF), F32),
                pltpu.SemaphoreType.DMA((2,)),
                pltpu.SemaphoreType.DMA((SLOTS,)),
                pltpu.SemaphoreType.DMA((SLOTS,)),
            ],
        ),
        compiler_params=limit(48),
        name="batches",
    )(plan, weights, basis, window)


STEP = math.log(2.0) / 128.0
FULL = 32767.0


def integer(values):
    return values.astype(jnp.int32).astype(jnp.int16)


def encode(values):
    top = jnp.max(jnp.max(jnp.abs(values), axis=0, keepdims=True), axis=1, keepdims=True)
    code = jnp.ceil(jnp.log(jnp.maximum(top, 2.0**-110)) * (1.0 / STEP))
    scaled = values * jnp.exp(math.log(FULL) - code * STEP)
    return jnp.clip(scaled, -FULL, FULL), code


def decode(words, code):
    return words.astype(F32) * jnp.exp(code.astype(F32) * STEP - math.log(FULL))


def collect_kernel(which, plan, arrived, *refs):
    where = position()
    on_diagonal = ((where[1] - where[0]) & (KB - 1)) == 0
    row, lane = lanes((16, BF))
    eight, _ = lanes((8, BF))
    if which:
        out, acc, energy = refs
        energy[...] = jnp.zeros(energy.shape, F32)
    else:
        acc, blank, zeros, sems = refs
        zeros[...] = jnp.zeros(zeros.shape, F32)
        fills = [pltpu.make_async_copy(zeros, blank.at[t], sems.at[t]) for t in range(TURNS)]
        for fill in fills:
            fill.start()
    acc[...] = jnp.zeros(acc.shape, F32)

    def one_chunk(chunk, carry):
        for k in range(CHUNK):
            peer = chunk * CHUNK + k
            count = live(plan, where[2] * PEERS + peer)
            if which:
                energy[...] += arrived[peer, EXT:, :].astype(F32)

            def one(slot, used):
                other, turn, at = entry(plan, peer, slot, where)
                wanted = other == which

                @pl.when(wanted if used is None else wanted & used)
                def _():
                    part = arrived[peer, slot * HB : (slot + 1) * HB, :]
                    acc[pl.ds(at, HB), :] += part.astype(F32)

                    @pl.when(on_diagonal)
                    def _():
                        ext = arrived[peer, EXT:, :].astype(F32)
                        line = jnp.where((row == slot) & (lane >= HB), ext, 0.0)
                        line = jnp.sum(line, axis=0, keepdims=True)
                        acc[BAND:, :] += jnp.where(eight == turn, line, 0.0)

            one(0, None)
            for slot in range(1, SLOTS):
                one(slot, slot < count)
        return carry

    lax.fori_loop(0, PEERS // CHUNK, one_chunk, 0)
    if not which:
        for fill in fills:
            fill.wait()
        return

    words, code = encode(acc[BAND:, :])
    ext = jnp.concatenate([words, words], axis=0)
    ext = jnp.where(row == 7, code, ext)
    total = jnp.where((row == 0) & (lane < 3), energy[...], 0.0)
    total = jnp.sum(jnp.sum(total, axis=0, keepdims=True), axis=1, keepdims=True)
    words, code = encode(total)
    first = jnp.floor(words + 0.5)
    ext = jnp.where(row == 4, first, ext)
    ext = jnp.where(row == 5, (words - first) * FULL, ext)
    ext = jnp.where(row == 6, code, ext)
    for k in range(2 * TURNS):
        words, code = encode(acc[k * HB : (k + 1) * HB, :])
        out[k * HB : (k + 1) * HB, :] = integer(jnp.floor(words + 0.5))
        ext = jnp.where(row == 8 + k, code, ext)
    out[BAND:, :] = integer(jnp.floor(ext + 0.5))


def collect(which, plan, arrived):
    acc = jax.ShapeDtypeStruct((BAND + 8, BF), F32)
    if which:
        out_shape = jax.ShapeDtypeStruct((BAND + 16, BF), jnp.int16)
        out_specs = VMEM
        scratch = [pltpu.VMEM((BAND + 8, BF), F32), pltpu.VMEM((16, BF), F32)]
    else:
        out_shape = [acc, jax.ShapeDtypeStruct((TURNS, N_COL, BF, BF), F32)]
        out_specs = [VMEM, HBM]
        scratch = [pltpu.VMEM((N_COL, BF, BF), F32), pltpu.SemaphoreType.DMA((TURNS,))]
    return pl.pallas_call(
        functools.partial(collect_kernel, which),
        out_shape=out_shape,
        grid_spec=scalars(1, [VMEM], out_specs, scratch),
        compiler_params=limit(8),
        cost_estimate=pl.CostEstimate(flops=10**6, bytes_accessed=4 * MIB, transcendentals=0),
        name=("collect_own", "collect_other")[which],
    )(plan, arrived)


def merge_kernel(mine, sent, theirs, upper, lower, rest, up_words, low_words):
    eight, _ = lanes((8, BF))
    row, _ = lanes((16, BF))
    got = theirs[BAND:, :].astype(F32)
    own = sent[BAND:, :].astype(F32)

    def line(rows, index):
        return rows[index : index + 1, :]

    def energy(rows):
        return decode(line(rows, 4) + line(rows, 5) * (1.0 / FULL), line(rows, 6))

    more = jnp.where(eight < TURNS, decode(got[:8, :], line(got, 7)), 0.0)
    rest[...] = jnp.where(eight == TURNS, energy(own) + energy(got), mine[BAND:, :] + more)
    for low, full, words in ((0, upper, up_words), (1, lower, low_words)):
        codes = jnp.zeros((16, BF), F32)
        for t in range(TURNS):
            k = low * TURNS + t
            span = slice(k * HB, (k + 1) * HB)
            total = mine[span, :] + decode(theirs[span, :].astype(F32), line(got, 8 + k))
            full[t * HB : (t + 1) * HB, :] = total
            scaled, code = encode(total)
            words[t * HB : (t + 1) * HB, :] = integer(jnp.floor(scaled + 0.5))
            codes = jnp.where(row == t, code, codes)
        words[TURNS * HB :, :] = integer(jnp.floor(codes + 0.5))


def merge(mine, sent, theirs):
    half = jax.ShapeDtypeStruct((TURNS * HB, BF), F32)
    words = jax.ShapeDtypeStruct((TURNS * HB + 16, BF), jnp.int16)
    return pl.pallas_call(
        merge_kernel,
        out_shape=[half, half, jax.ShapeDtypeStruct((8, BF), F32), words, words],
        in_specs=[VMEM] * 3,
        out_specs=[VMEM] * 5,
        compiler_params=limit(4),
        name="merge",
    )(mine, sent, theirs)


def place_kernel(upper, lower, rest, got_upper, got_lower, blank, out, blocks, sems):
    del blank
    row_id, col_id, _ = position()
    shift = (col_id - row_id) & (N_COL - 1)

    def part(ref, turn):
        return ref[pl.ds(pl.multiple_of(turn * HB, HB), HB), :]

    def coded(ref, turn):
        code = pick_row(ref[TURNS * HB :, :].astype(F32), turn)
        return decode(part(ref, turn).astype(F32), code)

    def write(t, low, at):
        slot = TURNS * low + t
        return pltpu.make_async_copy(blocks.at[slot], out.at[t, at], sems.at[slot])

    for finish in (False, True):
        for t in range(TURNS):
            at = (row_id + N_ROW * t + shift) >> 3

            @pl.when((shift > 0) & (at < N_COL))
            def _():
                if finish:
                    write(t, 0, at).wait()
                else:
                    turn = t + jnp.where(row_id + shift >= N_ROW, 1, 0)
                    blocks[t, :HB, :] = part(upper, t)
                    blocks[t, HB:, :] = coded(got_lower, jnp.minimum(turn, TURNS - 1))
                    write(t, 0, at).start()

            @pl.when((shift > 0) & (at > 0))
            def _():
                if finish:
                    write(t, 1, at - 1).wait()
                else:
                    turn = t - jnp.where(row_id + shift < N_COL, 1, 0)
                    top = coded(got_upper, jnp.maximum(turn, 0))
                    blocks[TURNS + t] = jnp.concatenate([top, part(lower, t)], axis=0).T
                    write(t, 1, at - 1).start()

            @pl.when(shift == 0)
            def _():
                if finish:
                    write(t, 0, at).wait()
                else:
                    blocks[t] = unpack_symmetric(part(upper, t), rest[t : t + 1, :])
                    write(t, 0, at).start()


def place(upper, lower, rest, got_upper, got_lower, blank):
    return pl.pallas_call(
        place_kernel,
        out_shape=jax.ShapeDtypeStruct((TURNS, N_COL, BF, BF), F32),
        in_specs=[VMEM] * 5 + [HBM],
        out_specs=HBM,
        scratch_shapes=[
            pltpu.VMEM((2 * TURNS, BF, BF), F32),
            pltpu.SemaphoreType.DMA((2 * TURNS,)),
        ],
        input_output_aliases={5: 0},
        compiler_params=limit(4),
        name="place",
    )(upper, lower, rest, got_upper, got_lower, blank)


def mirror_pairs():
    pairs = []
    for row in range(N_ROW):
        for col in range(N_COL):
            shift = (col - row) % N_COL
            pairs.append((row * N_COL + col, (row + shift) % N_ROW * N_COL + row % N_COL))
    return pairs


def shards(density, basis, weights, batch_start, batch_count):
    swap = [(0, 1), (1, 0)]
    there = mirror_pairs()
    plan = jnp.concatenate([batch_start, batch_count])
    held, sent = share(density)
    theirs = lax.ppermute(sent, "h", swap)
    packed = pack(plan, held, theirs)
    window = lax.all_to_all(packed, GROUP, split_axis=0, concat_axis=0, tiled=True)

    outgoing = batches(plan, weights.reshape(SLOTS, G, 1), basis, window)
    arrived = lax.all_to_all(outgoing, GROUP, split_axis=0, concat_axis=0, tiled=True)

    sent = collect(1, plan, arrived)
    theirs = lax.ppermute(sent, "h", swap)
    mine, blank = collect(0, plan, arrived)
    upper, lower, rest, up_words, low_words = merge(mine, sent, theirs)
    got_upper = lax.ppermute(up_words, ALL, there)
    got_lower = lax.ppermute(low_words, ALL, [(d, s) for s, d in there])
    potential = place(upper, lower, rest, got_upper, got_lower, blank)
    return potential, rest[TURNS, 0] / (NBLK * BF)


def solution(mesh):
    fine = Mesh(np.asarray(mesh.devices).reshape(2, 2, 4, 4, 2), ALL)
    in_specs = (P(ROW, COL), P(ALL), P(ALL), P(), P())
    out_specs = (P(ROW, COL), P())
    return jax.shard_map(shards, mesh=fine, in_specs=in_specs, out_specs=out_specs, check_vma=False)
```

```python
import functools
import math

import jax
import jax.numpy as jnp
import numpy as np
from jax import lax
from jax.experimental import pallas as pl
from jax.experimental.pallas import tpu as pltpu
from jax.sharding import Mesh, PartitionSpec as P

CX = 0.7385587663820224
MU = 0.2195149727645171
KAPPA = 0.804
BF = 128
KB = 8
NBLK = 64
G = 256
SLOTS = 3
KF = 1024
N_ROW = 16
N_COL = 8
TURNS = NBLK // N_ROW
PEERS = 64
MIB = 1024 * 1024
HB = BF // 2
EXT = SLOTS * HB
ROWS = EXT + 16
BAND = 2 * TURNS * HB
ROW = ("h", "xl", "y")
COL = ("z", "c")
ALL = ROW + COL
GROUP = ("xl", "y", "z", "c")
VMEM = pl.BlockSpec(memory_space=pltpu.VMEM)
HBM = pl.BlockSpec(memory_space=pltpu.HBM)
F32 = jnp.float32
BF16 = jnp.bfloat16


def lanes(shape):
    return lax.broadcasted_iota(jnp.int32, shape, 0), lax.broadcasted_iota(jnp.int32, shape, 1)


def pack_symmetric(full):
    r, c = lanes((HB, BF))
    top, bottom = full[:HB], full[HB:]
    packed = jnp.where((c >= HB) | (r <= c), top, pltpu.roll(bottom, HB, 1))
    row = jnp.sum(jnp.where(c - HB == r, bottom, 0.0), axis=0, keepdims=True)
    return packed, row


def unpack_symmetric(packed, row):
    r, c = lanes((HB, BF))
    flip = jnp.concatenate([packed, packed], axis=0).T
    top = jnp.where((c >= HB) | (r <= c), packed, flip[:HB])
    corner = jnp.where(c - HB < r, pltpu.roll(packed, HB, 1), flip[:HB])
    corner = jnp.where(c - HB == r, row, corner)
    return jnp.concatenate([top, jnp.where(c < HB, flip[HB:], corner)], axis=0)


def split_symmetric(packed, row):
    r, c = lanes((HB, BF))
    low = jnp.where((c >= HB) & (c - HB < r), pltpu.roll(packed, HB, 1), 0.0)
    first = [jnp.where((c >= HB) | (r <= c), packed, 0.0), jnp.where(c - HB == r, row, low)]
    second = [jnp.where((c >= HB) | (r < c), packed, 0.0), low]
    return jnp.concatenate(first, axis=0), jnp.concatenate(second, axis=0)


def pick_row(rows, index):
    r, _ = lanes(rows.shape)
    return jnp.sum(jnp.where(r == index, rows, 0.0), axis=0, keepdims=True)


def position():
    h = lax.axis_index("h")
    row_id = (h * 2 + lax.axis_index("xl")) * 4 + lax.axis_index("y")
    return row_id, lax.axis_index("z") * 2 + lax.axis_index("c"), h


def live(plan, device):
    return plan[N_ROW * N_COL * SLOTS + device]


def entry(plan, peer, slot, where):
    row_id, col_id, h = where
    start = plan[(h * PEERS + peer) * SLOTS + slot]
    i = start + ((row_id - start) & (KB - 1))
    j = start + ((col_id - start) & (KB - 1))
    other = ((i >> 3) & 1) ^ h
    turn = i >> 4
    below = jnp.where(j < i, TURNS, 0)
    return other, turn, pl.multiple_of((below + turn) * HB, HB)


def scalars(count, in_specs, out_specs, scratch_shapes=()):
    return pltpu.PrefetchScalarGridSpec(
        num_scalar_prefetch=count,
        grid=(),
        in_specs=in_specs,
        out_specs=out_specs,
        scratch_shapes=list(scratch_shapes),
    )


def limit(mib):
    return pltpu.CompilerParams(vmem_limit_bytes=mib * MIB)


def share_kernel(density, out, copy, ups, lows, sems):
    row_id, col_id, _ = position()
    shift = (col_id - row_id) & (N_COL - 1)
    row, _ = lanes((16, BF))
    loads = []
    for t in range(TURNS):
        at = (row_id + N_ROW * t + shift) >> 3
        up = density.at[t, jnp.minimum(at, N_COL - 1)]
        low = density.at[t, jnp.maximum(at - 1, 0)]
        loads.append(pltpu.make_async_copy(up, ups.at[t], sems.at[t]))
        loads.append(pltpu.make_async_copy(low, lows.at[t], sems.at[TURNS + t]))
    for load in loads:
        load.start()
    for load in loads:
        load.wait()

    @pl.when(shift > 0)
    def _():
        for t in range(TURNS):
            low = TURNS * HB + t * HB
            out[t * HB : (t + 1) * HB, :] = ups[t, :HB, :]
            out[low : low + HB, :] = lows[t].astype(F32).T[HB:].astype(BF16)
        out[BAND:, :] = jnp.zeros((16, BF), BF16)

    @pl.when(shift == 0)
    def _():
        ext = jnp.zeros((16, BF), F32)
        for t in range(TURNS):
            packed, line = pack_symmetric(ups[t].astype(F32))
            out[t * HB : (t + 1) * HB, :] = packed.astype(BF16)
            ext = jnp.where(row == t, line, ext)
        out[TURNS * HB : BAND, :] = jnp.zeros((TURNS * HB, BF), BF16)
        out[BAND:, :] = ext.astype(BF16)

    copy[...] = out[...]


def share(density):
    held = jax.ShapeDtypeStruct((BAND + 16, BF), BF16)
    return pl.pallas_call(
        share_kernel,
        out_shape=[held, held],
        in_specs=[HBM],
        out_specs=[VMEM, VMEM],
        scratch_shapes=[
            pltpu.VMEM((TURNS, BF, BF), BF16),
            pltpu.VMEM((TURNS, BF, BF), BF16),
            pltpu.SemaphoreType.DMA((2 * TURNS,)),
        ],
        compiler_params=limit(4),
        name="share",
    )(density)


CHUNK = 8


def pack_kernel(plan, mine, theirs, out, table, lines, buf, sems):
    where = position()
    on_diagonal = ((where[1] - where[0]) & (KB - 1)) == 0
    table[0] = mine[:BAND, :]
    table[1] = theirs[:BAND, :]
    lines[0] = mine[BAND:, :].astype(F32)
    lines[1] = theirs[BAND:, :].astype(F32)
    row, _ = lanes((16, BF))

    def send(chunk):
        span = pl.ds(pl.multiple_of(chunk * CHUNK, CHUNK), CHUNK)
        return pltpu.make_async_copy(buf.at[span], out.at[span], sems.at[chunk])

    def one_chunk(chunk, carry):
        for k in range(CHUNK):
            peer = chunk * CHUNK + k
            count = live(plan, where[2] * PEERS + peer)

            def one(slot):
                other, _, at = entry(plan, peer, slot, where)
                buf[peer, slot * HB : (slot + 1) * HB, :] = table[other, pl.ds(at, HB), :]

            one(0)
            for slot in range(1, SLOTS):
                pl.when(slot < count)(lambda slot=slot: one(slot))

            @pl.when(on_diagonal)
            def _():
                ext = jnp.zeros((16, BF), F32)
                for slot in range(SLOTS):
                    other, turn, _ = entry(plan, peer, slot, where)
                    ext = jnp.where(row == slot, lines[other, pl.ds(turn, 1), :], ext)
                buf[peer, EXT:, :] = ext.astype(BF16)

        send(chunk).start()
        return carry

    lax.fori_loop(0, PEERS // CHUNK, one_chunk, 0)

    def drain(chunk, carry):
        send(chunk).wait()
        return carry

    lax.fori_loop(0, PEERS // CHUNK, drain, 0)


def pack(plan, mine, theirs):
    return pl.pallas_call(
        pack_kernel,
        out_shape=jax.ShapeDtypeStruct((PEERS, ROWS, BF), BF16),
        grid_spec=scalars(
            1,
            [VMEM, VMEM],
            HBM,
            [
                pltpu.VMEM((2, BAND, BF), BF16),
                pltpu.VMEM((2, 16, BF), F32),
                pltpu.VMEM((PEERS, ROWS, BF), BF16),
                pltpu.SemaphoreType.DMA((PEERS // CHUNK,)),
            ],
        ),
        compiler_params=limit(8),
        name="pack",
    )(plan, mine, theirs)


def turn_kernel(plan, basis, out, held, turned, sem_in, sem_out):
    row_id, col_id, _ = position()
    count = live(plan, row_id * N_COL + col_id)

    def load(slot):
        return pltpu.make_async_copy(basis.at[slot], held.at[slot], sem_in.at[slot])

    def store(slot):
        return pltpu.make_async_copy(turned.at[slot], out.at[slot], sem_out.at[slot])

    def fetch(slot, carry):
        load(slot).start()
        return carry

    def work(slot, carry):
        load(slot).wait()
        for k in range(4):
            for o in range(KB):
                span = slice(o * BF, (o + 1) * BF)
                turned[slot, k, span, :] = held[slot, k, :, span].T
        store(slot).start()
        return carry

    def drain(slot, carry):
        store(slot).wait()
        return carry

    lax.fori_loop(0, count, fetch, 0)
    lax.fori_loop(0, count, work, 0)
    lax.fori_loop(0, count, drain, 0)


def turn(plan, basis):
    return pl.pallas_call(
        turn_kernel,
        out_shape=jax.ShapeDtypeStruct((SLOTS, 4, KF, G), BF16),
        grid_spec=scalars(
            1,
            [HBM],
            HBM,
            [
                pltpu.VMEM((SLOTS, 4, G, KF), BF16),
                pltpu.VMEM((SLOTS, 4, KF, G), BF16),
                pltpu.SemaphoreType.DMA((SLOTS,)),
                pltpu.SemaphoreType.DMA((SLOTS,)),
            ],
        ),
        compiler_params=limit(48),
        cost_estimate=pl.CostEstimate(flops=10**6, bytes_accessed=24 * MIB, transcendentals=0),
        name="turn",
    )(plan, basis)


def dot_nt(x, y):
    return lax.dot_general(x, y, (((1,), (1,)), ((), ())), preferred_element_type=F32)


def batch_kernel(
    plan, weights, basis, flipped, window, out,
    phis, turned, win, win_ext, mat, corner, left, right, lines, sem_e, sem_w, sem_b, sem_t,
):
    row_id, col_id, _ = position()
    me = row_id * N_COL + col_id
    count = live(plan, me)
    row, lane = lanes((16, BF))
    ext_copy = pltpu.make_async_copy(window.at[:, pl.ds(EXT, 16)], win_ext, sem_e)

    def window_copy(slot):
        span = pl.ds(pl.multiple_of(slot * HB, HB), HB)
        return pltpu.make_async_copy(window.at[:, span], win.at[slot], sem_w.at[slot])

    def basis_copy(slot):
        return pltpu.make_async_copy(basis.at[slot], phis.at[slot], sem_b.at[slot])

    def flipped_copy(slot):
        return pltpu.make_async_copy(flipped.at[slot], turned.at[slot], sem_t.at[slot])

    def fetch(slot, carry):
        window_copy(slot).start()
        basis_copy(slot).start()
        flipped_copy(slot).start()
        return carry

    ext_copy.start()
    lax.fori_loop(0, count, fetch, 0)
    lines[...] = jnp.zeros(lines.shape, F32)
    for t in range(4):
        lo = 256 * t
        mat[lo + BF : lo + 256, lo : lo + BF] = jnp.zeros((BF, BF), BF16)
        corner[t, BF:, :BF] = jnp.zeros((BF, BF), BF16)
    ext_copy.wait()

    def work(slot, total):
        start = plan[me * SLOTS + slot]
        cls = [(start + o) & (KB - 1) for o in range(KB)]
        span = pl.ds(pl.multiple_of(slot * HB, HB), HB)
        window_copy(slot).wait()
        for o1 in range(KB):
            r1, t, c1 = o1 * BF, o1 // 2, o1 % 2 * BF
            for o2 in range(o1 + 1, KB):
                top = win[slot, cls[o1] * KB + cls[o2]]
                bottom = win[slot, cls[o2] * KB + cls[o1]]
                mat[r1 : r1 + HB, o2 * BF : (o2 + 1) * BF] = top
                mat[r1 + HB : r1 + BF, o2 * BF : (o2 + 1) * BF] = bottom
                if o2 == o1 + 1 and o1 % 2 == 0:
                    corner[t, :HB, BF:] = top
                    corner[t, HB:BF, BF:] = bottom
            diagonal = cls[o1] * (KB + 1)
            line = pick_row(win_ext[diagonal].astype(F32), slot)
            first, second = split_symmetric(win[slot, diagonal].astype(F32), line)
            mat[r1 : r1 + BF, r1 : r1 + BF] = first.astype(BF16)
            corner[t, c1 : c1 + BF, c1 : c1 + BF] = second.astype(BF16)
        basis_copy(slot).wait()
        sums = [jnp.zeros((G, BF), F32) for _ in range(4)]
        for t in range(4):
            lo, hi = 256 * t, 256 * (t + 1)
            product = jnp.dot(phis[slot, 0, :, :hi], mat[:hi, lo:hi], preferred_element_type=F32)
            product += dot_nt(phis[slot, 0, :, lo:hi], corner[t])
            if hi < KF:
                product += dot_nt(phis[slot, 0, :, hi:], mat[lo:hi, hi:])
            for k in range(4):
                terms = phis[slot, k, :, lo:hi].astype(F32) * product
                sums[k] += terms[:, :BF] + terms[:, BF:]
        sums = [jnp.sum(x.T, axis=0, keepdims=True) for x in sums]
        rho = sums[0]
        grads = [2.0 * x for x in sums[1:]]
        sigma = grads[0] * grads[0] + grads[1] * grads[1] + grads[2] * grads[2]
        quad = weights[pl.ds(slot, 1), :]
        square = rho * rho + 1.0
        logs = jnp.log(square)
        cube = jnp.exp(logs * (1.0 / 3.0))
        scaled = cube * cube
        reduced = sigma / (scaled * scaled)
        denom = 1.0 + MU * reduced / KAPPA
        factor = 1.0 + MU * reduced / denom
        slope = MU / denom / denom
        point = -CX * scaled * factor
        by_rho = (-CX * 2.0) * rho / cube * ((2.0 / 3.0) * factor - (4.0 / 3.0) * slope * reduced)
        by_sigma = -CX * slope / scaled
        wr = 0.5 * quad * by_rho
        ws = 2.0 * quad * by_sigma
        total = total + jnp.sum(quad * point)
        coeffs = [wr] + [ws * x for x in grads]
        flipped_copy(slot).wait()
        for t in range(4):
            lo, hi = 256 * t, 256 * (t + 1)
            phi = turned[slot, 0, lo:hi, :]
            mixed = coeffs[0] * phi.astype(F32)
            for k in range(1, 4):
                mixed += coeffs[k] * turned[slot, k, lo:hi, :].astype(F32)
            mixed = mixed.astype(BF16)
            left[lo:hi, :G] = phi
            left[lo:hi, G:] = mixed
            right[lo:hi, :G] = mixed
            right[lo:hi, G:] = phi
        for t in range(4):
            lo, hi = 256 * t, 256 * (t + 1)
            rows = dot_nt(left[lo:hi, :], right[lo:, :])
            for k in range(2):
                o1 = 2 * t + k
                for o2 in range(o1, KB):
                    c0 = o2 * BF - lo
                    block = rows[k * BF : (k + 1) * BF, c0 : c0 + BF]
                    if o2 == o1:
                        packed, line = pack_symmetric(block)
                        out[cls[o1] * (KB + 1), span, :] = packed.astype(BF16)
                        lines[cls[o1]] = jnp.where(row == slot, line, lines[cls[o1]])
                    else:
                        out[cls[o1] * KB + cls[o2], span, :] = block[:HB].astype(BF16)
                        out[cls[o2] * KB + cls[o1], span, :] = block[HB:].astype(BF16)
        return total

    total = jnp.full((16, BF), lax.fori_loop(0, count, work, jnp.float32(0.0)), F32)
    first = total.astype(BF16).astype(F32)
    second = (total - first).astype(BF16).astype(F32)
    third = total - first - second
    spread = jnp.where(lane == 0, first, jnp.where(lane == 1, second, third))
    energy = jnp.where((row == 0) & (lane < 3), spread, 0.0)
    for peer in range(PEERS):
        if peer % (KB + 1) == 0:
            out[peer, EXT:, :] = (lines[peer // (KB + 1)] + energy).astype(BF16)
        else:
            out[peer, EXT:, :] = energy.astype(BF16)


def batches(plan, weights, basis, flipped, window):
    return pl.pallas_call(
        batch_kernel,
        out_shape=jax.ShapeDtypeStruct((PEERS, ROWS, BF), BF16),
        grid_spec=scalars(
            1,
            [VMEM, HBM, HBM, HBM],
            VMEM,
            [
                pltpu.VMEM((SLOTS, 4, G, KF), BF16),
                pltpu.VMEM((SLOTS, 4, KF, G), BF16),
                pltpu.VMEM((SLOTS, PEERS, HB, BF), BF16),
                pltpu.VMEM((PEERS, 16, BF), BF16),
                pltpu.VMEM((KF, KF), BF16),
                pltpu.VMEM((4, 256, 256), BF16),
                pltpu.VMEM((KF, 2 * G), BF16),
                pltpu.VMEM((KF, 2 * G), BF16),
                pltpu.VMEM((KB, 16, BF), F32),
                pltpu.SemaphoreType.DMA,
                pltpu.SemaphoreType.DMA((SLOTS,)),
                pltpu.SemaphoreType.DMA((SLOTS,)),
                pltpu.SemaphoreType.DMA((SLOTS,)),
            ],
        ),
        compiler_params=limit(48),
        name="batches",
    )(plan, weights, basis, flipped, window)


STEP = math.log(2.0) / 128.0
FULL = 32767.0


def integer(values):
    return values.astype(jnp.int32).astype(jnp.int16)


def encode(values):
    top = jnp.max(jnp.max(jnp.abs(values), axis=0, keepdims=True), axis=1, keepdims=True)
    code = jnp.ceil(jnp.log(jnp.maximum(top, 2.0**-110)) * (1.0 / STEP))
    scaled = values * jnp.exp(math.log(FULL) - code * STEP)
    return jnp.clip(scaled, -FULL, FULL), code


def decode(words, code):
    return words.astype(F32) * jnp.exp(code.astype(F32) * STEP - math.log(FULL))


def collect_kernel(which, plan, arrived, *refs):
    where = position()
    on_diagonal = ((where[1] - where[0]) & (KB - 1)) == 0
    row, lane = lanes((16, BF))
    eight, _ = lanes((8, BF))
    if which:
        out, acc, energy = refs
        energy[...] = jnp.zeros(energy.shape, F32)
    else:
        acc, blank, zeros, sems = refs
        zeros[...] = jnp.zeros(zeros.shape, F32)
        fills = [pltpu.make_async_copy(zeros, blank.at[t], sems.at[t]) for t in range(TURNS)]
        for fill in fills:
            fill.start()
    acc[...] = jnp.zeros(acc.shape, F32)

    def one_chunk(chunk, carry):
        for k in range(CHUNK):
            peer = chunk * CHUNK + k
            count = live(plan, where[2] * PEERS + peer)
            if which:
                energy[...] += arrived[peer, EXT:, :].astype(F32)

            def one(slot, used):
                other, turn, at = entry(plan, peer, slot, where)
                wanted = other == which

                @pl.when(wanted if used is None else wanted & used)
                def _():
                    part = arrived[peer, slot * HB : (slot + 1) * HB, :]
                    acc[pl.ds(at, HB), :] += part.astype(F32)

                    @pl.when(on_diagonal)
                    def _():
                        ext = arrived[peer, EXT:, :].astype(F32)
                        line = jnp.where((row == slot) & (lane >= HB), ext, 0.0)
                        line = jnp.sum(line, axis=0, keepdims=True)
                        acc[BAND:, :] += jnp.where(eight == turn, line, 0.0)

            one(0, None)
            for slot in range(1, SLOTS):
                one(slot, slot < count)
        return carry

    lax.fori_loop(0, PEERS // CHUNK, one_chunk, 0)
    if not which:
        for fill in fills:
            fill.wait()
        return

    words, code = encode(acc[BAND:, :])
    ext = jnp.concatenate([words, words], axis=0)
    ext = jnp.where(row == 7, code, ext)
    total = jnp.where((row == 0) & (lane < 3), energy[...], 0.0)
    total = jnp.sum(jnp.sum(total, axis=0, keepdims=True), axis=1, keepdims=True)
    words, code = encode(total)
    first = jnp.floor(words + 0.5)
    ext = jnp.where(row == 4, first, ext)
    ext = jnp.where(row == 5, (words - first) * FULL, ext)
    ext = jnp.where(row == 6, code, ext)
    for k in range(2 * TURNS):
        words, code = encode(acc[k * HB : (k + 1) * HB, :])
        out[k * HB : (k + 1) * HB, :] = integer(jnp.floor(words + 0.5))
        ext = jnp.where(row == 8 + k, code, ext)
    out[BAND:, :] = integer(jnp.floor(ext + 0.5))


def collect(which, plan, arrived):
    acc = jax.ShapeDtypeStruct((BAND + 8, BF), F32)
    if which:
        out_shape = jax.ShapeDtypeStruct((BAND + 16, BF), jnp.int16)
        out_specs = VMEM
        scratch = [pltpu.VMEM((BAND + 8, BF), F32), pltpu.VMEM((16, BF), F32)]
    else:
        out_shape = [acc, jax.ShapeDtypeStruct((TURNS, N_COL, BF, BF), F32)]
        out_specs = [VMEM, HBM]
        scratch = [pltpu.VMEM((N_COL, BF, BF), F32), pltpu.SemaphoreType.DMA((TURNS,))]
    return pl.pallas_call(
        functools.partial(collect_kernel, which),
        out_shape=out_shape,
        grid_spec=scalars(1, [VMEM], out_specs, scratch),
        compiler_params=limit(8),
        cost_estimate=pl.CostEstimate(flops=10**6, bytes_accessed=4 * MIB, transcendentals=0),
        name=("collect_own", "collect_other")[which],
    )(plan, arrived)


def merge_kernel(mine, sent, theirs, upper, lower, rest, up_words, low_words):
    eight, _ = lanes((8, BF))
    row, _ = lanes((16, BF))
    got = theirs[BAND:, :].astype(F32)
    own = sent[BAND:, :].astype(F32)

    def line(rows, index):
        return rows[index : index + 1, :]

    def energy(rows):
        return decode(line(rows, 4) + line(rows, 5) * (1.0 / FULL), line(rows, 6))

    more = jnp.where(eight < TURNS, decode(got[:8, :], line(got, 7)), 0.0)
    rest[...] = jnp.where(eight == TURNS, energy(own) + energy(got), mine[BAND:, :] + more)
    for low, full, words in ((0, upper, up_words), (1, lower, low_words)):
        codes = jnp.zeros((16, BF), F32)
        for t in range(TURNS):
            k = low * TURNS + t
            span = slice(k * HB, (k + 1) * HB)
            total = mine[span, :] + decode(theirs[span, :].astype(F32), line(got, 8 + k))
            full[t * HB : (t + 1) * HB, :] = total
            scaled, code = encode(total)
            words[t * HB : (t + 1) * HB, :] = integer(jnp.floor(scaled + 0.5))
            codes = jnp.where(row == t, code, codes)
        words[TURNS * HB :, :] = integer(jnp.floor(codes + 0.5))


def merge(mine, sent, theirs):
    half = jax.ShapeDtypeStruct((TURNS * HB, BF), F32)
    words = jax.ShapeDtypeStruct((TURNS * HB + 16, BF), jnp.int16)
    return pl.pallas_call(
        merge_kernel,
        out_shape=[half, half, jax.ShapeDtypeStruct((8, BF), F32), words, words],
        in_specs=[VMEM] * 3,
        out_specs=[VMEM] * 5,
        compiler_params=limit(4),
        name="merge",
    )(mine, sent, theirs)


def place_kernel(upper, lower, rest, got_upper, got_lower, blank, out, blocks, sems):
    del blank
    row_id, col_id, _ = position()
    shift = (col_id - row_id) & (N_COL - 1)

    def part(ref, turn):
        return ref[pl.ds(pl.multiple_of(turn * HB, HB), HB), :]

    def coded(ref, turn):
        code = pick_row(ref[TURNS * HB :, :].astype(F32), turn)
        return decode(part(ref, turn).astype(F32), code)

    def write(t, low, at):
        slot = TURNS * low + t
        return pltpu.make_async_copy(blocks.at[slot], out.at[t, at], sems.at[slot])

    for finish in (False, True):
        for t in range(TURNS):
            at = (row_id + N_ROW * t + shift) >> 3

            @pl.when((shift > 0) & (at < N_COL))
            def _():
                if finish:
                    write(t, 0, at).wait()
                else:
                    turn = t + jnp.where(row_id + shift >= N_ROW, 1, 0)
                    blocks[t, :HB, :] = part(upper, t)
                    blocks[t, HB:, :] = coded(got_lower, jnp.minimum(turn, TURNS - 1))
                    write(t, 0, at).start()

            @pl.when((shift > 0) & (at > 0))
            def _():
                if finish:
                    write(t, 1, at - 1).wait()
                else:
                    turn = t - jnp.where(row_id + shift < N_COL, 1, 0)
                    top = coded(got_upper, jnp.maximum(turn, 0))
                    blocks[TURNS + t] = jnp.concatenate([top, part(lower, t)], axis=0).T
                    write(t, 1, at - 1).start()

            @pl.when(shift == 0)
            def _():
                if finish:
                    write(t, 0, at).wait()
                else:
                    blocks[t] = unpack_symmetric(part(upper, t), rest[t : t + 1, :])
                    write(t, 0, at).start()


def place(upper, lower, rest, got_upper, got_lower, blank):
    return pl.pallas_call(
        place_kernel,
        out_shape=jax.ShapeDtypeStruct((TURNS, N_COL, BF, BF), F32),
        in_specs=[VMEM] * 5 + [HBM],
        out_specs=HBM,
        scratch_shapes=[
            pltpu.VMEM((2 * TURNS, BF, BF), F32),
            pltpu.SemaphoreType.DMA((2 * TURNS,)),
        ],
        input_output_aliases={5: 0},
        compiler_params=limit(4),
        name="place",
    )(upper, lower, rest, got_upper, got_lower, blank)


def mirror_pairs():
    pairs = []
    for row in range(N_ROW):
        for col in range(N_COL):
            shift = (col - row) % N_COL
            pairs.append((row * N_COL + col, (row + shift) % N_ROW * N_COL + row % N_COL))
    return pairs


def shards(density, basis, weights, batch_start, batch_count):
    swap = [(0, 1), (1, 0)]
    there = mirror_pairs()
    plan = jnp.concatenate([batch_start, batch_count])
    held, sent = share(density)
    theirs = lax.ppermute(sent, "h", swap)
    packed = pack(plan, held, theirs)
    window = lax.all_to_all(packed, GROUP, split_axis=0, concat_axis=0, tiled=True)

    outgoing = batches(plan, weights, basis, turn(plan, basis), window)
    arrived = lax.all_to_all(outgoing, GROUP, split_axis=0, concat_axis=0, tiled=True)

    sent = collect(1, plan, arrived)
    theirs = lax.ppermute(sent, "h", swap)
    mine, blank = collect(0, plan, arrived)
    upper, lower, rest, up_words, low_words = merge(mine, sent, theirs)
    got_upper = lax.ppermute(up_words, ALL, there)
    got_lower = lax.ppermute(low_words, ALL, [(d, s) for s, d in there])
    potential = place(upper, lower, rest, got_upper, got_lower, blank)
    return potential, rest[TURNS, 0] / (NBLK * BF)


def solution(mesh):
    fine = Mesh(np.asarray(mesh.devices).reshape(2, 2, 4, 4, 2), ALL)
    in_specs = (P(ROW, COL), P(ALL), P(ALL), P(), P())
    out_specs = (P(ROW, COL), P())
    return jax.shard_map(shards, mesh=fine, in_specs=in_specs, out_specs=out_specs, check_vma=False)
```

```python
import functools
import math

import jax
import jax.numpy as jnp
import numpy as np
from jax import lax
from jax.experimental import pallas as pl
from jax.experimental.pallas import tpu as pltpu
from jax.sharding import Mesh, PartitionSpec as P

CX = 0.7385587663820224
MU = 0.2195149727645171
KAPPA = 0.804
BF = 128
KB = 8
NBLK = 64
G = 256
SLOTS = 3
KF = 1024
N_ROW = 16
N_COL = 8
TURNS = NBLK // N_ROW
PEERS = 64
MIB = 1024 * 1024
HB = BF // 2
EXT = SLOTS * HB
ROWS = EXT + 16
BAND = 2 * TURNS * HB
ROW = ("h", "xl", "y")
COL = ("z", "c")
ALL = ROW + COL
GROUP = ("xl", "y", "z", "c")
VMEM = pl.BlockSpec(memory_space=pltpu.VMEM)
HBM = pl.BlockSpec(memory_space=pltpu.HBM)
F32 = jnp.float32
BF16 = jnp.bfloat16


def lanes(shape):
    return lax.broadcasted_iota(jnp.int32, shape, 0), lax.broadcasted_iota(jnp.int32, shape, 1)


def pack_symmetric(full):
    r, c = lanes((HB, BF))
    top, bottom = full[:HB], full[HB:]
    packed = jnp.where((c >= HB) | (r <= c), top, pltpu.roll(bottom, HB, 1))
    row = jnp.sum(jnp.where(c - HB == r, bottom, 0.0), axis=0, keepdims=True)
    return packed, row


def unpack_symmetric(packed, row):
    r, c = lanes((HB, BF))
    flip = jnp.concatenate([packed, packed], axis=0).T
    top = jnp.where((c >= HB) | (r <= c), packed, flip[:HB])
    corner = jnp.where(c - HB < r, pltpu.roll(packed, HB, 1), flip[:HB])
    corner = jnp.where(c - HB == r, row, corner)
    return jnp.concatenate([top, jnp.where(c < HB, flip[HB:], corner)], axis=0)


def pick_row(rows, index):
    r, _ = lanes(rows.shape)
    return jnp.sum(jnp.where(r == index, rows, 0.0), axis=0, keepdims=True)


def position():
    h = lax.axis_index("h")
    row_id = (h * 2 + lax.axis_index("xl")) * 4 + lax.axis_index("y")
    return row_id, lax.axis_index("z") * 2 + lax.axis_index("c"), h


def live(plan, device):
    return plan[N_ROW * N_COL * SLOTS + device]


def entry(plan, peer, slot, where):
    row_id, col_id, h = where
    start = plan[(h * PEERS + peer) * SLOTS + slot]
    i = start + ((row_id - start) & (KB - 1))
    j = start + ((col_id - start) & (KB - 1))
    other = ((i >> 3) & 1) ^ h
    turn = i >> 4
    below = jnp.where(j < i, TURNS, 0)
    return other, turn, pl.multiple_of((below + turn) * HB, HB)


def scalars(count, in_specs, out_specs, scratch_shapes=()):
    return pltpu.PrefetchScalarGridSpec(
        num_scalar_prefetch=count,
        grid=(),
        in_specs=in_specs,
        out_specs=out_specs,
        scratch_shapes=list(scratch_shapes),
    )


def limit(mib):
    return pltpu.CompilerParams(vmem_limit_bytes=mib * MIB)


def share_kernel(density, out, copy, ups, lows, sems):
    row_id, col_id, _ = position()
    shift = (col_id - row_id) & (N_COL - 1)
    row, _ = lanes((16, BF))
    loads = []
    for t in range(TURNS):
        at = (row_id + N_ROW * t + shift) >> 3
        up = density.at[t, jnp.minimum(at, N_COL - 1)]
        low = density.at[t, jnp.maximum(at - 1, 0)]
        loads.append(pltpu.make_async_copy(up, ups.at[t], sems.at[t]))
        loads.append(pltpu.make_async_copy(low, lows.at[t], sems.at[TURNS + t]))
    for load in loads:
        load.start()
    for load in loads:
        load.wait()

    @pl.when(shift > 0)
    def _():
        for t in range(TURNS):
            low = TURNS * HB + t * HB
            out[t * HB : (t + 1) * HB, :] = ups[t, :HB, :]
            out[low : low + HB, :] = lows[t].astype(F32).T[HB:].astype(BF16)
        out[BAND:, :] = jnp.zeros((16, BF), BF16)

    @pl.when(shift == 0)
    def _():
        ext = jnp.zeros((16, BF), F32)
        for t in range(TURNS):
            packed, line = pack_symmetric(ups[t].astype(F32))
            out[t * HB : (t + 1) * HB, :] = packed.astype(BF16)
            ext = jnp.where(row == t, line, ext)
        out[TURNS * HB : BAND, :] = jnp.zeros((TURNS * HB, BF), BF16)
        out[BAND:, :] = ext.astype(BF16)

    copy[...] = out[...]


def share(density):
    held = jax.ShapeDtypeStruct((BAND + 16, BF), BF16)
    return pl.pallas_call(
        share_kernel,
        out_shape=[held, held],
        in_specs=[HBM],
        out_specs=[VMEM, VMEM],
        scratch_shapes=[
            pltpu.VMEM((TURNS, BF, BF), BF16),
            pltpu.VMEM((TURNS, BF, BF), BF16),
            pltpu.SemaphoreType.DMA((2 * TURNS,)),
        ],
        compiler_params=limit(60),
        name="share",
    )(density)


CHUNK = 8


def pack_kernel(plan, mine, theirs, out, table, lines, buf, sems):
    where = position()
    on_diagonal = ((where[1] - where[0]) & (KB - 1)) == 0
    table[0] = mine[:BAND, :]
    table[1] = theirs[:BAND, :]
    lines[0] = mine[BAND:, :].astype(F32)
    lines[1] = theirs[BAND:, :].astype(F32)
    row, _ = lanes((16, BF))

    def send(chunk):
        span = pl.ds(pl.multiple_of(chunk * CHUNK, CHUNK), CHUNK)
        return pltpu.make_async_copy(buf.at[span], out.at[span], sems.at[chunk])

    def one_chunk(chunk, carry):
        for k in range(CHUNK):
            peer = chunk * CHUNK + k
            count = live(plan, where[2] * PEERS + peer)

            def one(slot):
                other, _, at = entry(plan, peer, slot, where)
                buf[peer, slot * HB : (slot + 1) * HB, :] = table[other, pl.ds(at, HB), :]

            one(0)
            for slot in range(1, SLOTS):
                pl.when(slot < count)(lambda slot=slot: one(slot))

            @pl.when(on_diagonal)
            def _():
                ext = jnp.zeros((16, BF), F32)
                for slot in range(SLOTS):
                    other, turn, _ = entry(plan, peer, slot, where)
                    ext = jnp.where(row == slot, lines[other, pl.ds(turn, 1), :], ext)
                buf[peer, EXT:, :] = ext.astype(BF16)

        send(chunk).start()
        return carry

    lax.fori_loop(0, PEERS // CHUNK, one_chunk, 0)

    def drain(chunk, carry):
        send(chunk).wait()
        return carry

    lax.fori_loop(0, PEERS // CHUNK, drain, 0)


def pack(plan, mine, theirs):
    return pl.pallas_call(
        pack_kernel,
        out_shape=jax.ShapeDtypeStruct((PEERS, ROWS, BF), BF16),
        grid_spec=scalars(
            1,
            [VMEM, VMEM],
            HBM,
            [
                pltpu.VMEM((2, BAND, BF), BF16),
                pltpu.VMEM((2, 16, BF), F32),
                pltpu.VMEM((PEERS, ROWS, BF), BF16),
                pltpu.SemaphoreType.DMA((PEERS // CHUNK,)),
            ],
        ),
        compiler_params=limit(8),
        name="pack",
    )(plan, mine, theirs)


def turn_kernel(plan, basis, out, held, sems):
    row_id, col_id, _ = position()
    count = live(plan, row_id * N_COL + col_id)

    def load(slot):
        return pltpu.make_async_copy(basis.at[slot], held.at[slot], sems.at[slot])

    def fetch(slot, carry):
        load(slot).start()
        return carry

    def work(slot, carry):
        load(slot).wait()
        for k in range(4):
            for o in range(KB):
                span = slice(o * BF, (o + 1) * BF)
                out[slot, k, span, :] = held[slot, k, :, span].T
        return carry

    lax.fori_loop(0, count, fetch, 0)
    lax.fori_loop(0, count, work, 0)


def turn(plan, basis):
    return pl.pallas_call(
        turn_kernel,
        out_shape=jax.ShapeDtypeStruct((SLOTS, 4, KF, G), BF16),
        grid_spec=scalars(
            1,
            [HBM],
            VMEM,
            [
                pltpu.VMEM((SLOTS, 4, G, KF), BF16),
                pltpu.SemaphoreType.DMA((SLOTS,)),
            ],
        ),
        compiler_params=limit(44),
        cost_estimate=pl.CostEstimate(flops=10**6, bytes_accessed=24 * MIB, transcendentals=0),
        name="turn",
    )(plan, basis)


def dot_nt(x, y):
    return lax.dot_general(x, y, (((1,), (1,)), ((), ())), preferred_element_type=F32)


def batch_kernel(
    plan, weights, turned, window, out, mat, product, left, right, lines
):
    row_id, col_id, _ = position()
    me = row_id * N_COL + col_id
    count = live(plan, me)
    row, lane = lanes((16, BF))
    lines[...] = jnp.zeros(lines.shape, F32)

    def work(slot, total):
        start = plan[me * SLOTS + slot]
        cls = [(start + o) & (KB - 1) for o in range(KB)]
        span = pl.ds(pl.multiple_of(slot * HB, HB), HB)
        for o1 in range(KB):
            r1 = slice(o1 * BF, (o1 + 1) * BF)
            for o2 in range(o1 + 1, KB):
                r2 = slice(o2 * BF, (o2 + 1) * BF)
                top = window[cls[o1] * KB + cls[o2], span, :]
                bottom = window[cls[o2] * KB + cls[o1], span, :]
                block = jnp.concatenate([top, bottom], axis=0)
                mat[r1, r2] = block
                mat[r2, r1] = block.T
            diagonal = cls[o1] * (KB + 1)
            line = pick_row(window[diagonal, EXT:, :].astype(F32), slot)
            block = unpack_symmetric(window[diagonal, span, :].astype(F32), line)
            mat[r1, r1] = block.astype(BF16)
        for t in range(4):
            part = slice(256 * t, 256 * (t + 1))
            product[part, :] = jnp.dot(mat[part, :], turned[slot, 0], preferred_element_type=F32)
        sums = [jnp.zeros((8, G), F32) for _ in range(4)]
        for t in range(KF // BF):
            span_t = slice(t * BF, (t + 1) * BF)
            for k in range(4):
                terms = turned[slot, k, span_t, :].astype(F32) * product[span_t, :]
                sums[k] += jnp.sum(terms.reshape(BF // 8, 8, G), axis=0)
        sums = [jnp.sum(x, axis=0, keepdims=True) for x in sums]
        rho = sums[0]
        grads = [2.0 * x for x in sums[1:]]
        sigma = grads[0] * grads[0] + grads[1] * grads[1] + grads[2] * grads[2]
        quad = weights[pl.ds(slot, 1), :]
        square = rho * rho + 1.0
        logs = jnp.log(square)
        cube = jnp.exp(logs * (1.0 / 3.0))
        scaled = cube * cube
        reduced = sigma / (scaled * scaled)
        denom = 1.0 + MU * reduced / KAPPA
        factor = 1.0 + MU * reduced / denom
        slope = MU / denom / denom
        point = -CX * scaled * factor
        by_rho = (-CX * 2.0) * rho / cube * ((2.0 / 3.0) * factor - (4.0 / 3.0) * slope * reduced)
        by_sigma = -CX * slope / scaled
        wr = 0.5 * quad * by_rho
        ws = 2.0 * quad * by_sigma
        total = total + jnp.sum(quad * point)
        coeffs = [wr] + [ws * x for x in grads]
        for t in range(4):
            lo, hi = 256 * t, 256 * (t + 1)
            phi = turned[slot, 0, lo:hi, :]
            mixed = coeffs[0] * phi.astype(F32)
            for k in range(1, 4):
                mixed += coeffs[k] * turned[slot, k, lo:hi, :].astype(F32)
            mixed = mixed.astype(BF16)
            left[lo:hi, :G] = phi
            left[lo:hi, G:] = mixed
            right[lo:hi, :G] = mixed
            right[lo:hi, G:] = phi
        for t in range(4):
            lo, hi = 256 * t, 256 * (t + 1)
            rows = dot_nt(left[lo:hi, :], right[lo:, :])
            for k in range(2):
                o1 = 2 * t + k
                for o2 in range(o1, KB):
                    c0 = o2 * BF - lo
                    block = rows[k * BF : (k + 1) * BF, c0 : c0 + BF]
                    if o2 == o1:
                        packed, line = pack_symmetric(block)
                        out[cls[o1] * (KB + 1), span, :] = packed.astype(BF16)
                        lines[cls[o1]] = jnp.where(row == slot, line, lines[cls[o1]])
                    else:
                        out[cls[o1] * KB + cls[o2], span, :] = block[:HB].astype(BF16)
                        out[cls[o2] * KB + cls[o1], span, :] = block[HB:].astype(BF16)
        return total

    total = jnp.full((16, BF), lax.fori_loop(0, count, work, jnp.float32(0.0)), F32)
    first = total.astype(BF16).astype(F32)
    second = (total - first).astype(BF16).astype(F32)
    third = total - first - second
    spread = jnp.where(lane == 0, first, jnp.where(lane == 1, second, third))
    energy = jnp.where((row == 0) & (lane < 3), spread, 0.0)
    for peer in range(PEERS):
        if peer % (KB + 1) == 0:
            out[peer, EXT:, :] = (lines[peer // (KB + 1)] + energy).astype(BF16)
        else:
            out[peer, EXT:, :] = energy.astype(BF16)


def batches(plan, weights, flipped, window):
    return pl.pallas_call(
        batch_kernel,
        out_shape=jax.ShapeDtypeStruct((PEERS, ROWS, BF), BF16),
        grid_spec=scalars(
            1,
            [VMEM, VMEM, VMEM],
            VMEM,
            [
                pltpu.VMEM((KF, KF), BF16),
                pltpu.VMEM((KF, G), F32),
                pltpu.VMEM((KF, 2 * G), BF16),
                pltpu.VMEM((KF, 2 * G), BF16),
                pltpu.VMEM((KB, 16, BF), F32),
            ],
        ),
        compiler_params=limit(28),
        name="batches",
    )(plan, weights, flipped, window)


STEP = math.log(2.0) / 128.0
FULL = 32767.0


def integer(values):
    return values.astype(jnp.int32).astype(jnp.int16)


def encode(values):
    top = jnp.max(jnp.max(jnp.abs(values), axis=0, keepdims=True), axis=1, keepdims=True)
    code = jnp.ceil(jnp.log(jnp.maximum(top, 2.0**-110)) * (1.0 / STEP))
    scaled = values * jnp.exp(math.log(FULL) - code * STEP)
    return jnp.clip(scaled, -FULL, FULL), code


def decode(words, code):
    return words.astype(F32) * jnp.exp(code.astype(F32) * STEP - math.log(FULL))


def collect_kernel(which, plan, arrived, *refs):
    where = position()
    on_diagonal = ((where[1] - where[0]) & (KB - 1)) == 0
    row, lane = lanes((16, BF))
    eight, _ = lanes((8, BF))
    if which:
        out, acc, energy = refs
        energy[...] = jnp.zeros(energy.shape, F32)
    else:
        acc, blank, zeros, sems = refs
        zeros[...] = jnp.zeros(zeros.shape, F32)
        fills = [pltpu.make_async_copy(zeros, blank.at[t], sems.at[t]) for t in range(TURNS)]
        for fill in fills:
            fill.start()
    acc[...] = jnp.zeros(acc.shape, F32)

    def one_chunk(chunk, carry):
        for k in range(CHUNK):
            peer = chunk * CHUNK + k
            count = live(plan, where[2] * PEERS + peer)
            if which:
                energy[...] += arrived[peer, EXT:, :].astype(F32)

            def one(slot, used):
                other, turn, at = entry(plan, peer, slot, where)
                wanted = other == which

                @pl.when(wanted if used is None else wanted & used)
                def _():
                    part = arrived[peer, slot * HB : (slot + 1) * HB, :]
                    acc[pl.ds(at, HB), :] += part.astype(F32)

                    @pl.when(on_diagonal)
                    def _():
                        ext = arrived[peer, EXT:, :].astype(F32)
                        line = jnp.where((row == slot) & (lane >= HB), ext, 0.0)
                        line = jnp.sum(line, axis=0, keepdims=True)
                        acc[BAND:, :] += jnp.where(eight == turn, line, 0.0)

            one(0, None)
            for slot in range(1, SLOTS):
                one(slot, slot < count)
        return carry

    lax.fori_loop(0, PEERS // CHUNK, one_chunk, 0)
    if not which:
        for fill in fills:
            fill.wait()
        return

    words, code = encode(acc[BAND:, :])
    ext = jnp.concatenate([words, words], axis=0)
    ext = jnp.where(row == 7, code, ext)
    total = jnp.where((row == 0) & (lane < 3), energy[...], 0.0)
    total = jnp.sum(jnp.sum(total, axis=0, keepdims=True), axis=1, keepdims=True)
    words, code = encode(total)
    first = jnp.floor(words + 0.5)
    ext = jnp.where(row == 4, first, ext)
    ext = jnp.where(row == 5, (words - first) * FULL, ext)
    ext = jnp.where(row == 6, code, ext)
    for k in range(2 * TURNS):
        words, code = encode(acc[k * HB : (k + 1) * HB, :])
        out[k * HB : (k + 1) * HB, :] = integer(jnp.floor(words + 0.5))
        ext = jnp.where(row == 8 + k, code, ext)
    out[BAND:, :] = integer(jnp.floor(ext + 0.5))


def collect(which, plan, arrived):
    acc = jax.ShapeDtypeStruct((BAND + 8, BF), F32)
    if which:
        out_shape = jax.ShapeDtypeStruct((BAND + 16, BF), jnp.int16)
        out_specs = VMEM
        scratch = [pltpu.VMEM((BAND + 8, BF), F32), pltpu.VMEM((16, BF), F32)]
    else:
        out_shape = [acc, jax.ShapeDtypeStruct((TURNS, N_COL, BF, BF), F32)]
        out_specs = [VMEM, HBM]
        scratch = [pltpu.VMEM((N_COL, BF, BF), F32), pltpu.SemaphoreType.DMA((TURNS,))]
    return pl.pallas_call(
        functools.partial(collect_kernel, which),
        out_shape=out_shape,
        grid_spec=scalars(1, [VMEM], out_specs, scratch),
        compiler_params=limit(8),
        cost_estimate=pl.CostEstimate(flops=10**6, bytes_accessed=4 * MIB, transcendentals=0),
        name=("collect_own", "collect_other")[which],
    )(plan, arrived)


def merge_kernel(mine, sent, theirs, upper, lower, rest, up_words, low_words):
    eight, _ = lanes((8, BF))
    row, _ = lanes((16, BF))
    got = theirs[BAND:, :].astype(F32)
    own = sent[BAND:, :].astype(F32)

    def line(rows, index):
        return rows[index : index + 1, :]

    def energy(rows):
        return decode(line(rows, 4) + line(rows, 5) * (1.0 / FULL), line(rows, 6))

    more = jnp.where(eight < TURNS, decode(got[:8, :], line(got, 7)), 0.0)
    rest[...] = jnp.where(eight == TURNS, energy(own) + energy(got), mine[BAND:, :] + more)
    for low, full, words in ((0, upper, up_words), (1, lower, low_words)):
        codes = jnp.zeros((16, BF), F32)
        for t in range(TURNS):
            k = low * TURNS + t
            span = slice(k * HB, (k + 1) * HB)
            total = mine[span, :] + decode(theirs[span, :].astype(F32), line(got, 8 + k))
            full[t * HB : (t + 1) * HB, :] = total
            scaled, code = encode(total)
            words[t * HB : (t + 1) * HB, :] = integer(jnp.floor(scaled + 0.5))
            codes = jnp.where(row == t, code, codes)
        words[TURNS * HB :, :] = integer(jnp.floor(codes + 0.5))


def merge(mine, sent, theirs):
    half = jax.ShapeDtypeStruct((TURNS * HB, BF), F32)
    words = jax.ShapeDtypeStruct((TURNS * HB + 16, BF), jnp.int16)
    return pl.pallas_call(
        merge_kernel,
        out_shape=[half, half, jax.ShapeDtypeStruct((8, BF), F32), words, words],
        in_specs=[VMEM] * 3,
        out_specs=[VMEM] * 5,
        compiler_params=limit(4),
        name="merge",
    )(mine, sent, theirs)


def place_kernel(upper, lower, rest, got_upper, got_lower, blank, out, blocks, sems):
    del blank
    row_id, col_id, _ = position()
    shift = (col_id - row_id) & (N_COL - 1)

    def part(ref, turn):
        return ref[pl.ds(pl.multiple_of(turn * HB, HB), HB), :]

    def coded(ref, turn):
        code = pick_row(ref[TURNS * HB :, :].astype(F32), turn)
        return decode(part(ref, turn).astype(F32), code)

    def write(t, low, at):
        slot = TURNS * low + t
        return pltpu.make_async_copy(blocks.at[slot], out.at[t, at], sems.at[slot])

    for finish in (False, True):
        for t in range(TURNS):
            at = (row_id + N_ROW * t + shift) >> 3

            @pl.when((shift > 0) & (at < N_COL))
            def _():
                if finish:
                    write(t, 0, at).wait()
                else:
                    turn = t + jnp.where(row_id + shift >= N_ROW, 1, 0)
                    blocks[t, :HB, :] = part(upper, t)
                    blocks[t, HB:, :] = coded(got_lower, jnp.minimum(turn, TURNS - 1))
                    write(t, 0, at).start()

            @pl.when((shift > 0) & (at > 0))
            def _():
                if finish:
                    write(t, 1, at - 1).wait()
                else:
                    turn = t - jnp.where(row_id + shift < N_COL, 1, 0)
                    top = coded(got_upper, jnp.maximum(turn, 0))
                    blocks[TURNS + t] = jnp.concatenate([top, part(lower, t)], axis=0).T
                    write(t, 1, at - 1).start()

            @pl.when(shift == 0)
            def _():
                if finish:
                    write(t, 0, at).wait()
                else:
                    blocks[t] = unpack_symmetric(part(upper, t), rest[t : t + 1, :])
                    write(t, 0, at).start()


def place(upper, lower, rest, got_upper, got_lower, blank):
    return pl.pallas_call(
        place_kernel,
        out_shape=jax.ShapeDtypeStruct((TURNS, N_COL, BF, BF), F32),
        in_specs=[VMEM] * 5 + [HBM],
        out_specs=HBM,
        scratch_shapes=[
            pltpu.VMEM((2 * TURNS, BF, BF), F32),
            pltpu.SemaphoreType.DMA((2 * TURNS,)),
        ],
        input_output_aliases={5: 0},
        compiler_params=limit(4),
        name="place",
    )(upper, lower, rest, got_upper, got_lower, blank)


def mirror_pairs():
    pairs = []
    for row in range(N_ROW):
        for col in range(N_COL):
            shift = (col - row) % N_COL
            pairs.append((row * N_COL + col, (row + shift) % N_ROW * N_COL + row % N_COL))
    return pairs


def shards(density, basis, weights, batch_start, batch_count):
    swap = [(0, 1), (1, 0)]
    there = mirror_pairs()
    plan = jnp.concatenate([batch_start, batch_count])
    held, sent = share(density)
    theirs = lax.ppermute(sent, "h", swap)
    packed = pack(plan, held, theirs)
    window = lax.all_to_all(packed, GROUP, split_axis=0, concat_axis=0, tiled=True)

    outgoing = batches(plan, weights, turn(plan, basis), window)
    arrived = lax.all_to_all(outgoing, GROUP, split_axis=0, concat_axis=0, tiled=True)

    sent = collect(1, plan, arrived)
    theirs = lax.ppermute(sent, "h", swap)
    mine, blank = collect(0, plan, arrived)
    upper, lower, rest, up_words, low_words = merge(mine, sent, theirs)
    got_upper = lax.ppermute(up_words, ALL, there)
    got_lower = lax.ppermute(low_words, ALL, [(d, s) for s, d in there])
    potential = place(upper, lower, rest, got_upper, got_lower, blank)
    return potential, rest[TURNS, 0] / (NBLK * BF)


def solution(mesh):
    fine = Mesh(np.asarray(mesh.devices).reshape(2, 2, 4, 4, 2), ALL)
    in_specs = (P(ROW, COL), P(ALL), P(ALL), P(), P())
    out_specs = (P(ROW, COL), P())
    return jax.shard_map(shards, mesh=fine, in_specs=in_specs, out_specs=out_specs, check_vma=False)
```

```python
import functools
import math

import jax
import jax.numpy as jnp
import numpy as np
from jax import lax
from jax.experimental import pallas as pl
from jax.experimental.pallas import tpu as pltpu
from jax.sharding import Mesh, PartitionSpec as P

CX = 0.7385587663820224
MU = 0.2195149727645171
KAPPA = 0.804
BF = 128
KB = 8
NBLK = 64
G = 256
SLOTS = 3
KF = 1024
N_ROW = 16
N_COL = 8
TURNS = NBLK // N_ROW
PEERS = 64
MIB = 1024 * 1024
HB = BF // 2
EXT = SLOTS * HB
ROWS = EXT + 16
BAND = 2 * TURNS * HB
ROW = ("h", "xl", "y")
COL = ("z", "c")
ALL = ROW + COL
GROUP = ("xl", "y", "z", "c")
VMEM = pl.BlockSpec(memory_space=pltpu.VMEM)
HBM = pl.BlockSpec(memory_space=pltpu.HBM)
F32 = jnp.float32
BF16 = jnp.bfloat16


def lanes(shape):
    return lax.broadcasted_iota(jnp.int32, shape, 0), lax.broadcasted_iota(jnp.int32, shape, 1)


def pack_symmetric(full):
    r, c = lanes((HB, BF))
    top, bottom = full[:HB], full[HB:]
    packed = jnp.where((c >= HB) | (r <= c), top, pltpu.roll(bottom, HB, 1))
    row = jnp.sum(jnp.where(c - HB == r, bottom, 0.0), axis=0, keepdims=True)
    return packed, row


def unpack_symmetric(packed, row):
    r, c = lanes((HB, BF))
    flip = jnp.concatenate([packed, packed], axis=0).T
    top = jnp.where((c >= HB) | (r <= c), packed, flip[:HB])
    corner = jnp.where(c - HB < r, pltpu.roll(packed, HB, 1), flip[:HB])
    corner = jnp.where(c - HB == r, row, corner)
    return jnp.concatenate([top, jnp.where(c < HB, flip[HB:], corner)], axis=0)


def pick_row(rows, index):
    r, _ = lanes(rows.shape)
    return jnp.sum(jnp.where(r == index, rows, 0.0), axis=0, keepdims=True)


def position():
    h = lax.axis_index("h")
    row_id = (h * 2 + lax.axis_index("xl")) * 4 + lax.axis_index("y")
    return row_id, lax.axis_index("z") * 2 + lax.axis_index("c"), h


def live(plan, device):
    return plan[N_ROW * N_COL * SLOTS + device]


def entry(plan, peer, slot, where):
    row_id, col_id, h = where
    start = plan[(h * PEERS + peer) * SLOTS + slot]
    i = start + ((row_id - start) & (KB - 1))
    j = start + ((col_id - start) & (KB - 1))
    other = ((i >> 3) & 1) ^ h
    turn = i >> 4
    below = jnp.where(j < i, TURNS, 0)
    return other, turn, below + turn


def scalars(count, in_specs, out_specs, scratch_shapes=()):
    return pltpu.PrefetchScalarGridSpec(
        num_scalar_prefetch=count,
        grid=(),
        in_specs=in_specs,
        out_specs=out_specs,
        scratch_shapes=list(scratch_shapes),
    )


def limit(mib):
    return pltpu.CompilerParams(vmem_limit_bytes=mib * MIB)


def share_kernel(density, out, copy, ups, lows, sems):
    row_id, col_id, _ = position()
    shift = (col_id - row_id) & (N_COL - 1)
    row, _ = lanes((16, BF))
    loads = []
    for t in range(TURNS):
        at = (row_id + N_ROW * t + shift) >> 3
        up = density.at[t, jnp.minimum(at, N_COL - 1)]
        low = density.at[t, jnp.maximum(at - 1, 0)]
        loads.append(pltpu.make_async_copy(up, ups.at[t], sems.at[t]))
        loads.append(pltpu.make_async_copy(low, lows.at[t], sems.at[TURNS + t]))
    for load in loads:
        load.start()
    for load in loads:
        load.wait()

    @pl.when(shift > 0)
    def _():
        for t in range(TURNS):
            low = TURNS * HB + t * HB
            out[t * HB : (t + 1) * HB, :] = ups[t, :HB, :]
            out[low : low + HB, :] = lows[t].astype(F32).T[HB:].astype(BF16)
        out[BAND:, :] = jnp.zeros((16, BF), BF16)

    @pl.when(shift == 0)
    def _():
        ext = jnp.zeros((16, BF), F32)
        for t in range(TURNS):
            packed, line = pack_symmetric(ups[t].astype(F32))
            out[t * HB : (t + 1) * HB, :] = packed.astype(BF16)
            ext = jnp.where(row == t, line, ext)
        out[TURNS * HB : BAND, :] = jnp.zeros((TURNS * HB, BF), BF16)
        out[BAND:, :] = ext.astype(BF16)

    copy[...] = out[...]


def share(density):
    held = jax.ShapeDtypeStruct((BAND + 16, BF), BF16)
    return pl.pallas_call(
        share_kernel,
        out_shape=[held, held],
        in_specs=[HBM],
        out_specs=[VMEM, VMEM],
        scratch_shapes=[
            pltpu.VMEM((TURNS, BF, BF), BF16),
            pltpu.VMEM((TURNS, BF, BF), BF16),
            pltpu.SemaphoreType.DMA((2 * TURNS,)),
        ],
        compiler_params=limit(4),
        name="share",
    )(density)


CHUNK = 8
ALL_SLOTS = PEERS * SLOTS
BOUNDS = 2 * ALL_SLOTS
STRIDE = 16


def route_kernel(plan, table):
    where = position()

    def one_peer(peer, ends):
        count = live(plan, where[2] * PEERS + peer)

        @pl.when((peer & (CHUNK - 1)) == 0)
        def _():
            for which in range(2):
                table[BOUNDS + which * STRIDE + peer // CHUNK] = ends[which]

        for slot in range(SLOTS):
            other, _, at = entry(plan, peer, slot, where)
            used = jnp.where(slot < count, 1, 0)
            index = jnp.where(other == 1, ends[1], ALL_SLOTS + ends[0])
            table[index] = peer + slot * PEERS + at * (4 * PEERS)
            ends = (ends[0] + used * (1 - other), ends[1] + used * other)
        return ends

    ends = lax.fori_loop(0, PEERS, one_peer, (jnp.int32(0), jnp.int32(0)))
    for which in range(2):
        table[BOUNDS + which * STRIDE + PEERS // CHUNK] = ends[which]


def route(plan):
    return pl.pallas_call(
        route_kernel,
        out_shape=jax.ShapeDtypeStruct((BOUNDS + 2 * STRIDE,), jnp.int32),
        grid_spec=scalars(1, [], pl.BlockSpec(memory_space=pltpu.SMEM)),
        compiler_params=limit(4),
        cost_estimate=pl.CostEstimate(flops=10**6, bytes_accessed=4 * MIB, transcendentals=0),
        name="route",
    )(plan)


def first_of(table, which, chunk):
    return table[BOUNDS + which * STRIDE + chunk]


def walk(table, which, low, high, body):
    base = 0 if which else ALL_SLOTS

    def step(index, carry):
        code = table[base + index]
        slot = (code >> 6) & 3
        at = pl.multiple_of((code >> 8) * HB, HB)
        body(code & (PEERS - 1), pl.multiple_of(slot * HB, HB), at, slot)
        return carry

    lax.fori_loop(low, high, step, 0)


def pack_kernel(table, mine, theirs, out, buf, sems):
    row_id, col_id, h = position()
    row, _ = lanes((16, BF))
    held = (mine, theirs)

    @pl.when(((col_id - row_id) & (KB - 1)) == 0)
    def _():
        ext = jnp.zeros((16, BF), F32)
        for which in range(2):
            lines = held[which][BAND:, :].astype(F32)
            for turn in range(TURNS):
                at = 2 * turn + (h ^ which)
                ext = jnp.where(row == at, lines[turn : turn + 1, :], ext)
        ext = ext.astype(BF16)
        for peer in range(PEERS):
            buf[peer, EXT:, :] = ext

    def send(chunk):
        span = pl.ds(pl.multiple_of(chunk * CHUNK, CHUNK), CHUNK)
        return pltpu.make_async_copy(buf.at[span], out.at[span], sems.at[chunk])

    def one_chunk(chunk, carry):
        for which in range(2):

            def copy(peer, span, at, slot):
                buf[peer, pl.ds(span, HB), :] = held[which][pl.ds(at, HB), :]

            low, high = first_of(table, which, chunk), first_of(table, which, chunk + 1)
            walk(table, which, low, high, copy)
        send(chunk).start()
        return carry

    lax.fori_loop(0, PEERS // CHUNK, one_chunk, 0)

    def drain(chunk, carry):
        send(chunk).wait()
        return carry

    lax.fori_loop(0, PEERS // CHUNK, drain, 0)


def pack(table, mine, theirs):
    return pl.pallas_call(
        pack_kernel,
        out_shape=jax.ShapeDtypeStruct((PEERS, ROWS, BF), BF16),
        grid_spec=scalars(
            1,
            [VMEM, VMEM],
            HBM,
            [
                pltpu.VMEM((PEERS, ROWS, BF), BF16),
                pltpu.SemaphoreType.DMA((PEERS // CHUNK,)),
            ],
        ),
        compiler_params=limit(8),
        name="pack",
    )(table, mine, theirs)


def turn_kernel(plan, basis, out, held, turned, sem_in, sem_out):
    row_id, col_id, _ = position()
    count = live(plan, row_id * N_COL + col_id)

    def load(slot):
        return pltpu.make_async_copy(basis.at[slot], held.at[slot], sem_in.at[slot])

    def store(slot):
        return pltpu.make_async_copy(turned.at[slot], out.at[slot], sem_out.at[slot])

    def fetch(slot, carry):
        load(slot).start()
        return carry

    def work(slot, carry):
        load(slot).wait()
        for k in range(4):
            for o in range(KB):
                span = slice(o * BF, (o + 1) * BF)
                turned[slot, k, span, :] = held[slot, k, :, span].T
        store(slot).start()
        return carry

    def drain(slot, carry):
        store(slot).wait()
        return carry

    lax.fori_loop(0, count, fetch, 0)
    lax.fori_loop(0, count, work, 0)
    lax.fori_loop(0, count, drain, 0)


def turn(plan, basis):
    return pl.pallas_call(
        turn_kernel,
        out_shape=jax.ShapeDtypeStruct((SLOTS, 4, KF, G), BF16),
        grid_spec=scalars(
            1,
            [HBM],
            HBM,
            [
                pltpu.VMEM((SLOTS, 4, G, KF), BF16),
                pltpu.VMEM((SLOTS, 4, KF, G), BF16),
                pltpu.SemaphoreType.DMA((SLOTS,)),
                pltpu.SemaphoreType.DMA((SLOTS,)),
            ],
        ),
        compiler_params=limit(48),
        cost_estimate=pl.CostEstimate(flops=10**6, bytes_accessed=24 * MIB, transcendentals=0),
        name="turn",
    )(plan, basis)


def dot_nt(x, y):
    return lax.dot_general(x, y, (((1,), (1,)), ((), ())), preferred_element_type=F32)


def batch_kernel(
    plan, weights, flipped, window, out, turned, mat, product, left, right, lines, sems
):
    row_id, col_id, _ = position()
    me = row_id * N_COL + col_id
    count = live(plan, me)
    row, lane = lanes((16, BF))

    def flipped_copy(slot, k):
        return pltpu.make_async_copy(flipped.at[slot, k], turned.at[slot, k], sems.at[slot, k])

    def fetch(slot, carry):
        for k in range(4):
            flipped_copy(slot, k).start()
        return carry

    lax.fori_loop(0, count, fetch, 0)
    lines[...] = jnp.zeros(lines.shape, F32)

    def classes(slot):
        start = plan[me * SLOTS + slot]
        return start, [(start + o) & (KB - 1) for o in range(KB)]

    def rows_of(slot):
        return pl.ds(pl.multiple_of(slot * HB, HB), HB)

    def assemble(slot):
        start, cls = classes(slot)
        span = rows_of(slot)
        for o1 in range(KB):
            r1 = slice(o1 * BF, (o1 + 1) * BF)
            for o2 in range(o1 + 1, KB):
                r2 = slice(o2 * BF, (o2 + 1) * BF)
                top = window[cls[o1] * KB + cls[o2], span, :]
                bottom = window[cls[o2] * KB + cls[o1], span, :]
                block = jnp.concatenate([top, bottom], axis=0)
                mat[r1, r2] = block
                mat[r2, r1] = block.T
            diagonal = cls[o1] * (KB + 1)
            line = pick_row(window[diagonal, EXT:, :].astype(F32), (start + o1) >> 3)
            block = unpack_symmetric(window[diagonal, span, :].astype(F32), line)
            mat[r1, r1] = block.astype(BF16)

    assemble(0)

    def work(slot, total):
        _, cls = classes(slot)
        span = rows_of(slot)
        flipped_copy(slot, 0).wait()
        for t in range(4):
            part = slice(256 * t, 256 * (t + 1))
            product[part, :] = jnp.dot(mat[part, :], turned[slot, 0], preferred_element_type=F32)
        for k in range(1, 4):
            flipped_copy(slot, k).wait()
        sums = [jnp.zeros((8, G), F32) for _ in range(4)]
        for t in range(KF // BF):
            span_t = slice(t * BF, (t + 1) * BF)
            for k in range(4):
                terms = turned[slot, k, span_t, :].astype(F32) * product[span_t, :]
                sums[k] += jnp.sum(terms.reshape(BF // 8, 8, G), axis=0)
        sums = [jnp.sum(x, axis=0, keepdims=True) for x in sums]
        rho = sums[0]
        grads = [2.0 * x for x in sums[1:]]
        sigma = grads[0] * grads[0] + grads[1] * grads[1] + grads[2] * grads[2]
        quad = weights[pl.ds(slot, 1), :]
        square = rho * rho + 1.0
        logs = jnp.log(square)
        cube = jnp.exp(logs * (1.0 / 3.0))
        scaled = cube * cube
        reduced = sigma / (scaled * scaled)
        denom = 1.0 + MU * reduced / KAPPA
        factor = 1.0 + MU * reduced / denom
        slope = MU / denom / denom
        point = -CX * scaled * factor
        by_rho = (-CX * 2.0) * rho / cube * ((2.0 / 3.0) * factor - (4.0 / 3.0) * slope * reduced)
        by_sigma = -CX * slope / scaled
        wr = 0.5 * quad * by_rho
        ws = 2.0 * quad * by_sigma
        total = total + jnp.sum(quad * point)
        coeffs = [wr] + [ws * x for x in grads]
        for t in range(4):
            lo, hi = 256 * t, 256 * (t + 1)
            phi = turned[slot, 0, lo:hi, :]
            mixed = coeffs[0] * phi.astype(F32)
            for k in range(1, 4):
                mixed += coeffs[k] * turned[slot, k, lo:hi, :].astype(F32)
            mixed = mixed.astype(BF16)
            left[lo:hi, :G] = phi
            left[lo:hi, G:] = mixed
            right[lo:hi, :G] = mixed
            right[lo:hi, G:] = phi
        for t in range(4):
            lo, hi = 256 * t, 256 * (t + 1)
            rows = dot_nt(left[lo:hi, :], right[lo:, :])
            for k in range(2):
                o1 = 2 * t + k
                for o2 in range(o1, KB):
                    c0 = o2 * BF - lo
                    block = rows[k * BF : (k + 1) * BF, c0 : c0 + BF]
                    if o2 == o1:
                        packed, line = pack_symmetric(block)
                        out[cls[o1] * (KB + 1), span, :] = packed.astype(BF16)
                        lines[cls[o1]] = jnp.where(row == slot, line, lines[cls[o1]])
                    else:
                        out[cls[o1] * KB + cls[o2], span, :] = block[:HB].astype(BF16)
                        out[cls[o2] * KB + cls[o1], span, :] = block[HB:].astype(BF16)
        assemble(jnp.minimum(slot + 1, SLOTS - 1))
        return total

    total = jnp.full((16, BF), lax.fori_loop(0, count, work, jnp.float32(0.0)), F32)
    first = total.astype(BF16).astype(F32)
    second = (total - first).astype(BF16).astype(F32)
    third = total - first - second
    spread = jnp.where(lane == 0, first, jnp.where(lane == 1, second, third))
    energy = jnp.where((row == 0) & (lane < 3), spread, 0.0)
    for peer in range(PEERS):
        if peer % (KB + 1) == 0:
            out[peer, EXT:, :] = (lines[peer // (KB + 1)] + energy).astype(BF16)
        else:
            out[peer, EXT:, :] = energy.astype(BF16)


def batches(plan, weights, flipped, window):
    return pl.pallas_call(
        batch_kernel,
        out_shape=jax.ShapeDtypeStruct((PEERS, ROWS, BF), BF16),
        grid_spec=scalars(
            1,
            [VMEM, HBM, VMEM],
            VMEM,
            [
                pltpu.VMEM((SLOTS, 4, KF, G), BF16),
                pltpu.VMEM((KF, KF), BF16),
                pltpu.VMEM((KF, G), F32),
                pltpu.VMEM((KF, 2 * G), BF16),
                pltpu.VMEM((KF, 2 * G), BF16),
                pltpu.VMEM((KB, 16, BF), F32),
                pltpu.SemaphoreType.DMA((SLOTS, 4)),
            ],
        ),
        compiler_params=limit(44),
        name="batches",
    )(plan, weights, flipped, window)


STEP = math.log(2.0) / 128.0
FULL = 32767.0


def integer(values):
    return values.astype(jnp.int32).astype(jnp.int16)


def encode(values):
    top = jnp.max(jnp.max(jnp.abs(values), axis=0, keepdims=True), axis=1, keepdims=True)
    code = jnp.ceil(jnp.log(jnp.maximum(top, 2.0**-110)) * (1.0 / STEP))
    scaled = values * jnp.exp(math.log(FULL) - code * STEP)
    return jnp.clip(scaled, -FULL, FULL), code


def decode(words, code):
    return words.astype(F32) * jnp.exp(code.astype(F32) * STEP - math.log(FULL))


def collect_kernel(which, table, arrived, *refs):
    row_id, col_id, _ = position()
    on_diagonal = ((col_id - row_id) & (KB - 1)) == 0
    row, lane = lanes((16, BF))
    eight, _ = lanes((8, BF))
    if which:
        out, acc = refs
    else:
        acc, blank, zeros, sems = refs
        zeros[...] = jnp.zeros(zeros.shape, F32)
        fills = [pltpu.make_async_copy(zeros, blank.at[t], sems.at[t]) for t in range(TURNS)]
        for fill in fills:
            fill.start()
    acc[...] = jnp.zeros(acc.shape, F32)
    high = first_of(table, which, PEERS // CHUNK)

    def add(peer, span, at, slot):
        acc[pl.ds(at, HB), :] += arrived[peer, pl.ds(span, HB), :].astype(F32)

    def add_line(peer, span, at, slot):
        line = jnp.where(lane >= HB, arrived[peer, EXT:, :].astype(F32), 0.0)
        acc[BAND:, :] += jnp.where(eight == at // HB, pick_row(line, slot), 0.0)

    walk(table, which, 0, high, add)
    pl.when(on_diagonal)(lambda: walk(table, which, 0, high, add_line))
    if not which:
        for fill in fills:
            fill.wait()
        return

    words, code = encode(acc[BAND:, :])
    ext = jnp.concatenate([words, words], axis=0)
    ext = jnp.where(row == 7, code, ext)
    total = jnp.sum(arrived[:, EXT:, :].astype(F32), axis=0)
    total = jnp.where((row == 0) & (lane < 3), total, 0.0)
    total = jnp.sum(jnp.sum(total, axis=0, keepdims=True), axis=1, keepdims=True)
    words, code = encode(total)
    first = jnp.floor(words + 0.5)
    ext = jnp.where(row == 4, first, ext)
    ext = jnp.where(row == 5, (words - first) * FULL, ext)
    ext = jnp.where(row == 6, code, ext)
    for k in range(2 * TURNS):
        words, code = encode(acc[k * HB : (k + 1) * HB, :])
        out[k * HB : (k + 1) * HB, :] = integer(jnp.floor(words + 0.5))
        ext = jnp.where(row == 8 + k, code, ext)
    out[BAND:, :] = integer(jnp.floor(ext + 0.5))


def collect(which, table, arrived):
    acc = jax.ShapeDtypeStruct((BAND + 8, BF), F32)
    if which:
        out_shape = jax.ShapeDtypeStruct((BAND + 16, BF), jnp.int16)
        out_specs = VMEM
        scratch = [pltpu.VMEM((BAND + 8, BF), F32)]
    else:
        out_shape = [acc, jax.ShapeDtypeStruct((TURNS, N_COL, BF, BF), F32)]
        out_specs = [VMEM, HBM]
        scratch = [pltpu.VMEM((N_COL, BF, BF), F32), pltpu.SemaphoreType.DMA((TURNS,))]
    return pl.pallas_call(
        functools.partial(collect_kernel, which),
        out_shape=out_shape,
        grid_spec=scalars(1, [VMEM], out_specs, scratch),
        compiler_params=limit(8),
        cost_estimate=pl.CostEstimate(flops=10**6, bytes_accessed=4 * MIB, transcendentals=0),
        name=("collect_own", "collect_other")[which],
    )(table, arrived)


def merge_kernel(mine, sent, theirs, upper, lower, rest, up_words, low_words):
    eight, _ = lanes((8, BF))
    row, _ = lanes((16, BF))
    got = theirs[BAND:, :].astype(F32)
    own = sent[BAND:, :].astype(F32)

    def line(rows, index):
        return rows[index : index + 1, :]

    def energy(rows):
        return decode(line(rows, 4) + line(rows, 5) * (1.0 / FULL), line(rows, 6))

    more = jnp.where(eight < TURNS, decode(got[:8, :], line(got, 7)), 0.0)
    rest[...] = jnp.where(eight == TURNS, energy(own) + energy(got), mine[BAND:, :] + more)
    for low, full, words in ((0, upper, up_words), (1, lower, low_words)):
        codes = jnp.zeros((16, BF), F32)
        for t in range(TURNS):
            k = low * TURNS + t
            span = slice(k * HB, (k + 1) * HB)
            total = mine[span, :] + decode(theirs[span, :].astype(F32), line(got, 8 + k))
            full[t * HB : (t + 1) * HB, :] = total
            scaled, code = encode(total)
            words[t * HB : (t + 1) * HB, :] = integer(jnp.floor(scaled + 0.5))
            codes = jnp.where(row == t, code, codes)
        words[TURNS * HB :, :] = integer(jnp.floor(codes + 0.5))


def merge(mine, sent, theirs):
    half = jax.ShapeDtypeStruct((TURNS * HB, BF), F32)
    words = jax.ShapeDtypeStruct((TURNS * HB + 16, BF), jnp.int16)
    return pl.pallas_call(
        merge_kernel,
        out_shape=[half, half, jax.ShapeDtypeStruct((8, BF), F32), words, words],
        in_specs=[VMEM] * 3,
        out_specs=[VMEM] * 5,
        compiler_params=limit(4),
        name="merge",
    )(mine, sent, theirs)


def place_kernel(upper, lower, rest, got_upper, got_lower, blank, out, blocks, sems):
    del blank
    row_id, col_id, _ = position()
    shift = (col_id - row_id) & (N_COL - 1)

    def part(ref, turn):
        return ref[pl.ds(pl.multiple_of(turn * HB, HB), HB), :]

    def coded(ref, turn):
        code = pick_row(ref[TURNS * HB :, :].astype(F32), turn)
        return decode(part(ref, turn).astype(F32), code)

    def write(t, low, at):
        slot = TURNS * low + t
        return pltpu.make_async_copy(blocks.at[slot], out.at[t, at], sems.at[slot])

    for finish in (False, True):
        for t in range(TURNS):
            at = (row_id + N_ROW * t + shift) >> 3

            @pl.when((shift > 0) & (at < N_COL))
            def _():
                if finish:
                    write(t, 0, at).wait()
                else:
                    turn = t + jnp.where(row_id + shift >= N_ROW, 1, 0)
                    blocks[t, :HB, :] = part(upper, t)
                    blocks[t, HB:, :] = coded(got_lower, jnp.minimum(turn, TURNS - 1))
                    write(t, 0, at).start()

            @pl.when((shift > 0) & (at > 0))
            def _():
                if finish:
                    write(t, 1, at - 1).wait()
                else:
                    turn = t - jnp.where(row_id + shift < N_COL, 1, 0)
                    top = coded(got_upper, jnp.maximum(turn, 0))
                    blocks[TURNS + t] = jnp.concatenate([top, part(lower, t)], axis=0).T
                    write(t, 1, at - 1).start()

            @pl.when(shift == 0)
            def _():
                if finish:
                    write(t, 0, at).wait()
                else:
                    blocks[t] = unpack_symmetric(part(upper, t), rest[t : t + 1, :])
                    write(t, 0, at).start()


def place(upper, lower, rest, got_upper, got_lower, blank):
    return pl.pallas_call(
        place_kernel,
        out_shape=jax.ShapeDtypeStruct((TURNS, N_COL, BF, BF), F32),
        in_specs=[VMEM] * 5 + [HBM],
        out_specs=HBM,
        scratch_shapes=[
            pltpu.VMEM((2 * TURNS, BF, BF), F32),
            pltpu.SemaphoreType.DMA((2 * TURNS,)),
        ],
        input_output_aliases={5: 0},
        compiler_params=limit(4),
        name="place",
    )(upper, lower, rest, got_upper, got_lower, blank)


def mirror_pairs():
    pairs = []
    for row in range(N_ROW):
        for col in range(N_COL):
            shift = (col - row) % N_COL
            pairs.append((row * N_COL + col, (row + shift) % N_ROW * N_COL + row % N_COL))
    return pairs


def shards(density, basis, weights, batch_start, batch_count):
    swap = [(0, 1), (1, 0)]
    there = mirror_pairs()
    plan = jnp.concatenate([batch_start, batch_count])
    held, sent = share(density)
    theirs = lax.ppermute(sent, "h", swap)
    table = route(plan)
    packed = pack(table, held, theirs)
    window = lax.all_to_all(packed, GROUP, split_axis=0, concat_axis=0, tiled=True)

    outgoing = batches(plan, weights, turn(plan, basis), window)
    arrived = lax.all_to_all(outgoing, GROUP, split_axis=0, concat_axis=0, tiled=True)

    sent = collect(1, table, arrived)
    theirs = lax.ppermute(sent, "h", swap)
    mine, blank = collect(0, table, arrived)
    upper, lower, rest, up_words, low_words = merge(mine, sent, theirs)
    got_upper = lax.ppermute(up_words, ALL, there)
    got_lower = lax.ppermute(low_words, ALL, [(d, s) for s, d in there])
    potential = place(upper, lower, rest, got_upper, got_lower, blank)
    return potential, rest[TURNS, 0] / (NBLK * BF)


def solution(mesh):
    fine = Mesh(np.asarray(mesh.devices).reshape(2, 2, 4, 4, 2), ALL)
    in_specs = (P(ROW, COL), P(ALL), P(ALL), P(), P())
    out_specs = (P(ROW, COL), P())
    return jax.shard_map(shards, mesh=fine, in_specs=in_specs, out_specs=out_specs, check_vma=False)
```

```python
import functools
import math

import jax
import jax.numpy as jnp
import numpy as np
from jax import lax
from jax.experimental import pallas as pl
from jax.experimental.pallas import tpu as pltpu
from jax.sharding import Mesh, PartitionSpec as P

CX = 0.7385587663820224
MU = 0.2195149727645171
KAPPA = 0.804
BF = 128
KB = 8
NBLK = 64
G = 256
SLOTS = 3
KF = 1024
N_ROW = 16
N_COL = 8
TURNS = NBLK // N_ROW
PEERS = 64
MIB = 1024 * 1024
HB = BF // 2
EXT = SLOTS * HB
ROWS = EXT + 16
BAND = 2 * TURNS * HB
ROW = ("h", "xl", "y")
COL = ("z", "c")
ALL = ROW + COL
GROUP = ("xl", "y", "z", "c")
VMEM = pl.BlockSpec(memory_space=pltpu.VMEM)
HBM = pl.BlockSpec(memory_space=pltpu.HBM)
F32 = jnp.float32
BF16 = jnp.bfloat16


def lanes(shape):
    return lax.broadcasted_iota(jnp.int32, shape, 0), lax.broadcasted_iota(jnp.int32, shape, 1)


def pack_symmetric(full):
    r, c = lanes((HB, BF))
    top, bottom = full[:HB], full[HB:]
    packed = jnp.where((c >= HB) | (r <= c), top, pltpu.roll(bottom, HB, 1))
    row = jnp.sum(jnp.where(c - HB == r, bottom, 0.0), axis=0, keepdims=True)
    return packed, row


def unpack_symmetric(packed, row):
    r, c = lanes((HB, BF))
    flip = jnp.concatenate([packed, packed], axis=0).T
    top = jnp.where((c >= HB) | (r <= c), packed, flip[:HB])
    corner = jnp.where(c - HB < r, pltpu.roll(packed, HB, 1), flip[:HB])
    corner = jnp.where(c - HB == r, row, corner)
    return jnp.concatenate([top, jnp.where(c < HB, flip[HB:], corner)], axis=0)


def pick_row(rows, index):
    r, _ = lanes(rows.shape)
    return jnp.sum(jnp.where(r == index, rows, 0.0), axis=0, keepdims=True)


def position():
    h = lax.axis_index("h")
    row_id = (h * 2 + lax.axis_index("xl")) * 4 + lax.axis_index("y")
    return row_id, lax.axis_index("z") * 2 + lax.axis_index("c"), h


def entry(starts, peer, slot, where):
    row_id, col_id, h = where
    start = starts[(h * PEERS + peer) * SLOTS + slot]
    i = start + ((row_id - start) & (KB - 1))
    j = start + ((col_id - start) & (KB - 1))
    other = ((i >> 3) & 1) ^ h
    turn = i >> 4
    below = jnp.where(j < i, TURNS, 0)
    return other, turn, below + turn


def scalars(count, in_specs, out_specs, scratch_shapes=()):
    return pltpu.PrefetchScalarGridSpec(
        num_scalar_prefetch=count,
        grid=(),
        in_specs=in_specs,
        out_specs=out_specs,
        scratch_shapes=list(scratch_shapes),
    )


def limit(mib):
    return pltpu.CompilerParams(vmem_limit_bytes=mib * MIB)


def share_kernel(density, out, copy, ups, lows, sems):
    row_id, col_id, _ = position()
    shift = (col_id - row_id) & (N_COL - 1)
    row, _ = lanes((16, BF))
    loads = []
    for t in range(TURNS):
        at = (row_id + N_ROW * t + shift) >> 3
        up = density.at[t, jnp.minimum(at, N_COL - 1)]
        low = density.at[t, jnp.maximum(at - 1, 0)]
        loads.append(pltpu.make_async_copy(up, ups.at[t], sems.at[t]))
        loads.append(pltpu.make_async_copy(low, lows.at[t], sems.at[TURNS + t]))
    for load in loads:
        load.start()
    for load in loads:
        load.wait()

    @pl.when(shift > 0)
    def _():
        for t in range(TURNS):
            low = TURNS * HB + t * HB
            out[t * HB : (t + 1) * HB, :] = ups[t, :HB, :]
            out[low : low + HB, :] = lows[t].astype(F32).T[HB:].astype(BF16)
        out[BAND:, :] = jnp.zeros((16, BF), BF16)

    @pl.when(shift == 0)
    def _():
        ext = jnp.zeros((16, BF), F32)
        for t in range(TURNS):
            packed, line = pack_symmetric(ups[t].astype(F32))
            out[t * HB : (t + 1) * HB, :] = packed.astype(BF16)
            ext = jnp.where(row == t, line, ext)
        out[TURNS * HB : BAND, :] = jnp.zeros((TURNS * HB, BF), BF16)
        out[BAND:, :] = ext.astype(BF16)

    copy[...] = out[...]


def share(density):
    held = jax.ShapeDtypeStruct((BAND + 16, BF), BF16)
    return pl.pallas_call(
        share_kernel,
        out_shape=[held, held],
        in_specs=[HBM],
        out_specs=[VMEM, VMEM],
        scratch_shapes=[
            pltpu.VMEM((TURNS, BF, BF), BF16),
            pltpu.VMEM((TURNS, BF, BF), BF16),
            pltpu.SemaphoreType.DMA((2 * TURNS,)),
        ],
        compiler_params=limit(4),
        name="share",
    )(density)


CHUNK = 8
ALL_SLOTS = PEERS * SLOTS
BOUNDS = 2 * ALL_SLOTS
STRIDE = 16
OWN = BOUNDS + 2 * STRIDE


def route_kernel(starts, counts, table):
    where = position()
    me = where[0] * N_COL + where[1]
    for slot in range(SLOTS):
        table[OWN + slot] = starts[me * SLOTS + slot]
    table[OWN + SLOTS] = counts[me]

    def one_chunk(chunk, ends):
        for which in range(2):
            table[BOUNDS + which * STRIDE + chunk] = ends[which]

        for k in range(CHUNK):
            peer = chunk * CHUNK + k

            def one(slot, ends):
                other, _, at = entry(starts, peer, slot, where)
                index = jnp.where(other == 1, ends[1], ALL_SLOTS + ends[0])
                table[index] = peer + slot * PEERS + at * (4 * PEERS)
                return ends[0] + 1 - other, ends[1] + other

            ends = one(0, ends)
            ends = lax.fori_loop(1, counts[where[2] * PEERS + peer], one, ends)
        return ends

    ends = lax.fori_loop(0, PEERS // CHUNK, one_chunk, (jnp.int32(0), jnp.int32(0)))
    for which in range(2):
        table[BOUNDS + which * STRIDE + PEERS // CHUNK] = ends[which]


def route(starts, counts):
    scalar = pl.BlockSpec(memory_space=pltpu.SMEM)
    return pl.pallas_call(
        route_kernel,
        out_shape=jax.ShapeDtypeStruct((OWN + STRIDE,), jnp.int32),
        in_specs=[scalar, scalar],
        out_specs=scalar,
        compiler_params=limit(4),
        cost_estimate=pl.CostEstimate(flops=10**6, bytes_accessed=4 * MIB, transcendentals=0),
        name="route",
    )(starts, counts)


def first_of(table, which, chunk):
    return table[BOUNDS + which * STRIDE + chunk]


def walk(table, which, low, high, body):
    base = 0 if which else ALL_SLOTS

    def step(index, carry):
        code = table[base + index]
        slot = (code >> 6) & 3
        at = pl.multiple_of((code >> 8) * HB, HB)
        body(code & (PEERS - 1), pl.multiple_of(slot * HB, HB), at, slot)
        return carry

    lax.fori_loop(low, high, step, 0)


def pack_kernel(table, mine, theirs, out, buf, sems):
    row_id, col_id, h = position()
    row, _ = lanes((16, BF))
    held = (mine, theirs)

    @pl.when(((col_id - row_id) & (KB - 1)) == 0)
    def _():
        ext = jnp.zeros((16, BF), F32)
        for which in range(2):
            lines = held[which][BAND:, :].astype(F32)
            for turn in range(TURNS):
                at = 2 * turn + (h ^ which)
                ext = jnp.where(row == at, lines[turn : turn + 1, :], ext)
        ext = ext.astype(BF16)
        for peer in range(PEERS):
            buf[peer, EXT:, :] = ext

    def send(chunk):
        span = pl.ds(pl.multiple_of(chunk * CHUNK, CHUNK), CHUNK)
        return pltpu.make_async_copy(buf.at[span], out.at[span], sems.at[chunk])

    def one_chunk(chunk, carry):
        for which in range(2):

            def copy(peer, span, at, slot):
                buf[peer, pl.ds(span, HB), :] = held[which][pl.ds(at, HB), :]

            low, high = first_of(table, which, chunk), first_of(table, which, chunk + 1)
            walk(table, which, low, high, copy)
        send(chunk).start()
        return carry

    lax.fori_loop(0, PEERS // CHUNK, one_chunk, 0)

    def drain(chunk, carry):
        send(chunk).wait()
        return carry

    lax.fori_loop(0, PEERS // CHUNK, drain, 0)


def pack(table, mine, theirs):
    return pl.pallas_call(
        pack_kernel,
        out_shape=jax.ShapeDtypeStruct((PEERS, ROWS, BF), BF16),
        grid_spec=scalars(
            1,
            [VMEM, VMEM],
            HBM,
            [
                pltpu.VMEM((PEERS, ROWS, BF), BF16),
                pltpu.SemaphoreType.DMA((PEERS // CHUNK,)),
            ],
        ),
        compiler_params=limit(8),
        name="pack",
    )(table, mine, theirs)


def turn_kernel(table, basis, out, held, turned, sem_in, sem_out):
    count = table[OWN + SLOTS]

    def load(slot):
        return pltpu.make_async_copy(basis.at[slot], held.at[slot], sem_in.at[slot])

    def store(slot):
        return pltpu.make_async_copy(turned.at[slot], out.at[slot], sem_out.at[slot])

    def fetch(slot, carry):
        load(slot).start()
        return carry

    def work(slot, carry):
        load(slot).wait()
        for k in range(4):
            for o in range(KB):
                span = slice(o * BF, (o + 1) * BF)
                turned[slot, k, span, :] = held[slot, k, :, span].T
        store(slot).start()
        return carry

    def drain(slot, carry):
        store(slot).wait()
        return carry

    lax.fori_loop(0, count, fetch, 0)
    lax.fori_loop(0, count, work, 0)
    lax.fori_loop(0, count, drain, 0)


def turn(table, basis):
    return pl.pallas_call(
        turn_kernel,
        out_shape=jax.ShapeDtypeStruct((SLOTS, 4, KF, G), BF16),
        grid_spec=scalars(
            1,
            [HBM],
            HBM,
            [
                pltpu.VMEM((SLOTS, 4, G, KF), BF16),
                pltpu.VMEM((SLOTS, 4, KF, G), BF16),
                pltpu.SemaphoreType.DMA((SLOTS,)),
                pltpu.SemaphoreType.DMA((SLOTS,)),
            ],
        ),
        compiler_params=limit(48),
        cost_estimate=pl.CostEstimate(flops=10**6, bytes_accessed=24 * MIB, transcendentals=0),
        name="turn",
    )(table, basis)


def dot_nt(x, y):
    return lax.dot_general(x, y, (((1,), (1,)), ((), ())), preferred_element_type=F32)


def batch_kernel(
    table, weights, flipped, window, out, turned, mat, product, left, right, lines, sems
):
    count = table[OWN + SLOTS]
    row, lane = lanes((16, BF))

    def flipped_copy(slot, k):
        return pltpu.make_async_copy(flipped.at[slot, k], turned.at[slot, k], sems.at[slot, k])

    def fetch(slot, carry):
        for k in range(4):
            flipped_copy(slot, k).start()
        return carry

    lax.fori_loop(0, count, fetch, 0)
    lines[...] = jnp.zeros(lines.shape, F32)

    def classes(slot):
        start = table[OWN + slot]
        return start, [(start + o) & (KB - 1) for o in range(KB)]

    def rows_of(slot):
        return pl.ds(pl.multiple_of(slot * HB, HB), HB)

    def assemble(slot):
        start, cls = classes(slot)
        span = rows_of(slot)
        for o1 in range(KB):
            r1 = slice(o1 * BF, (o1 + 1) * BF)
            for o2 in range(o1 + 1, KB):
                r2 = slice(o2 * BF, (o2 + 1) * BF)
                top = window[cls[o1] * KB + cls[o2], span, :]
                bottom = window[cls[o2] * KB + cls[o1], span, :]
                block = jnp.concatenate([top, bottom], axis=0)
                mat[r1, r2] = block
                mat[r2, r1] = block.T
            diagonal = cls[o1] * (KB + 1)
            line = pick_row(window[diagonal, EXT:, :].astype(F32), (start + o1) >> 3)
            block = unpack_symmetric(window[diagonal, span, :].astype(F32), line)
            mat[r1, r1] = block.astype(BF16)

    assemble(0)

    def work(slot, total):
        _, cls = classes(slot)
        span = rows_of(slot)
        flipped_copy(slot, 0).wait()
        for t in range(4):
            part = slice(256 * t, 256 * (t + 1))
            product[part, :] = jnp.dot(mat[part, :], turned[slot, 0], preferred_element_type=F32)
        for k in range(1, 4):
            flipped_copy(slot, k).wait()
        sums = [jnp.zeros((8, G), F32) for _ in range(4)]
        for t in range(KF // BF):
            span_t = slice(t * BF, (t + 1) * BF)
            for k in range(4):
                terms = turned[slot, k, span_t, :].astype(F32) * product[span_t, :]
                sums[k] += jnp.sum(terms.reshape(BF // 8, 8, G), axis=0)
        sums = [jnp.sum(x, axis=0, keepdims=True) for x in sums]
        rho = sums[0]
        grads = [2.0 * x for x in sums[1:]]
        sigma = grads[0] * grads[0] + grads[1] * grads[1] + grads[2] * grads[2]
        quad = weights[pl.ds(slot, 1), :]
        square = rho * rho + 1.0
        logs = jnp.log(square)
        cube = jnp.exp(logs * (1.0 / 3.0))
        scaled = cube * cube
        reduced = sigma / (scaled * scaled)
        denom = 1.0 + MU * reduced / KAPPA
        factor = 1.0 + MU * reduced / denom
        slope = MU / denom / denom
        point = -CX * scaled * factor
        by_rho = (-CX * 2.0) * rho / cube * ((2.0 / 3.0) * factor - (4.0 / 3.0) * slope * reduced)
        by_sigma = -CX * slope / scaled
        wr = 0.5 * quad * by_rho
        ws = 2.0 * quad * by_sigma
        total = total + jnp.sum(quad * point)
        coeffs = [wr] + [ws * x for x in grads]
        for t in range(4):
            lo, hi = 256 * t, 256 * (t + 1)
            phi = turned[slot, 0, lo:hi, :]
            mixed = coeffs[0] * phi.astype(F32)
            for k in range(1, 4):
                mixed += coeffs[k] * turned[slot, k, lo:hi, :].astype(F32)
            mixed = mixed.astype(BF16)
            left[lo:hi, :G] = phi
            left[lo:hi, G:] = mixed
            right[lo:hi, :G] = mixed
            right[lo:hi, G:] = phi
        for t in range(4):
            lo, hi = 256 * t, 256 * (t + 1)
            rows = dot_nt(left[lo:hi, :], right[lo:, :])
            for k in range(2):
                o1 = 2 * t + k
                for o2 in range(o1, KB):
                    c0 = o2 * BF - lo
                    block = rows[k * BF : (k + 1) * BF, c0 : c0 + BF]
                    if o2 == o1:
                        packed, line = pack_symmetric(block)
                        out[cls[o1] * (KB + 1), span, :] = packed.astype(BF16)
                        lines[cls[o1]] = jnp.where(row == slot, line, lines[cls[o1]])
                    else:
                        out[cls[o1] * KB + cls[o2], span, :] = block[:HB].astype(BF16)
                        out[cls[o2] * KB + cls[o1], span, :] = block[HB:].astype(BF16)
        assemble(jnp.minimum(slot + 1, SLOTS - 1))
        return total

    total = jnp.full((16, BF), lax.fori_loop(0, count, work, jnp.float32(0.0)), F32)
    first = total.astype(BF16).astype(F32)
    second = (total - first).astype(BF16).astype(F32)
    third = total - first - second
    spread = jnp.where(lane == 0, first, jnp.where(lane == 1, second, third))
    energy = jnp.where((row == 0) & (lane < 3), spread, 0.0)
    for peer in range(PEERS):
        if peer % (KB + 1) == 0:
            out[peer, EXT:, :] = (lines[peer // (KB + 1)] + energy).astype(BF16)
        else:
            out[peer, EXT:, :] = energy.astype(BF16)


def batches(table, weights, flipped, window):
    return pl.pallas_call(
        batch_kernel,
        out_shape=jax.ShapeDtypeStruct((PEERS, ROWS, BF), BF16),
        grid_spec=scalars(
            1,
            [VMEM, HBM, VMEM],
            VMEM,
            [
                pltpu.VMEM((SLOTS, 4, KF, G), BF16),
                pltpu.VMEM((KF, KF), BF16),
                pltpu.VMEM((KF, G), F32),
                pltpu.VMEM((KF, 2 * G), BF16),
                pltpu.VMEM((KF, 2 * G), BF16),
                pltpu.VMEM((KB, 16, BF), F32),
                pltpu.SemaphoreType.DMA((SLOTS, 4)),
            ],
        ),
        compiler_params=limit(44),
        name="batches",
    )(table, weights, flipped, window)


STEP = math.log(2.0) / 128.0
FULL = 32767.0


def integer(values):
    return values.astype(jnp.int32).astype(jnp.int16)


def encode(values):
    top = jnp.max(jnp.max(jnp.abs(values), axis=0, keepdims=True), axis=1, keepdims=True)
    code = jnp.ceil(jnp.log(jnp.maximum(top, 2.0**-110)) * (1.0 / STEP))
    scaled = values * jnp.exp(math.log(FULL) - code * STEP)
    return jnp.clip(scaled, -FULL, FULL), code


def decode(words, code):
    return words.astype(F32) * jnp.exp(code.astype(F32) * STEP - math.log(FULL))


def collect_kernel(which, table, arrived, *refs):
    row_id, col_id, _ = position()
    on_diagonal = ((col_id - row_id) & (KB - 1)) == 0
    row, lane = lanes((16, BF))
    eight, _ = lanes((8, BF))
    if which:
        out, acc = refs
    else:
        acc, blank, zeros, sems = refs
        zeros[...] = jnp.zeros(zeros.shape, F32)
        fills = [pltpu.make_async_copy(zeros, blank.at[t], sems.at[t]) for t in range(TURNS)]
        for fill in fills:
            fill.start()
    acc[...] = jnp.zeros(acc.shape, F32)
    high = first_of(table, which, PEERS // CHUNK)

    def add(peer, span, at, slot):
        acc[pl.ds(at, HB), :] += arrived[peer, pl.ds(span, HB), :].astype(F32)

    def add_line(peer, span, at, slot):
        line = jnp.where(lane >= HB, arrived[peer, EXT:, :].astype(F32), 0.0)
        acc[BAND:, :] += jnp.where(eight == at // HB, pick_row(line, slot), 0.0)

    walk(table, which, 0, high, add)
    pl.when(on_diagonal)(lambda: walk(table, which, 0, high, add_line))
    if not which:
        for fill in fills:
            fill.wait()
        return

    words, code = encode(acc[BAND:, :])
    ext = jnp.concatenate([words, words], axis=0)
    ext = jnp.where(row == 7, code, ext)
    total = jnp.sum(arrived[:, EXT:, :].astype(F32), axis=0)
    total = jnp.where((row == 0) & (lane < 3), total, 0.0)
    total = jnp.sum(jnp.sum(total, axis=0, keepdims=True), axis=1, keepdims=True)
    words, code = encode(total)
    first = jnp.floor(words + 0.5)
    ext = jnp.where(row == 4, first, ext)
    ext = jnp.where(row == 5, (words - first) * FULL, ext)
    ext = jnp.where(row == 6, code, ext)
    for k in range(2 * TURNS):
        words, code = encode(acc[k * HB : (k + 1) * HB, :])
        out[k * HB : (k + 1) * HB, :] = integer(jnp.floor(words + 0.5))
        ext = jnp.where(row == 8 + k, code, ext)
    out[BAND:, :] = integer(jnp.floor(ext + 0.5))


def collect(which, table, arrived):
    acc = jax.ShapeDtypeStruct((BAND + 8, BF), F32)
    if which:
        out_shape = jax.ShapeDtypeStruct((BAND + 16, BF), jnp.int16)
        out_specs = VMEM
        scratch = [pltpu.VMEM((BAND + 8, BF), F32)]
    else:
        out_shape = [acc, jax.ShapeDtypeStruct((TURNS, N_COL, BF, BF), F32)]
        out_specs = [VMEM, HBM]
        scratch = [pltpu.VMEM((N_COL, BF, BF), F32), pltpu.SemaphoreType.DMA((TURNS,))]
    return pl.pallas_call(
        functools.partial(collect_kernel, which),
        out_shape=out_shape,
        grid_spec=scalars(1, [VMEM], out_specs, scratch),
        compiler_params=limit(8),
        cost_estimate=pl.CostEstimate(flops=10**6, bytes_accessed=4 * MIB, transcendentals=0),
        name=("collect_own", "collect_other")[which],
    )(table, arrived)


def merge_kernel(mine, sent, theirs, upper, lower, rest, near, far):
    eight, _ = lanes((8, BF))
    row, _ = lanes((16, BF))
    got = theirs[BAND:, :].astype(F32)
    own = sent[BAND:, :].astype(F32)

    def line(rows, index):
        return rows[index : index + 1, :]

    def energy(rows):
        return decode(line(rows, 4) + line(rows, 5) * (1.0 / FULL), line(rows, 6))

    more = jnp.where(eight < TURNS, decode(got[:8, :], line(got, 7)), 0.0)
    rest[...] = jnp.where(eight == TURNS, energy(own) + energy(got), mine[BAND:, :] + more)
    row_id, col_id, _ = position()
    ahead = (row_id & (KB - 1)) < col_id
    codes = [jnp.zeros((16, BF), F32)] * 2
    for t in range(TURNS):
        span = slice(t * HB, (t + 1) * HB)
        words = []
        for low, full in ((0, upper), (1, lower)):
            k = low * TURNS + t
            whole = slice(k * HB, (k + 1) * HB)
            total = mine[whole, :] + decode(theirs[whole, :].astype(F32), line(got, 8 + k))
            full[span, :] = total
            scaled, code = encode(total)
            words.append(scaled)
            codes[low] = jnp.where(row == t, code, codes[low])
        near[span, :] = integer(jnp.floor(jnp.where(ahead, words[0], words[1]) + 0.5))
        far[span, :] = integer(jnp.floor(jnp.where(ahead, words[1], words[0]) + 0.5))
    near[TURNS * HB :, :] = integer(jnp.floor(jnp.where(ahead, codes[0], codes[1]) + 0.5))
    far[TURNS * HB :, :] = integer(jnp.floor(jnp.where(ahead, codes[1], codes[0]) + 0.5))


def merge(mine, sent, theirs):
    half = jax.ShapeDtypeStruct((TURNS * HB, BF), F32)
    words = jax.ShapeDtypeStruct((TURNS * HB + 16, BF), jnp.int16)
    return pl.pallas_call(
        merge_kernel,
        out_shape=[half, half, jax.ShapeDtypeStruct((8, BF), F32), words, words],
        in_specs=[VMEM] * 3,
        out_specs=[VMEM] * 5,
        compiler_params=limit(4),
        name="merge",
    )(mine, sent, theirs)


def place_kernel(upper, lower, rest, near, far, blank, out, blocks, sems):
    del blank
    row_id, col_id, _ = position()
    shift = (col_id - row_id) & (N_COL - 1)

    def part(ref, turn):
        return ref[pl.ds(pl.multiple_of(turn * HB, HB), HB), :]

    ahead = (row_id & (KB - 1)) < col_id

    def coded(from_near, turn):
        code = jnp.where(from_near, near[TURNS * HB :, :].astype(F32), far[TURNS * HB :, :].astype(F32))
        words = jnp.where(from_near, part(near, turn).astype(F32), part(far, turn).astype(F32))
        return decode(words, pick_row(code, turn))

    def write(t, low, at):
        slot = TURNS * low + t
        return pltpu.make_async_copy(blocks.at[slot], out.at[t, at], sems.at[slot])

    for finish in (False, True):
        for t in range(TURNS):
            at = (row_id + N_ROW * t + shift) >> 3

            @pl.when((shift > 0) & (at < N_COL))
            def _():
                if finish:
                    write(t, 0, at).wait()
                else:
                    turn = t + jnp.where(row_id + shift >= N_ROW, 1, 0)
                    blocks[t, :HB, :] = part(upper, t)
                    blocks[t, HB:, :] = coded(ahead, jnp.minimum(turn, TURNS - 1))
                    write(t, 0, at).start()

            @pl.when((shift > 0) & (at > 0))
            def _():
                if finish:
                    write(t, 1, at - 1).wait()
                else:
                    turn = t - jnp.where(row_id + shift < N_COL, 1, 0)
                    top = coded(jnp.logical_not(ahead), jnp.maximum(turn, 0))
                    blocks[TURNS + t] = jnp.concatenate([top, part(lower, t)], axis=0).T
                    write(t, 1, at - 1).start()

            @pl.when(shift == 0)
            def _():
                if finish:
                    write(t, 0, at).wait()
                else:
                    blocks[t] = unpack_symmetric(part(upper, t), rest[t : t + 1, :])
                    write(t, 0, at).start()


def place(upper, lower, rest, near, far, blank):
    return pl.pallas_call(
        place_kernel,
        out_shape=jax.ShapeDtypeStruct((TURNS, N_COL, BF, BF), F32),
        in_specs=[VMEM] * 5 + [HBM],
        out_specs=HBM,
        scratch_shapes=[
            pltpu.VMEM((2 * TURNS, BF, BF), F32),
            pltpu.SemaphoreType.DMA((2 * TURNS,)),
        ],
        input_output_aliases={5: 0},
        compiler_params=limit(4),
        name="place",
    )(upper, lower, rest, near, far, blank)


def mirror_pairs(across):
    pairs = []
    for row in range(N_ROW):
        for col in range(N_COL):
            half = (row // KB) ^ across
            pairs.append((row * N_COL + col, (half * KB + col) * N_COL + row % KB))
    return pairs


def shards(density, basis, weights, batch_start, batch_count):
    swap = [(0, 1), (1, 0)]
    held, sent = share(density)
    theirs = lax.ppermute(sent, "h", swap)
    table = route(batch_start, batch_count)
    packed = pack(table, held, theirs)
    window = lax.all_to_all(packed, GROUP, split_axis=0, concat_axis=0, tiled=True)

    outgoing = batches(table, weights, turn(table, basis), window)
    arrived = lax.all_to_all(outgoing, GROUP, split_axis=0, concat_axis=0, tiled=True)

    sent = collect(1, table, arrived)
    theirs = lax.ppermute(sent, "h", swap)
    mine, blank = collect(0, table, arrived)
    upper, lower, rest, near, far = merge(mine, sent, theirs)
    near = lax.ppermute(near, ALL, mirror_pairs(0))
    far = lax.ppermute(far, ALL, mirror_pairs(1))
    potential = place(upper, lower, rest, near, far, blank)
    return potential, rest[TURNS, 0] / (NBLK * BF)


def solution(mesh):
    fine = Mesh(np.asarray(mesh.devices).reshape(2, 2, 4, 4, 2), ALL)
    in_specs = (P(ROW, COL), P(ALL), P(ALL), P(), P())
    out_specs = (P(ROW, COL), P())
    return jax.shard_map(shards, mesh=fine, in_specs=in_specs, out_specs=out_specs, check_vma=False)
```

```python
import functools
import math

import jax
import jax.numpy as jnp
import numpy as np
from jax import lax
from jax.experimental import pallas as pl
from jax.experimental.pallas import tpu as pltpu
from jax.sharding import Mesh, PartitionSpec as P

CX = 0.7385587663820224
MU = 0.2195149727645171
KAPPA = 0.804
BF = 128
KB = 8
NBLK = 64
G = 256
SLOTS = 3
KF = 1024
N_ROW = 16
N_COL = 8
TURNS = NBLK // N_ROW
PEERS = 64
MIB = 1024 * 1024
HB = BF // 2
EXT = SLOTS * HB
ROWS = EXT + 16
BAND = 2 * TURNS * HB
ROW = ("h", "xl", "y")
COL = ("z", "c")
ALL = ROW + COL
ORDER = [
    53, 42, 62, 31, 35, 37, 59, 57, 45, 33, 49, 50, 54, 38, 5, 0,
    13, 14, 30, 21, 52, 41, 28, 58, 1, 3, 61, 48, 12, 17, 29, 16,
    11, 15, 24, 7, 23, 39, 36, 20, 51, 34, 10, 27, 32, 63, 43, 26,
    8, 40, 60, 9, 47, 55, 22, 19, 56, 6, 46, 18, 44, 2, 4, 25,
]
PLACE = [ORDER.index(x) for x in range(PEERS)]
GROUPS = [[h * PEERS + x for x in ORDER] for h in range(2)]
VMEM = pl.BlockSpec(memory_space=pltpu.VMEM)
HBM = pl.BlockSpec(memory_space=pltpu.HBM)
F32 = jnp.float32
BF16 = jnp.bfloat16


def lanes(shape):
    return lax.broadcasted_iota(jnp.int32, shape, 0), lax.broadcasted_iota(jnp.int32, shape, 1)


def pack_symmetric(full):
    r, c = lanes((HB, BF))
    top, bottom = full[:HB], full[HB:]
    packed = jnp.where((c >= HB) | (r <= c), top, pltpu.roll(bottom, HB, 1))
    row = jnp.sum(jnp.where(c - HB == r, bottom, 0.0), axis=0, keepdims=True)
    return packed, row


def unpack_symmetric(packed, row):
    r, c = lanes((HB, BF))
    flip = jnp.concatenate([packed, packed], axis=0).T
    top = jnp.where((c >= HB) | (r <= c), packed, flip[:HB])
    corner = jnp.where(c - HB < r, pltpu.roll(packed, HB, 1), flip[:HB])
    corner = jnp.where(c - HB == r, row, corner)
    return jnp.concatenate([top, jnp.where(c < HB, flip[HB:], corner)], axis=0)


def pick_row(rows, index):
    r, _ = lanes(rows.shape)
    return jnp.sum(jnp.where(r == index, rows, 0.0), axis=0, keepdims=True)


def position():
    h = lax.axis_index("h")
    row_id = (h * 2 + lax.axis_index("xl")) * 4 + lax.axis_index("y")
    return row_id, lax.axis_index("z") * 2 + lax.axis_index("c"), h


def entry(starts, peer, slot, where):
    row_id, col_id, h = where
    start = starts[(h * PEERS + ORDER[peer]) * SLOTS + slot]
    i = start + ((row_id - start) & (KB - 1))
    j = start + ((col_id - start) & (KB - 1))
    other = ((i >> 3) & 1) ^ h
    turn = i >> 4
    below = jnp.where(j < i, TURNS, 0)
    return other, turn, below + turn


def scalars(count, in_specs, out_specs, scratch_shapes=()):
    return pltpu.PrefetchScalarGridSpec(
        num_scalar_prefetch=count,
        grid=(),
        in_specs=in_specs,
        out_specs=out_specs,
        scratch_shapes=list(scratch_shapes),
    )


def limit(mib):
    return pltpu.CompilerParams(vmem_limit_bytes=mib * MIB)


def share_kernel(density, out, copy, ups, lows, sems):
    row_id, col_id, _ = position()
    shift = (col_id - row_id) & (N_COL - 1)
    row, _ = lanes((16, BF))
    loads = []
    for t in range(TURNS):
        at = (row_id + N_ROW * t + shift) >> 3
        up = density.at[t, jnp.minimum(at, N_COL - 1)]
        low = density.at[t, jnp.maximum(at - 1, 0)]
        loads.append(pltpu.make_async_copy(up, ups.at[t], sems.at[t]))
        loads.append(pltpu.make_async_copy(low, lows.at[t], sems.at[TURNS + t]))
    for load in loads:
        load.start()
    for load in loads:
        load.wait()

    @pl.when(shift > 0)
    def _():
        for t in range(TURNS):
            low = TURNS * HB + t * HB
            out[t * HB : (t + 1) * HB, :] = ups[t, :HB, :]
            out[low : low + HB, :] = lows[t].astype(F32).T[HB:].astype(BF16)
        out[BAND:, :] = jnp.zeros((16, BF), BF16)

    @pl.when(shift == 0)
    def _():
        ext = jnp.zeros((16, BF), F32)
        for t in range(TURNS):
            packed, line = pack_symmetric(ups[t].astype(F32))
            out[t * HB : (t + 1) * HB, :] = packed.astype(BF16)
            ext = jnp.where(row == t, line, ext)
        out[TURNS * HB : BAND, :] = jnp.zeros((TURNS * HB, BF), BF16)
        out[BAND:, :] = ext.astype(BF16)

    copy[...] = out[...]


def share(density):
    held = jax.ShapeDtypeStruct((BAND + 16, BF), BF16)
    return pl.pallas_call(
        share_kernel,
        out_shape=[held, held],
        in_specs=[HBM],
        out_specs=[VMEM, VMEM],
        scratch_shapes=[
            pltpu.VMEM((TURNS, BF, BF), BF16),
            pltpu.VMEM((TURNS, BF, BF), BF16),
            pltpu.SemaphoreType.DMA((2 * TURNS,)),
        ],
        compiler_params=limit(4),
        name="share",
    )(density)


CHUNK = 8
ALL_SLOTS = PEERS * SLOTS
BOUNDS = 2 * ALL_SLOTS
STRIDE = 16
OWN = BOUNDS + 2 * STRIDE
PLACES = OWN + STRIDE


def route_kernel(starts, counts, table):
    where = position()
    me = where[0] * N_COL + where[1]
    for slot in range(SLOTS):
        table[OWN + slot] = starts[me * SLOTS + slot]
    table[OWN + SLOTS] = counts[me]

    ends = (jnp.int32(0), jnp.int32(0))
    for peer in range(PEERS):
        table[PLACES + peer] = PLACE[peer]
        if peer % CHUNK == 0:
            for which in range(2):
                table[BOUNDS + which * STRIDE + peer // CHUNK] = ends[which]

        def one(slot, ends):
            other, _, at = entry(starts, peer, slot, where)
            index = jnp.where(other == 1, ends[1], ALL_SLOTS + ends[0])
            table[index] = peer + slot * PEERS + at * (4 * PEERS)
            return ends[0] + 1 - other, ends[1] + other

        ends = one(0, ends)
        ends = lax.fori_loop(1, counts[where[2] * PEERS + ORDER[peer]], one, ends)
    for which in range(2):
        table[BOUNDS + which * STRIDE + PEERS // CHUNK] = ends[which]


def route(starts, counts):
    scalar = pl.BlockSpec(memory_space=pltpu.SMEM)
    return pl.pallas_call(
        route_kernel,
        out_shape=jax.ShapeDtypeStruct((PLACES + PEERS,), jnp.int32),
        in_specs=[scalar, scalar],
        out_specs=scalar,
        compiler_params=limit(4),
        cost_estimate=pl.CostEstimate(flops=10**6, bytes_accessed=4 * MIB, transcendentals=0),
        name="route",
    )(starts, counts)


def first_of(table, which, chunk):
    return table[BOUNDS + which * STRIDE + chunk]


def walk(table, which, low, high, body):
    base = 0 if which else ALL_SLOTS

    def step(index, carry):
        code = table[base + index]
        slot = (code >> 6) & 3
        at = pl.multiple_of((code >> 8) * HB, HB)
        body(code & (PEERS - 1), pl.multiple_of(slot * HB, HB), at, slot)
        return carry

    lax.fori_loop(low, high, step, 0)


def pack_kernel(table, mine, theirs, out, buf, sems):
    row_id, col_id, h = position()
    row, _ = lanes((16, BF))
    held = (mine, theirs)

    @pl.when(((col_id - row_id) & (KB - 1)) == 0)
    def _():
        ext = jnp.zeros((16, BF), F32)
        for which in range(2):
            lines = held[which][BAND:, :].astype(F32)
            for turn in range(TURNS):
                at = 2 * turn + (h ^ which)
                ext = jnp.where(row == at, lines[turn : turn + 1, :], ext)
        ext = ext.astype(BF16)
        for peer in range(PEERS):
            buf[peer, EXT:, :] = ext

    def send(chunk):
        span = pl.ds(pl.multiple_of(chunk * CHUNK, CHUNK), CHUNK)
        return pltpu.make_async_copy(buf.at[span], out.at[span], sems.at[chunk])

    def one_chunk(chunk, carry):
        for which in range(2):

            def copy(peer, span, at, slot):
                buf[peer, pl.ds(span, HB), :] = held[which][pl.ds(at, HB), :]

            low, high = first_of(table, which, chunk), first_of(table, which, chunk + 1)
            walk(table, which, low, high, copy)
        send(chunk).start()
        return carry

    lax.fori_loop(0, PEERS // CHUNK, one_chunk, 0)

    def drain(chunk, carry):
        send(chunk).wait()
        return carry

    lax.fori_loop(0, PEERS // CHUNK, drain, 0)


def pack(table, mine, theirs):
    return pl.pallas_call(
        pack_kernel,
        out_shape=jax.ShapeDtypeStruct((PEERS, ROWS, BF), BF16),
        grid_spec=scalars(
            1,
            [VMEM, VMEM],
            HBM,
            [
                pltpu.VMEM((PEERS, ROWS, BF), BF16),
                pltpu.SemaphoreType.DMA((PEERS // CHUNK,)),
            ],
        ),
        compiler_params=limit(8),
        name="pack",
    )(table, mine, theirs)


def turn_kernel(table, basis, out, held, turned, sem_in, sem_out):
    count = table[OWN + SLOTS]

    def load(slot):
        return pltpu.make_async_copy(basis.at[slot], held.at[slot], sem_in.at[slot])

    def store(slot):
        return pltpu.make_async_copy(turned.at[slot], out.at[slot], sem_out.at[slot])

    def fetch(slot, carry):
        load(slot).start()
        return carry

    def work(slot, carry):
        load(slot).wait()
        for k in range(4):
            for o in range(KB):
                span = slice(o * BF, (o + 1) * BF)
                turned[slot, k, span, :] = held[slot, k, :, span].T
        store(slot).start()
        return carry

    def drain(slot, carry):
        store(slot).wait()
        return carry

    lax.fori_loop(0, count, fetch, 0)
    lax.fori_loop(0, count, work, 0)
    lax.fori_loop(0, count, drain, 0)


def turn(table, basis):
    return pl.pallas_call(
        turn_kernel,
        out_shape=jax.ShapeDtypeStruct((SLOTS, 4, KF, G), BF16),
        grid_spec=scalars(
            1,
            [HBM],
            HBM,
            [
                pltpu.VMEM((SLOTS, 4, G, KF), BF16),
                pltpu.VMEM((SLOTS, 4, KF, G), BF16),
                pltpu.SemaphoreType.DMA((SLOTS,)),
                pltpu.SemaphoreType.DMA((SLOTS,)),
            ],
        ),
        compiler_params=limit(48),
        cost_estimate=pl.CostEstimate(flops=10**6, bytes_accessed=24 * MIB, transcendentals=0),
        name="turn",
    )(table, basis)


def dot_nt(x, y):
    return lax.dot_general(x, y, (((1,), (1,)), ((), ())), preferred_element_type=F32)


def batch_kernel(
    table, weights, flipped, window, out, turned, mat, product, left, right, lines, sems
):
    count = table[OWN + SLOTS]
    row, lane = lanes((16, BF))

    def flipped_copy(slot, k):
        return pltpu.make_async_copy(flipped.at[slot, k], turned.at[slot, k], sems.at[slot, k])

    def fetch(slot, carry):
        for k in range(4):
            flipped_copy(slot, k).start()
        return carry

    lax.fori_loop(0, count, fetch, 0)
    lines[...] = jnp.zeros(lines.shape, F32)

    def classes(slot):
        start = table[OWN + slot]
        return start, [(start + o) & (KB - 1) for o in range(KB)]

    def place_of(a, b):
        return table[PLACES + a * KB + b]

    def rows_of(slot):
        return pl.ds(pl.multiple_of(slot * HB, HB), HB)

    def assemble(slot):
        start, cls = classes(slot)
        span = rows_of(slot)
        for o1 in range(KB):
            r1 = slice(o1 * BF, (o1 + 1) * BF)
            for o2 in range(o1 + 1, KB):
                r2 = slice(o2 * BF, (o2 + 1) * BF)
                top = window[place_of(cls[o1], cls[o2]), span, :]
                bottom = window[place_of(cls[o2], cls[o1]), span, :]
                block = jnp.concatenate([top, bottom], axis=0)
                mat[r1, r2] = block
                mat[r2, r1] = block.T
            diagonal = place_of(cls[o1], cls[o1])
            line = pick_row(window[diagonal, EXT:, :].astype(F32), (start + o1) >> 3)
            block = unpack_symmetric(window[diagonal, span, :].astype(F32), line)
            mat[r1, r1] = block.astype(BF16)

    assemble(0)

    def work(slot, total):
        _, cls = classes(slot)
        span = rows_of(slot)
        flipped_copy(slot, 0).wait()
        for t in range(4):
            part = slice(256 * t, 256 * (t + 1))
            product[part, :] = jnp.dot(mat[part, :], turned[slot, 0], preferred_element_type=F32)
        for k in range(1, 4):
            flipped_copy(slot, k).wait()
        sums = [jnp.zeros((8, G), F32) for _ in range(4)]
        for t in range(KF // BF):
            span_t = slice(t * BF, (t + 1) * BF)
            for k in range(4):
                terms = turned[slot, k, span_t, :].astype(F32) * product[span_t, :]
                sums[k] += jnp.sum(terms.reshape(BF // 8, 8, G), axis=0)
        sums = [jnp.sum(x, axis=0, keepdims=True) for x in sums]
        rho = sums[0]
        grads = [2.0 * x for x in sums[1:]]
        sigma = grads[0] * grads[0] + grads[1] * grads[1] + grads[2] * grads[2]
        quad = weights[pl.ds(slot, 1), :]
        square = rho * rho + 1.0
        logs = jnp.log(square)
        cube = jnp.exp(logs * (1.0 / 3.0))
        scaled = cube * cube
        reduced = sigma / (scaled * scaled)
        denom = 1.0 + MU * reduced / KAPPA
        factor = 1.0 + MU * reduced / denom
        slope = MU / denom / denom
        point = -CX * scaled * factor
        by_rho = (-CX * 2.0) * rho / cube * ((2.0 / 3.0) * factor - (4.0 / 3.0) * slope * reduced)
        by_sigma = -CX * slope / scaled
        wr = 0.5 * quad * by_rho
        ws = 2.0 * quad * by_sigma
        total = total + jnp.sum(quad * point)
        coeffs = [wr] + [ws * x for x in grads]
        for t in range(4):
            lo, hi = 256 * t, 256 * (t + 1)
            phi = turned[slot, 0, lo:hi, :]
            mixed = coeffs[0] * phi.astype(F32)
            for k in range(1, 4):
                mixed += coeffs[k] * turned[slot, k, lo:hi, :].astype(F32)
            mixed = mixed.astype(BF16)
            left[lo:hi, :G] = phi
            left[lo:hi, G:] = mixed
            right[lo:hi, :G] = mixed
            right[lo:hi, G:] = phi
        for t in range(4):
            lo, hi = 256 * t, 256 * (t + 1)
            rows = dot_nt(left[lo:hi, :], right[lo:, :])
            for k in range(2):
                o1 = 2 * t + k
                for o2 in range(o1, KB):
                    c0 = o2 * BF - lo
                    block = rows[k * BF : (k + 1) * BF, c0 : c0 + BF]
                    if o2 == o1:
                        packed, line = pack_symmetric(block)
                        out[place_of(cls[o1], cls[o1]), span, :] = packed.astype(BF16)
                        lines[cls[o1]] = jnp.where(row == slot, line, lines[cls[o1]])
                    else:
                        out[place_of(cls[o1], cls[o2]), span, :] = block[:HB].astype(BF16)
                        out[place_of(cls[o2], cls[o1]), span, :] = block[HB:].astype(BF16)
        assemble(jnp.minimum(slot + 1, SLOTS - 1))
        return total

    total = jnp.full((16, BF), lax.fori_loop(0, count, work, jnp.float32(0.0)), F32)
    first = total.astype(BF16).astype(F32)
    second = (total - first).astype(BF16).astype(F32)
    third = total - first - second
    spread = jnp.where(lane == 0, first, jnp.where(lane == 1, second, third))
    energy = jnp.where((row == 0) & (lane < 3), spread, 0.0)
    for peer in range(PEERS):
        if peer % (KB + 1) == 0:
            out[PLACE[peer], EXT:, :] = (lines[peer // (KB + 1)] + energy).astype(BF16)
        else:
            out[PLACE[peer], EXT:, :] = energy.astype(BF16)


def batches(table, weights, flipped, window):
    return pl.pallas_call(
        batch_kernel,
        out_shape=jax.ShapeDtypeStruct((PEERS, ROWS, BF), BF16),
        grid_spec=scalars(
            1,
            [VMEM, HBM, VMEM],
            VMEM,
            [
                pltpu.VMEM((SLOTS, 4, KF, G), BF16),
                pltpu.VMEM((KF, KF), BF16),
                pltpu.VMEM((KF, G), F32),
                pltpu.VMEM((KF, 2 * G), BF16),
                pltpu.VMEM((KF, 2 * G), BF16),
                pltpu.VMEM((KB, 16, BF), F32),
                pltpu.SemaphoreType.DMA((SLOTS, 4)),
            ],
        ),
        compiler_params=limit(44),
        name="batches",
    )(table, weights, flipped, window)


STEP = math.log(2.0) / 128.0
FULL = 32767.0


def integer(values):
    return values.astype(jnp.int32).astype(jnp.int16)


def encode(values):
    top = jnp.max(jnp.max(jnp.abs(values), axis=0, keepdims=True), axis=1, keepdims=True)
    code = jnp.ceil(jnp.log(jnp.maximum(top, 2.0**-110)) * (1.0 / STEP))
    scaled = values * jnp.exp(math.log(FULL) - code * STEP)
    return jnp.clip(scaled, -FULL, FULL), code


def decode(words, code):
    return words.astype(F32) * jnp.exp(code.astype(F32) * STEP - math.log(FULL))


def collect_kernel(which, table, arrived, *refs):
    row_id, col_id, _ = position()
    on_diagonal = ((col_id - row_id) & (KB - 1)) == 0
    row, lane = lanes((16, BF))
    eight, _ = lanes((8, BF))
    if which:
        out, acc = refs
    else:
        acc, blank, zeros, sems = refs
        zeros[...] = jnp.zeros(zeros.shape, F32)
        fills = [pltpu.make_async_copy(zeros, blank.at[t], sems.at[t]) for t in range(TURNS)]
        for fill in fills:
            fill.start()
    acc[...] = jnp.zeros(acc.shape, F32)
    high = first_of(table, which, PEERS // CHUNK)

    def add(peer, span, at, slot):
        acc[pl.ds(at, HB), :] += arrived[peer, pl.ds(span, HB), :].astype(F32)

    def add_line(peer, span, at, slot):
        line = jnp.where(lane >= HB, arrived[peer, EXT:, :].astype(F32), 0.0)
        acc[BAND:, :] += jnp.where(eight == at // HB, pick_row(line, slot), 0.0)

    walk(table, which, 0, high, add)
    pl.when(on_diagonal)(lambda: walk(table, which, 0, high, add_line))
    if not which:
        for fill in fills:
            fill.wait()
        return

    words, code = encode(acc[BAND:, :])
    ext = jnp.concatenate([words, words], axis=0)
    ext = jnp.where(row == 7, code, ext)
    total = jnp.sum(arrived[:, EXT:, :].astype(F32), axis=0)
    total = jnp.where((row == 0) & (lane < 3), total, 0.0)
    total = jnp.sum(jnp.sum(total, axis=0, keepdims=True), axis=1, keepdims=True)
    words, code = encode(total)
    first = jnp.floor(words + 0.5)
    ext = jnp.where(row == 4, first, ext)
    ext = jnp.where(row == 5, (words - first) * FULL, ext)
    ext = jnp.where(row == 6, code, ext)
    for k in range(2 * TURNS):
        words, code = encode(acc[k * HB : (k + 1) * HB, :])
        out[k * HB : (k + 1) * HB, :] = integer(jnp.floor(words + 0.5))
        ext = jnp.where(row == 8 + k, code, ext)
    out[BAND:, :] = integer(jnp.floor(ext + 0.5))


def collect(which, table, arrived):
    acc = jax.ShapeDtypeStruct((BAND + 8, BF), F32)
    if which:
        out_shape = jax.ShapeDtypeStruct((BAND + 16, BF), jnp.int16)
        out_specs = VMEM
        scratch = [pltpu.VMEM((BAND + 8, BF), F32)]
    else:
        out_shape = [acc, jax.ShapeDtypeStruct((TURNS, N_COL, BF, BF), F32)]
        out_specs = [VMEM, HBM]
        scratch = [pltpu.VMEM((N_COL, BF, BF), F32), pltpu.SemaphoreType.DMA((TURNS,))]
    return pl.pallas_call(
        functools.partial(collect_kernel, which),
        out_shape=out_shape,
        grid_spec=scalars(1, [VMEM], out_specs, scratch),
        compiler_params=limit(8),
        cost_estimate=pl.CostEstimate(flops=10**6, bytes_accessed=4 * MIB, transcendentals=0),
        name=("collect_own", "collect_other")[which],
    )(table, arrived)


def merge_kernel(mine, sent, theirs, upper, lower, rest, near, far):
    eight, _ = lanes((8, BF))
    row, _ = lanes((16, BF))
    got = theirs[BAND:, :].astype(F32)
    own = sent[BAND:, :].astype(F32)

    def line(rows, index):
        return rows[index : index + 1, :]

    def energy(rows):
        return decode(line(rows, 4) + line(rows, 5) * (1.0 / FULL), line(rows, 6))

    more = jnp.where(eight < TURNS, decode(got[:8, :], line(got, 7)), 0.0)
    rest[...] = jnp.where(eight == TURNS, energy(own) + energy(got), mine[BAND:, :] + more)
    row_id, col_id, _ = position()
    ahead = (row_id & (KB - 1)) < col_id
    codes = [jnp.zeros((16, BF), F32)] * 2
    for t in range(TURNS):
        span = slice(t * HB, (t + 1) * HB)
        words = []
        for low, full in ((0, upper), (1, lower)):
            k = low * TURNS + t
            whole = slice(k * HB, (k + 1) * HB)
            total = mine[whole, :] + decode(theirs[whole, :].astype(F32), line(got, 8 + k))
            full[span, :] = total
            scaled, code = encode(total)
            words.append(scaled)
            codes[low] = jnp.where(row == t, code, codes[low])
        near[span, :] = integer(jnp.floor(jnp.where(ahead, words[0], words[1]) + 0.5))
        far[span, :] = integer(jnp.floor(jnp.where(ahead, words[1], words[0]) + 0.5))
    near[TURNS * HB :, :] = integer(jnp.floor(jnp.where(ahead, codes[0], codes[1]) + 0.5))
    far[TURNS * HB :, :] = integer(jnp.floor(jnp.where(ahead, codes[1], codes[0]) + 0.5))


def merge(mine, sent, theirs):
    half = jax.ShapeDtypeStruct((TURNS * HB, BF), F32)
    words = jax.ShapeDtypeStruct((TURNS * HB + 16, BF), jnp.int16)
    return pl.pallas_call(
        merge_kernel,
        out_shape=[half, half, jax.ShapeDtypeStruct((8, BF), F32), words, words],
        in_specs=[VMEM] * 3,
        out_specs=[VMEM] * 5,
        compiler_params=limit(4),
        name="merge",
    )(mine, sent, theirs)


def place_kernel(upper, lower, rest, near, far, blank, out, blocks, sems):
    del blank
    row_id, col_id, _ = position()
    shift = (col_id - row_id) & (N_COL - 1)

    def part(ref, turn):
        return ref[pl.ds(pl.multiple_of(turn * HB, HB), HB), :]

    ahead = (row_id & (KB - 1)) < col_id

    def coded(from_near, turn):
        code = jnp.where(from_near, near[TURNS * HB :, :].astype(F32), far[TURNS * HB :, :].astype(F32))
        words = jnp.where(from_near, part(near, turn).astype(F32), part(far, turn).astype(F32))
        return decode(words, pick_row(code, turn))

    def write(t, low, at):
        slot = TURNS * low + t
        return pltpu.make_async_copy(blocks.at[slot], out.at[t, at], sems.at[slot])

    for finish in (False, True):
        for t in range(TURNS):
            at = (row_id + N_ROW * t + shift) >> 3

            @pl.when((shift > 0) & (at < N_COL))
            def _():
                if finish:
                    write(t, 0, at).wait()
                else:
                    turn = t + jnp.where(row_id + shift >= N_ROW, 1, 0)
                    blocks[t, :HB, :] = part(upper, t)
                    blocks[t, HB:, :] = coded(ahead, jnp.minimum(turn, TURNS - 1))
                    write(t, 0, at).start()

            @pl.when((shift > 0) & (at > 0))
            def _():
                if finish:
                    write(t, 1, at - 1).wait()
                else:
                    turn = t - jnp.where(row_id + shift < N_COL, 1, 0)
                    top = coded(jnp.logical_not(ahead), jnp.maximum(turn, 0))
                    blocks[TURNS + t] = jnp.concatenate([top, part(lower, t)], axis=0).T
                    write(t, 1, at - 1).start()

            @pl.when(shift == 0)
            def _():
                if finish:
                    write(t, 0, at).wait()
                else:
                    blocks[t] = unpack_symmetric(part(upper, t), rest[t : t + 1, :])
                    write(t, 0, at).start()


def place(upper, lower, rest, near, far, blank):
    return pl.pallas_call(
        place_kernel,
        out_shape=jax.ShapeDtypeStruct((TURNS, N_COL, BF, BF), F32),
        in_specs=[VMEM] * 5 + [HBM],
        out_specs=HBM,
        scratch_shapes=[
            pltpu.VMEM((2 * TURNS, BF, BF), F32),
            pltpu.SemaphoreType.DMA((2 * TURNS,)),
        ],
        input_output_aliases={5: 0},
        compiler_params=limit(4),
        name="place",
    )(upper, lower, rest, near, far, blank)


def mirror_pairs(across):
    pairs = []
    for row in range(N_ROW):
        for col in range(N_COL):
            half = (row // KB) ^ across
            pairs.append((row * N_COL + col, (half * KB + col) * N_COL + row % KB))
    return pairs


def exchange(parts):
    return lax.all_to_all(parts, ALL, 0, 0, axis_index_groups=GROUPS, tiled=True)


def shards(density, basis, weights, batch_start, batch_count):
    swap = [(0, 1), (1, 0)]
    held, sent = share(density)
    theirs = lax.ppermute(sent, "h", swap)
    table = route(batch_start, batch_count)
    packed = pack(table, held, theirs)
    window = exchange(packed)

    outgoing = batches(table, weights, turn(table, basis), window)
    arrived = exchange(outgoing)

    sent = collect(1, table, arrived)
    theirs = lax.ppermute(sent, "h", swap)
    mine, blank = collect(0, table, arrived)
    upper, lower, rest, near, far = merge(mine, sent, theirs)
    near = lax.ppermute(near, ALL, mirror_pairs(0))
    far = lax.ppermute(far, ALL, mirror_pairs(1))
    potential = place(upper, lower, rest, near, far, blank)
    return potential, rest[TURNS, 0] / (NBLK * BF)


def solution(mesh):
    fine = Mesh(np.asarray(mesh.devices).reshape(2, 2, 4, 4, 2), ALL)
    in_specs = (P(ROW, COL), P(ALL), P(ALL), P(), P())
    out_specs = (P(ROW, COL), P())
    return jax.shard_map(shards, mesh=fine, in_specs=in_specs, out_specs=out_specs, check_vma=False)
```

```python
import functools
import math

import jax
import jax.numpy as jnp
import numpy as np
from jax import lax
from jax.experimental import pallas as pl
from jax.experimental.pallas import tpu as pltpu
from jax.sharding import Mesh, PartitionSpec as P

CX = 0.7385587663820224
MU = 0.2195149727645171
KAPPA = 0.804
BF = 128
KB = 8
NBLK = 64
G = 256
SLOTS = 3
KF = 1024
N_ROW = 16
N_COL = 8
TURNS = NBLK // N_ROW
PEERS = 64
MIB = 1024 * 1024
HB = BF // 2
EXT = SLOTS * HB
ROWS = EXT + 16
BAND = 2 * TURNS * HB
ROW = ("h", "xl", "y")
COL = ("z", "c")
ALL = ROW + COL
ORDER = [
    47, 14, 49, 25, 4, 51, 17, 37, 3, 26, 56, 35, 52, 29, 33, 10,
    36, 42, 20, 32, 43, 41, 48, 62, 12, 27, 39, 44, 16, 55, 57, 46,
    19, 0, 15, 8, 28, 24, 30, 58, 34, 13, 23, 9, 61, 1, 11, 38,
    18, 60, 59, 7, 2, 5, 21, 6, 45, 53, 54, 22, 63, 50, 40, 31,
]
PLACE = [ORDER.index(x) for x in range(PEERS)]
GROUPS = [[h * PEERS + x for x in ORDER] for h in range(2)]
VMEM = pl.BlockSpec(memory_space=pltpu.VMEM)
HBM = pl.BlockSpec(memory_space=pltpu.HBM)
F32 = jnp.float32
BF16 = jnp.bfloat16


def lanes(shape):
    return lax.broadcasted_iota(jnp.int32, shape, 0), lax.broadcasted_iota(jnp.int32, shape, 1)


def pack_symmetric(full):
    r, c = lanes((HB, BF))
    top, bottom = full[:HB], full[HB:]
    packed = jnp.where((c >= HB) | (r <= c), top, pltpu.roll(bottom, HB, 1))
    row = jnp.sum(jnp.where(c - HB == r, bottom, 0.0), axis=0, keepdims=True)
    return packed, row


def unpack_symmetric(packed, row):
    r, c = lanes((HB, BF))
    flip = jnp.concatenate([packed, packed], axis=0).T
    top = jnp.where((c >= HB) | (r <= c), packed, flip[:HB])
    corner = jnp.where(c - HB < r, pltpu.roll(packed, HB, 1), flip[:HB])
    corner = jnp.where(c - HB == r, row, corner)
    return jnp.concatenate([top, jnp.where(c < HB, flip[HB:], corner)], axis=0)


def pick_row(rows, index):
    r, _ = lanes(rows.shape)
    return jnp.sum(jnp.where(r == index, rows, 0.0), axis=0, keepdims=True)


def position():
    h = lax.axis_index("h")
    row_id = (h * 2 + lax.axis_index("xl")) * 4 + lax.axis_index("y")
    return row_id, lax.axis_index("z") * 2 + lax.axis_index("c"), h


def entry(starts, peer, slot, where):
    row_id, col_id, h = where
    start = starts[(h * PEERS + ORDER[peer]) * SLOTS + slot]
    i = start + ((row_id - start) & (KB - 1))
    j = start + ((col_id - start) & (KB - 1))
    other = ((i >> 3) & 1) ^ h
    turn = i >> 4
    below = jnp.where(j < i, TURNS, 0)
    return other, turn, below + turn


def scalars(count, in_specs, out_specs, scratch_shapes=()):
    return pltpu.PrefetchScalarGridSpec(
        num_scalar_prefetch=count,
        grid=(),
        in_specs=in_specs,
        out_specs=out_specs,
        scratch_shapes=list(scratch_shapes),
    )


def limit(mib):
    return pltpu.CompilerParams(vmem_limit_bytes=mib * MIB)


def share_kernel(density, out, copy, ups, lows, sems):
    row_id, col_id, _ = position()
    shift = (col_id - row_id) & (N_COL - 1)
    row, _ = lanes((16, BF))
    loads = []
    for t in range(TURNS):
        at = (row_id + N_ROW * t + shift) >> 3
        up = density.at[t, jnp.minimum(at, N_COL - 1)]
        low = density.at[t, jnp.maximum(at - 1, 0)]
        loads.append(pltpu.make_async_copy(up, ups.at[t], sems.at[t]))
        loads.append(pltpu.make_async_copy(low, lows.at[t], sems.at[TURNS + t]))
    for load in loads:
        load.start()
    for load in loads:
        load.wait()

    @pl.when(shift > 0)
    def _():
        for t in range(TURNS):
            low = TURNS * HB + t * HB
            out[t * HB : (t + 1) * HB, :] = ups[t, :HB, :]
            out[low : low + HB, :] = lows[t].astype(F32).T[HB:].astype(BF16)
        out[BAND:, :] = jnp.zeros((16, BF), BF16)

    @pl.when(shift == 0)
    def _():
        ext = jnp.zeros((16, BF), F32)
        for t in range(TURNS):
            packed, line = pack_symmetric(ups[t].astype(F32))
            out[t * HB : (t + 1) * HB, :] = packed.astype(BF16)
            ext = jnp.where(row == t, line, ext)
        out[TURNS * HB : BAND, :] = jnp.zeros((TURNS * HB, BF), BF16)
        out[BAND:, :] = ext.astype(BF16)

    copy[...] = out[...]


def share(density):
    held = jax.ShapeDtypeStruct((BAND + 16, BF), BF16)
    return pl.pallas_call(
        share_kernel,
        out_shape=[held, held],
        in_specs=[HBM],
        out_specs=[VMEM, VMEM],
        scratch_shapes=[
            pltpu.VMEM((TURNS, BF, BF), BF16),
            pltpu.VMEM((TURNS, BF, BF), BF16),
            pltpu.SemaphoreType.DMA((2 * TURNS,)),
        ],
        compiler_params=limit(4),
        name="share",
    )(density)


CHUNK = 8
ALL_SLOTS = PEERS * SLOTS
BOUNDS = 2 * ALL_SLOTS
STRIDE = 16
OWN = BOUNDS + 2 * STRIDE
PLACES = OWN + STRIDE


def route_kernel(starts, counts, table):
    where = position()
    me = where[0] * N_COL + where[1]
    for slot in range(SLOTS):
        table[OWN + slot] = starts[me * SLOTS + slot]
    table[OWN + SLOTS] = counts[me]

    ends = (jnp.int32(0), jnp.int32(0))
    for peer in range(PEERS):
        table[PLACES + peer] = PLACE[peer]
        if peer % CHUNK == 0:
            for which in range(2):
                table[BOUNDS + which * STRIDE + peer // CHUNK] = ends[which]

        def one(slot, ends):
            other, _, at = entry(starts, peer, slot, where)
            index = jnp.where(other == 1, ends[1], ALL_SLOTS + ends[0])
            table[index] = peer + slot * PEERS + at * (4 * PEERS)
            return ends[0] + 1 - other, ends[1] + other

        ends = one(0, ends)
        ends = lax.fori_loop(1, counts[where[2] * PEERS + ORDER[peer]], one, ends)
    for which in range(2):
        table[BOUNDS + which * STRIDE + PEERS // CHUNK] = ends[which]


def route(starts, counts):
    scalar = pl.BlockSpec(memory_space=pltpu.SMEM)
    return pl.pallas_call(
        route_kernel,
        out_shape=jax.ShapeDtypeStruct((PLACES + PEERS,), jnp.int32),
        in_specs=[scalar, scalar],
        out_specs=scalar,
        compiler_params=limit(4),
        cost_estimate=pl.CostEstimate(flops=10**6, bytes_accessed=4 * MIB, transcendentals=0),
        name="route",
    )(starts, counts)


def first_of(table, which, chunk):
    return table[BOUNDS + which * STRIDE + chunk]


def walk(table, which, low, high, body):
    base = 0 if which else ALL_SLOTS

    def step(index, carry):
        code = table[base + index]
        slot = (code >> 6) & 3
        at = pl.multiple_of((code >> 8) * HB, HB)
        body(code & (PEERS - 1), pl.multiple_of(slot * HB, HB), at, slot)
        return carry

    lax.fori_loop(low, high, step, 0)


def pack_kernel(table, mine, theirs, out, buf, sems):
    row_id, col_id, h = position()
    row, _ = lanes((16, BF))
    held = (mine, theirs)

    @pl.when(((col_id - row_id) & (KB - 1)) == 0)
    def _():
        ext = jnp.zeros((16, BF), F32)
        for which in range(2):
            lines = held[which][BAND:, :].astype(F32)
            for turn in range(TURNS):
                at = 2 * turn + (h ^ which)
                ext = jnp.where(row == at, lines[turn : turn + 1, :], ext)
        ext = ext.astype(BF16)
        for peer in range(PEERS):
            buf[peer, EXT:, :] = ext

    def send(chunk):
        span = pl.ds(pl.multiple_of(chunk * CHUNK, CHUNK), CHUNK)
        return pltpu.make_async_copy(buf.at[span], out.at[span], sems.at[chunk])

    def one_chunk(chunk, carry):
        for which in range(2):

            def copy(peer, span, at, slot):
                buf[peer, pl.ds(span, HB), :] = held[which][pl.ds(at, HB), :]

            low, high = first_of(table, which, chunk), first_of(table, which, chunk + 1)
            walk(table, which, low, high, copy)
        send(chunk).start()
        return carry

    lax.fori_loop(0, PEERS // CHUNK, one_chunk, 0)

    def drain(chunk, carry):
        send(chunk).wait()
        return carry

    lax.fori_loop(0, PEERS // CHUNK, drain, 0)


def pack(table, mine, theirs):
    return pl.pallas_call(
        pack_kernel,
        out_shape=jax.ShapeDtypeStruct((PEERS, ROWS, BF), BF16),
        grid_spec=scalars(
            1,
            [VMEM, VMEM],
            HBM,
            [
                pltpu.VMEM((PEERS, ROWS, BF), BF16),
                pltpu.SemaphoreType.DMA((PEERS // CHUNK,)),
            ],
        ),
        compiler_params=limit(8),
        name="pack",
    )(table, mine, theirs)


def turn_kernel(table, basis, out, held, turned, sem_in, sem_out):
    count = table[OWN + SLOTS]

    def load(slot):
        return pltpu.make_async_copy(basis.at[slot], held.at[slot], sem_in.at[slot])

    def store(slot):
        return pltpu.make_async_copy(turned.at[slot], out.at[slot], sem_out.at[slot])

    def fetch(slot, carry):
        load(slot).start()
        return carry

    def work(slot, carry):
        load(slot).wait()
        for k in range(4):
            for o in range(KB):
                span = slice(o * BF, (o + 1) * BF)
                turned[slot, k, span, :] = held[slot, k, :, span].T
        store(slot).start()
        return carry

    def drain(slot, carry):
        store(slot).wait()
        return carry

    lax.fori_loop(0, count, fetch, 0)
    lax.fori_loop(0, count, work, 0)
    lax.fori_loop(0, count, drain, 0)


def turn(table, basis):
    return pl.pallas_call(
        turn_kernel,
        out_shape=jax.ShapeDtypeStruct((SLOTS, 4, KF, G), BF16),
        grid_spec=scalars(
            1,
            [HBM],
            HBM,
            [
                pltpu.VMEM((SLOTS, 4, G, KF), BF16),
                pltpu.VMEM((SLOTS, 4, KF, G), BF16),
                pltpu.SemaphoreType.DMA((SLOTS,)),
                pltpu.SemaphoreType.DMA((SLOTS,)),
            ],
        ),
        compiler_params=limit(48),
        cost_estimate=pl.CostEstimate(flops=10**6, bytes_accessed=24 * MIB, transcendentals=0),
        name="turn",
    )(table, basis)


def dot_nt(x, y):
    return lax.dot_general(x, y, (((1,), (1,)), ((), ())), preferred_element_type=F32)


def batch_kernel(
    table, weights, flipped, window, out, turned, mat, product, left, right, lines, sems
):
    count = table[OWN + SLOTS]
    row, lane = lanes((16, BF))

    def flipped_copy(slot, k):
        return pltpu.make_async_copy(flipped.at[slot, k], turned.at[slot, k], sems.at[slot, k])

    def fetch(slot, carry):
        for k in range(4):
            flipped_copy(slot, k).start()
        return carry

    lax.fori_loop(0, count, fetch, 0)
    lines[...] = jnp.zeros(lines.shape, F32)

    def classes(slot):
        start = table[OWN + slot]
        return start, [(start + o) & (KB - 1) for o in range(KB)]

    def place_of(a, b):
        return table[PLACES + a * KB + b]

    def rows_of(slot):
        return pl.ds(pl.multiple_of(slot * HB, HB), HB)

    def assemble(slot, quarter):
        start, cls = classes(slot)
        span = rows_of(slot)
        for o1 in ((0, 7), (1, 6), (2, 5), (3, 4))[quarter]:
            r1 = slice(o1 * BF, (o1 + 1) * BF)
            for o2 in range(o1 + 1, KB):
                r2 = slice(o2 * BF, (o2 + 1) * BF)
                top = window[place_of(cls[o1], cls[o2]), span, :]
                bottom = window[place_of(cls[o2], cls[o1]), span, :]
                block = jnp.concatenate([top, bottom], axis=0)
                mat[r1, r2] = block
                mat[r2, r1] = block.T
            diagonal = place_of(cls[o1], cls[o1])
            line = pick_row(window[diagonal, EXT:, :].astype(F32), (start + o1) >> 3)
            block = unpack_symmetric(window[diagonal, span, :].astype(F32), line)
            mat[r1, r1] = block.astype(BF16)

    for quarter in range(4):
        assemble(0, quarter)

    def work(slot, total):
        _, cls = classes(slot)
        span = rows_of(slot)
        flipped_copy(slot, 0).wait()
        for t in range(4):
            part = slice(256 * t, 256 * (t + 1))
            product[part, :] = jnp.dot(mat[part, :], turned[slot, 0], preferred_element_type=F32)
        for k in range(1, 4):
            flipped_copy(slot, k).wait()
        sums = [jnp.zeros((8, G), F32) for _ in range(4)]
        for t in range(KF // BF):
            span_t = slice(t * BF, (t + 1) * BF)
            for k in range(4):
                terms = turned[slot, k, span_t, :].astype(F32) * product[span_t, :]
                sums[k] += jnp.sum(terms.reshape(BF // 8, 8, G), axis=0)
        sums = [jnp.sum(x, axis=0, keepdims=True) for x in sums]
        rho = sums[0]
        grads = [2.0 * x for x in sums[1:]]
        sigma = grads[0] * grads[0] + grads[1] * grads[1] + grads[2] * grads[2]
        quad = weights[pl.ds(slot, 1), :]
        square = rho * rho + 1.0
        logs = jnp.log(square)
        cube = jnp.exp(logs * (1.0 / 3.0))
        scaled = cube * cube
        reduced = sigma / (scaled * scaled)
        denom = 1.0 + MU * reduced / KAPPA
        factor = 1.0 + MU * reduced / denom
        slope = MU / denom / denom
        point = -CX * scaled * factor
        by_rho = (-CX * 2.0) * rho / cube * ((2.0 / 3.0) * factor - (4.0 / 3.0) * slope * reduced)
        by_sigma = -CX * slope / scaled
        wr = 0.5 * quad * by_rho
        ws = 2.0 * quad * by_sigma
        total = total + jnp.sum(quad * point)
        coeffs = [wr] + [ws * x for x in grads]
        for t in range(4):
            lo, hi = 256 * t, 256 * (t + 1)
            phi = turned[slot, 0, lo:hi, :]
            mixed = coeffs[0] * phi.astype(F32)
            for k in range(1, 4):
                mixed += coeffs[k] * turned[slot, k, lo:hi, :].astype(F32)
            mixed = mixed.astype(BF16)
            left[lo:hi, :G] = phi
            left[lo:hi, G:] = mixed
            right[lo:hi, :G] = mixed
            right[lo:hi, G:] = phi
        for t in range(4):
            lo, hi = 256 * t, 256 * (t + 1)
            assemble(jnp.minimum(slot + 1, SLOTS - 1), t)
            rows = dot_nt(left[lo:hi, :], right[lo:, :])
            for k in range(2):
                o1 = 2 * t + k
                for o2 in range(o1, KB):
                    c0 = o2 * BF - lo
                    block = rows[k * BF : (k + 1) * BF, c0 : c0 + BF]
                    if o2 == o1:
                        packed, line = pack_symmetric(block)
                        out[place_of(cls[o1], cls[o1]), span, :] = packed.astype(BF16)
                        lines[cls[o1]] = jnp.where(row == slot, line, lines[cls[o1]])
                    else:
                        out[place_of(cls[o1], cls[o2]), span, :] = block[:HB].astype(BF16)
                        out[place_of(cls[o2], cls[o1]), span, :] = block[HB:].astype(BF16)
        return total

    total = jnp.full((16, BF), lax.fori_loop(0, count, work, jnp.float32(0.0)), F32)
    first = total.astype(BF16).astype(F32)
    second = (total - first).astype(BF16).astype(F32)
    third = total - first - second
    spread = jnp.where(lane == 0, first, jnp.where(lane == 1, second, third))
    energy = jnp.where((row == 0) & (lane < 3), spread, 0.0)
    for peer in range(PEERS):
        if peer % (KB + 1) == 0:
            out[PLACE[peer], EXT:, :] = (lines[peer // (KB + 1)] + energy).astype(BF16)
        else:
            out[PLACE[peer], EXT:, :] = energy.astype(BF16)


def batches(table, weights, flipped, window):
    return pl.pallas_call(
        batch_kernel,
        out_shape=jax.ShapeDtypeStruct((PEERS, ROWS, BF), BF16),
        grid_spec=scalars(
            1,
            [VMEM, HBM, VMEM],
            VMEM,
            [
                pltpu.VMEM((SLOTS, 4, KF, G), BF16),
                pltpu.VMEM((KF, KF), BF16),
                pltpu.VMEM((KF, G), F32),
                pltpu.VMEM((KF, 2 * G), BF16),
                pltpu.VMEM((KF, 2 * G), BF16),
                pltpu.VMEM((KB, 16, BF), F32),
                pltpu.SemaphoreType.DMA((SLOTS, 4)),
            ],
        ),
        compiler_params=limit(44),
        name="batches",
    )(table, weights, flipped, window)


STEP = math.log(2.0) / 128.0
FULL = 32767.0


def integer(values):
    return values.astype(jnp.int32).astype(jnp.int16)


def encode(values):
    top = jnp.max(jnp.max(jnp.abs(values), axis=0, keepdims=True), axis=1, keepdims=True)
    code = jnp.ceil(jnp.log(jnp.maximum(top, 2.0**-110)) * (1.0 / STEP))
    scaled = values * jnp.exp(math.log(FULL) - code * STEP)
    return jnp.clip(scaled, -FULL, FULL), code


def decode(words, code):
    return words.astype(F32) * jnp.exp(code.astype(F32) * STEP - math.log(FULL))


def collect_kernel(which, table, arrived, *refs):
    row_id, col_id, _ = position()
    on_diagonal = ((col_id - row_id) & (KB - 1)) == 0
    row, lane = lanes((16, BF))
    eight, _ = lanes((8, BF))
    if which:
        out, acc = refs
    else:
        acc, blank, zeros, sems = refs
        zeros[...] = jnp.zeros(zeros.shape, F32)
        fills = [pltpu.make_async_copy(zeros, blank.at[t], sems.at[t]) for t in range(TURNS)]
        for fill in fills:
            fill.start()
    acc[...] = jnp.zeros(acc.shape, F32)
    high = first_of(table, which, PEERS // CHUNK)

    def add(peer, span, at, slot):
        acc[pl.ds(at, HB), :] += arrived[peer, pl.ds(span, HB), :].astype(F32)

    def add_line(peer, span, at, slot):
        line = jnp.where(lane >= HB, arrived[peer, EXT:, :].astype(F32), 0.0)
        acc[BAND:, :] += jnp.where(eight == at // HB, pick_row(line, slot), 0.0)

    walk(table, which, 0, high, add)
    pl.when(on_diagonal)(lambda: walk(table, which, 0, high, add_line))
    if not which:
        for fill in fills:
            fill.wait()
        return

    words, code = encode(acc[BAND:, :])
    ext = jnp.concatenate([words, words], axis=0)
    ext = jnp.where(row == 7, code, ext)
    total = jnp.sum(arrived[:, EXT:, :].astype(F32), axis=0)
    total = jnp.where((row == 0) & (lane < 3), total, 0.0)
    total = jnp.sum(jnp.sum(total, axis=0, keepdims=True), axis=1, keepdims=True)
    words, code = encode(total)
    first = jnp.floor(words + 0.5)
    ext = jnp.where(row == 4, first, ext)
    ext = jnp.where(row == 5, (words - first) * FULL, ext)
    ext = jnp.where(row == 6, code, ext)
    for k in range(2 * TURNS):
        words, code = encode(acc[k * HB : (k + 1) * HB, :])
        out[k * HB : (k + 1) * HB, :] = integer(jnp.floor(words + 0.5))
        ext = jnp.where(row == 8 + k, code, ext)
    out[BAND:, :] = integer(jnp.floor(ext + 0.5))


def collect(which, table, arrived):
    acc = jax.ShapeDtypeStruct((BAND + 8, BF), F32)
    if which:
        out_shape = jax.ShapeDtypeStruct((BAND + 16, BF), jnp.int16)
        out_specs = VMEM
        scratch = [pltpu.VMEM((BAND + 8, BF), F32)]
    else:
        out_shape = [acc, jax.ShapeDtypeStruct((TURNS, N_COL, BF, BF), F32)]
        out_specs = [VMEM, HBM]
        scratch = [pltpu.VMEM((N_COL, BF, BF), F32), pltpu.SemaphoreType.DMA((TURNS,))]
    return pl.pallas_call(
        functools.partial(collect_kernel, which),
        out_shape=out_shape,
        grid_spec=scalars(1, [VMEM], out_specs, scratch),
        compiler_params=limit(8),
        cost_estimate=pl.CostEstimate(flops=10**6, bytes_accessed=4 * MIB, transcendentals=0),
        name=("collect_own", "collect_other")[which],
    )(table, arrived)


def merge_kernel(mine, sent, theirs, upper, lower, rest, near, far):
    eight, _ = lanes((8, BF))
    row, _ = lanes((16, BF))
    got = theirs[BAND:, :].astype(F32)
    own = sent[BAND:, :].astype(F32)

    def line(rows, index):
        return rows[index : index + 1, :]

    def energy(rows):
        return decode(line(rows, 4) + line(rows, 5) * (1.0 / FULL), line(rows, 6))

    more = jnp.where(eight < TURNS, decode(got[:8, :], line(got, 7)), 0.0)
    rest[...] = jnp.where(eight == TURNS, energy(own) + energy(got), mine[BAND:, :] + more)
    row_id, col_id, _ = position()
    ahead = (row_id & (KB - 1)) < col_id
    codes = [jnp.zeros((16, BF), F32)] * 2
    for t in range(TURNS):
        span = slice(t * HB, (t + 1) * HB)
        words = []
        for low, full in ((0, upper), (1, lower)):
            k = low * TURNS + t
            whole = slice(k * HB, (k + 1) * HB)
            total = mine[whole, :] + decode(theirs[whole, :].astype(F32), line(got, 8 + k))
            full[span, :] = total
            scaled, code = encode(total)
            words.append(scaled)
            codes[low] = jnp.where(row == t, code, codes[low])
        near[span, :] = integer(jnp.floor(jnp.where(ahead, words[0], words[1]) + 0.5))
        far[span, :] = integer(jnp.floor(jnp.where(ahead, words[1], words[0]) + 0.5))
    near[TURNS * HB :, :] = integer(jnp.floor(jnp.where(ahead, codes[0], codes[1]) + 0.5))
    far[TURNS * HB :, :] = integer(jnp.floor(jnp.where(ahead, codes[1], codes[0]) + 0.5))


def merge(mine, sent, theirs):
    half = jax.ShapeDtypeStruct((TURNS * HB, BF), F32)
    words = jax.ShapeDtypeStruct((TURNS * HB + 16, BF), jnp.int16)
    return pl.pallas_call(
        merge_kernel,
        out_shape=[half, half, jax.ShapeDtypeStruct((8, BF), F32), words, words],
        in_specs=[VMEM] * 3,
        out_specs=[VMEM] * 5,
        compiler_params=limit(4),
        name="merge",
    )(mine, sent, theirs)


def place_kernel(upper, lower, rest, near, far, blank, out, blocks, sems):
    del blank
    row_id, col_id, _ = position()
    shift = (col_id - row_id) & (N_COL - 1)

    def part(ref, turn):
        return ref[pl.ds(pl.multiple_of(turn * HB, HB), HB), :]

    ahead = (row_id & (KB - 1)) < col_id

    def coded(from_near, turn):
        code = jnp.where(from_near, near[TURNS * HB :, :].astype(F32), far[TURNS * HB :, :].astype(F32))
        words = jnp.where(from_near, part(near, turn).astype(F32), part(far, turn).astype(F32))
        return decode(words, pick_row(code, turn))

    def write(t, low, at):
        slot = TURNS * low + t
        return pltpu.make_async_copy(blocks.at[slot], out.at[t, at], sems.at[slot])

    for finish in (False, True):
        for t in range(TURNS):
            at = (row_id + N_ROW * t + shift) >> 3

            @pl.when((shift > 0) & (at < N_COL))
            def _():
                if finish:
                    write(t, 0, at).wait()
                else:
                    turn = t + jnp.where(row_id + shift >= N_ROW, 1, 0)
                    blocks[t, :HB, :] = part(upper, t)
                    blocks[t, HB:, :] = coded(ahead, jnp.minimum(turn, TURNS - 1))
                    write(t, 0, at).start()

            @pl.when((shift > 0) & (at > 0))
            def _():
                if finish:
                    write(t, 1, at - 1).wait()
                else:
                    turn = t - jnp.where(row_id + shift < N_COL, 1, 0)
                    top = coded(jnp.logical_not(ahead), jnp.maximum(turn, 0))
                    blocks[TURNS + t] = jnp.concatenate([top, part(lower, t)], axis=0).T
                    write(t, 1, at - 1).start()

            @pl.when(shift == 0)
            def _():
                if finish:
                    write(t, 0, at).wait()
                else:
                    blocks[t] = unpack_symmetric(part(upper, t), rest[t : t + 1, :])
                    write(t, 0, at).start()


def place(upper, lower, rest, near, far, blank):
    return pl.pallas_call(
        place_kernel,
        out_shape=jax.ShapeDtypeStruct((TURNS, N_COL, BF, BF), F32),
        in_specs=[VMEM] * 5 + [HBM],
        out_specs=HBM,
        scratch_shapes=[
            pltpu.VMEM((2 * TURNS, BF, BF), F32),
            pltpu.SemaphoreType.DMA((2 * TURNS,)),
        ],
        input_output_aliases={5: 0},
        compiler_params=limit(4),
        name="place",
    )(upper, lower, rest, near, far, blank)


def mirror_pairs(across):
    pairs = []
    for row in range(N_ROW):
        for col in range(N_COL):
            half = (row // KB) ^ across
            pairs.append((row * N_COL + col, (half * KB + col) * N_COL + row % KB))
    return pairs


def exchange(parts):
    return lax.all_to_all(parts, ALL, 0, 0, axis_index_groups=GROUPS, tiled=True)


def shards(density, basis, weights, batch_start, batch_count):
    swap = [(0, 1), (1, 0)]
    held, sent = share(density)
    theirs = lax.ppermute(sent, "h", swap)
    table = route(batch_start, batch_count)
    packed = pack(table, held, theirs)
    window = exchange(packed)

    outgoing = batches(table, weights, turn(table, basis), window)
    arrived = exchange(outgoing)

    sent = collect(1, table, arrived)
    theirs = lax.ppermute(sent, "h", swap)
    mine, blank = collect(0, table, arrived)
    upper, lower, rest, near, far = merge(mine, sent, theirs)
    near = lax.ppermute(near, ALL, mirror_pairs(0))
    far = lax.ppermute(far, ALL, mirror_pairs(1))
    potential = place(upper, lower, rest, near, far, blank)
    return potential, rest[TURNS, 0] / (NBLK * BF)


def solution(mesh):
    fine = Mesh(np.asarray(mesh.devices).reshape(2, 2, 4, 4, 2), ALL)
    in_specs = (P(ROW, COL), P(ALL), P(ALL), P(), P())
    out_specs = (P(ROW, COL), P())
    return jax.shard_map(shards, mesh=fine, in_specs=in_specs, out_specs=out_specs, check_vma=False)
```

```python
import functools
import math

import jax
import jax.numpy as jnp
import numpy as np
from jax import lax
from jax.experimental import pallas as pl
from jax.experimental.pallas import tpu as pltpu
from jax.sharding import Mesh, PartitionSpec as P

CX = 0.7385587663820224
MU = 0.2195149727645171
KAPPA = 0.804
BF = 128
KB = 8
NBLK = 64
G = 256
SLOTS = 3
KF = 1024
N_ROW = 16
N_COL = 8
TURNS = NBLK // N_ROW
PEERS = 64
MIB = 1024 * 1024
HB = BF // 2
EXT = SLOTS * HB
ROWS = EXT + 16
BAND = 2 * TURNS * HB
ROW = ("h", "xl", "y")
COL = ("z", "c")
ALL = ROW + COL
ORDER = [
    47, 14, 49, 25, 4, 51, 17, 37, 3, 26, 56, 35, 52, 29, 33, 10,
    36, 42, 20, 32, 43, 41, 48, 62, 12, 27, 39, 44, 16, 55, 57, 46,
    19, 0, 15, 8, 28, 24, 30, 58, 34, 13, 23, 9, 61, 1, 11, 38,
    18, 60, 59, 7, 2, 5, 21, 6, 45, 53, 54, 22, 63, 50, 40, 31,
]
PLACE = [ORDER.index(x) for x in range(PEERS)]
GROUPS = [[h * PEERS + x for x in ORDER] for h in range(2)]
VMEM = pl.BlockSpec(memory_space=pltpu.VMEM)
HBM = pl.BlockSpec(memory_space=pltpu.HBM)
F32 = jnp.float32
BF16 = jnp.bfloat16


def lanes(shape):
    return lax.broadcasted_iota(jnp.int32, shape, 0), lax.broadcasted_iota(jnp.int32, shape, 1)


def pack_symmetric(full):
    r, c = lanes((HB, BF))
    top, bottom = full[:HB], full[HB:]
    packed = jnp.where((c >= HB) | (r <= c), top, pltpu.roll(bottom, HB, 1))
    row = jnp.sum(jnp.where(c - HB == r, bottom, 0.0), axis=0, keepdims=True)
    return packed, row


def unpack_symmetric(packed, row):
    r, c = lanes((HB, BF))
    flip = jnp.concatenate([packed, packed], axis=0).T
    top = jnp.where((c >= HB) | (r <= c), packed, flip[:HB])
    corner = jnp.where(c - HB < r, pltpu.roll(packed, HB, 1), flip[:HB])
    corner = jnp.where(c - HB == r, row, corner)
    return jnp.concatenate([top, jnp.where(c < HB, flip[HB:], corner)], axis=0)


def pick_row(rows, index):
    r, _ = lanes(rows.shape)
    return jnp.sum(jnp.where(r == index, rows, 0.0), axis=0, keepdims=True)


def position():
    h = lax.axis_index("h")
    row_id = (h * 2 + lax.axis_index("xl")) * 4 + lax.axis_index("y")
    return row_id, lax.axis_index("z") * 2 + lax.axis_index("c"), h


def entry(starts, peer, slot, where):
    row_id, col_id, h = where
    start = starts[(h * PEERS + ORDER[peer]) * SLOTS + slot]
    i = start + ((row_id - start) & (KB - 1))
    j = start + ((col_id - start) & (KB - 1))
    other = ((i >> 3) & 1) ^ h
    turn = i >> 4
    below = jnp.where(j < i, TURNS, 0)
    return other, turn, below + turn


def scalars(count, in_specs, out_specs, scratch_shapes=()):
    return pltpu.PrefetchScalarGridSpec(
        num_scalar_prefetch=count,
        grid=(),
        in_specs=in_specs,
        out_specs=out_specs,
        scratch_shapes=list(scratch_shapes),
    )


def limit(mib):
    return pltpu.CompilerParams(vmem_limit_bytes=mib * MIB)


def share_kernel(density, out, copy, ups, lows, sems):
    row_id, col_id, _ = position()
    shift = (col_id - row_id) & (N_COL - 1)
    row, _ = lanes((16, BF))
    loads = []
    for t in range(TURNS):
        at = (row_id + N_ROW * t + shift) >> 3
        up = density.at[t, jnp.minimum(at, N_COL - 1)]
        low = density.at[t, jnp.maximum(at - 1, 0)]
        loads.append(pltpu.make_async_copy(up, ups.at[t], sems.at[t]))
        loads.append(pltpu.make_async_copy(low, lows.at[t], sems.at[TURNS + t]))
    for load in loads:
        load.start()
    for load in loads:
        load.wait()

    @pl.when(shift > 0)
    def _():
        for t in range(TURNS):
            low = TURNS * HB + t * HB
            out[t * HB : (t + 1) * HB, :] = ups[t, :HB, :]
            out[low : low + HB, :] = lows[t].astype(F32).T[HB:].astype(BF16)
        out[BAND:, :] = jnp.zeros((16, BF), BF16)

    @pl.when(shift == 0)
    def _():
        ext = jnp.zeros((16, BF), F32)
        for t in range(TURNS):
            packed, line = pack_symmetric(ups[t].astype(F32))
            out[t * HB : (t + 1) * HB, :] = packed.astype(BF16)
            ext = jnp.where(row == t, line, ext)
        out[TURNS * HB : BAND, :] = jnp.zeros((TURNS * HB, BF), BF16)
        out[BAND:, :] = ext.astype(BF16)

    copy[...] = out[...]


def share(density):
    held = jax.ShapeDtypeStruct((BAND + 16, BF), BF16)
    return pl.pallas_call(
        share_kernel,
        out_shape=[held, held],
        in_specs=[HBM],
        out_specs=[VMEM, VMEM],
        scratch_shapes=[
            pltpu.VMEM((TURNS, BF, BF), BF16),
            pltpu.VMEM((TURNS, BF, BF), BF16),
            pltpu.SemaphoreType.DMA((2 * TURNS,)),
        ],
        compiler_params=limit(4),
        name="share",
    )(density)


CHUNK = 16
ALL_SLOTS = PEERS * SLOTS
BOUNDS = 2 * ALL_SLOTS
STRIDE = 16
OWN = BOUNDS + 2 * STRIDE
PLACES = OWN + STRIDE


def route_kernel(starts, counts, table):
    where = position()
    me = where[0] * N_COL + where[1]
    for slot in range(SLOTS):
        table[OWN + slot] = starts[me * SLOTS + slot]
    table[OWN + SLOTS] = counts[me]

    ends = (jnp.int32(0), jnp.int32(0))
    for peer in range(PEERS):
        table[PLACES + peer] = PLACE[peer]
        if peer % CHUNK == 0:
            for which in range(2):
                table[BOUNDS + which * STRIDE + peer // CHUNK] = ends[which]

        def one(slot, ends):
            other, _, at = entry(starts, peer, slot, where)
            index = jnp.where(other == 1, ends[1], ALL_SLOTS + ends[0])
            table[index] = peer + slot * PEERS + at * (4 * PEERS)
            return ends[0] + 1 - other, ends[1] + other

        ends = one(0, ends)
        ends = lax.fori_loop(1, counts[where[2] * PEERS + ORDER[peer]], one, ends)
    for which in range(2):
        table[BOUNDS + which * STRIDE + PEERS // CHUNK] = ends[which]


def route(starts, counts):
    scalar = pl.BlockSpec(memory_space=pltpu.SMEM)
    return pl.pallas_call(
        route_kernel,
        out_shape=jax.ShapeDtypeStruct((PLACES + PEERS,), jnp.int32),
        in_specs=[scalar, scalar],
        out_specs=scalar,
        compiler_params=limit(4),
        cost_estimate=pl.CostEstimate(flops=10**6, bytes_accessed=4 * MIB, transcendentals=0),
        name="route",
    )(starts, counts)


def first_of(table, which, chunk):
    return table[BOUNDS + which * STRIDE + chunk]


def walk(table, which, low, high, body):
    base = 0 if which else ALL_SLOTS

    def step(index, carry):
        code = table[base + index]
        slot = (code >> 6) & 3
        at = pl.multiple_of((code >> 8) * HB, HB)
        body(code & (PEERS - 1), pl.multiple_of(slot * HB, HB), at, slot)
        return carry

    lax.fori_loop(low, high, step, 0)


def pack_kernel(table, mine, theirs, out, buf, sems):
    row_id, col_id, h = position()
    row, _ = lanes((16, BF))
    held = (mine, theirs)

    @pl.when(((col_id - row_id) & (KB - 1)) == 0)
    def _():
        ext = jnp.zeros((16, BF), F32)
        for which in range(2):
            lines = held[which][BAND:, :].astype(F32)
            for turn in range(TURNS):
                at = 2 * turn + (h ^ which)
                ext = jnp.where(row == at, lines[turn : turn + 1, :], ext)
        ext = ext.astype(BF16)
        for peer in range(PEERS):
            buf[peer, EXT:, :] = ext

    def send(chunk):
        span = pl.ds(pl.multiple_of(chunk * CHUNK, CHUNK), CHUNK)
        return pltpu.make_async_copy(buf.at[span], out.at[span], sems.at[chunk])

    def one_chunk(chunk, carry):
        for which in range(2):

            def copy(peer, span, at, slot):
                buf[peer, pl.ds(span, HB), :] = held[which][pl.ds(at, HB), :]

            low, high = first_of(table, which, chunk), first_of(table, which, chunk + 1)
            walk(table, which, low, high, copy)
        send(chunk).start()
        return carry

    lax.fori_loop(0, PEERS // CHUNK, one_chunk, 0)

    def drain(chunk, carry):
        send(chunk).wait()
        return carry

    lax.fori_loop(0, PEERS // CHUNK, drain, 0)


def pack(table, mine, theirs):
    return pl.pallas_call(
        pack_kernel,
        out_shape=jax.ShapeDtypeStruct((PEERS, ROWS, BF), BF16),
        grid_spec=scalars(
            1,
            [VMEM, VMEM],
            HBM,
            [
                pltpu.VMEM((PEERS, ROWS, BF), BF16),
                pltpu.SemaphoreType.DMA((PEERS // CHUNK,)),
            ],
        ),
        compiler_params=limit(8),
        name="pack",
    )(table, mine, theirs)


def turn_kernel(table, basis, out, held, turned, sem_in, sem_out):
    count = table[OWN + SLOTS]

    def load(slot):
        return pltpu.make_async_copy(basis.at[slot], held.at[slot], sem_in.at[slot])

    def store(slot):
        return pltpu.make_async_copy(turned.at[slot], out.at[slot], sem_out.at[slot])

    def fetch(slot, carry):
        load(slot).start()
        return carry

    def work(slot, carry):
        load(slot).wait()
        for k in range(4):
            for o in range(KB):
                span = slice(o * BF, (o + 1) * BF)
                turned[slot, k, span, :] = held[slot, k, :, span].T
        store(slot).start()
        return carry

    def drain(slot, carry):
        store(slot).wait()
        return carry

    lax.fori_loop(0, count, fetch, 0)
    lax.fori_loop(0, count, work, 0)
    lax.fori_loop(0, count, drain, 0)


def turn(table, basis):
    return pl.pallas_call(
        turn_kernel,
        out_shape=jax.ShapeDtypeStruct((SLOTS, 4, KF, G), BF16),
        grid_spec=scalars(
            1,
            [HBM],
            HBM,
            [
                pltpu.VMEM((SLOTS, 4, G, KF), BF16),
                pltpu.VMEM((SLOTS, 4, KF, G), BF16),
                pltpu.SemaphoreType.DMA((SLOTS,)),
                pltpu.SemaphoreType.DMA((SLOTS,)),
            ],
        ),
        compiler_params=limit(48),
        cost_estimate=pl.CostEstimate(flops=10**6, bytes_accessed=24 * MIB, transcendentals=0),
        name="turn",
    )(table, basis)


def dot_nt(x, y):
    return lax.dot_general(x, y, (((1,), (1,)), ((), ())), preferred_element_type=F32)


def batch_kernel(
    table, weights, flipped, window, out, turned, mat, product, left, right, lines, sems
):
    count = table[OWN + SLOTS]
    row, lane = lanes((16, BF))

    def flipped_copy(slot, k):
        return pltpu.make_async_copy(flipped.at[slot, k], turned.at[slot, k], sems.at[slot, k])

    def fetch(slot, carry):
        for k in range(4):
            flipped_copy(slot, k).start()
        return carry

    lax.fori_loop(0, count, fetch, 0)
    lines[...] = jnp.zeros(lines.shape, F32)

    def classes(slot):
        start = table[OWN + slot]
        return start, [(start + o) & (KB - 1) for o in range(KB)]

    def place_of(a, b):
        return table[PLACES + a * KB + b]

    def rows_of(slot):
        return pl.ds(pl.multiple_of(slot * HB, HB), HB)

    def assemble(slot, quarter):
        start, cls = classes(slot)
        span = rows_of(slot)
        for o1 in ((0, 7), (1, 6), (2, 5), (3, 4))[quarter]:
            r1 = slice(o1 * BF, (o1 + 1) * BF)
            for o2 in range(o1 + 1, KB):
                r2 = slice(o2 * BF, (o2 + 1) * BF)
                top = window[place_of(cls[o1], cls[o2]), span, :]
                bottom = window[place_of(cls[o2], cls[o1]), span, :]
                block = jnp.concatenate([top, bottom], axis=0)
                mat[r1, r2] = block
                mat[r2, r1] = block.T
            diagonal = place_of(cls[o1], cls[o1])
            line = pick_row(window[diagonal, EXT:, :].astype(F32), (start + o1) >> 3)
            block = unpack_symmetric(window[diagonal, span, :].astype(F32), line)
            mat[r1, r1] = block.astype(BF16)

    for quarter in range(4):
        assemble(0, quarter)

    def work(slot, total):
        _, cls = classes(slot)
        span = rows_of(slot)
        flipped_copy(slot, 0).wait()
        for t in range(4):
            part = slice(256 * t, 256 * (t + 1))
            product[part, :] = jnp.dot(mat[part, :], turned[slot, 0], preferred_element_type=F32)
        for k in range(1, 4):
            flipped_copy(slot, k).wait()
        sums = [jnp.zeros((8, G), F32) for _ in range(4)]
        for t in range(KF // BF):
            span_t = slice(t * BF, (t + 1) * BF)
            for k in range(4):
                terms = turned[slot, k, span_t, :].astype(F32) * product[span_t, :]
                sums[k] += jnp.sum(terms.reshape(BF // 8, 8, G), axis=0)
        sums = [jnp.sum(x, axis=0, keepdims=True) for x in sums]
        rho = sums[0]
        grads = [2.0 * x for x in sums[1:]]
        sigma = grads[0] * grads[0] + grads[1] * grads[1] + grads[2] * grads[2]
        quad = weights[pl.ds(slot, 1), :]
        square = rho * rho + 1.0
        logs = jnp.log(square)
        cube = jnp.exp(logs * (1.0 / 3.0))
        scaled = cube * cube
        reduced = sigma / (scaled * scaled)
        denom = 1.0 + MU * reduced / KAPPA
        factor = 1.0 + MU * reduced / denom
        slope = MU / denom / denom
        point = -CX * scaled * factor
        by_rho = (-CX * 2.0) * rho / cube * ((2.0 / 3.0) * factor - (4.0 / 3.0) * slope * reduced)
        by_sigma = -CX * slope / scaled
        wr = 0.5 * quad * by_rho
        ws = 2.0 * quad * by_sigma
        total = total + jnp.sum(quad * point)
        coeffs = [wr] + [ws * x for x in grads]
        for t in range(4):
            lo, hi = 256 * t, 256 * (t + 1)
            phi = turned[slot, 0, lo:hi, :]
            mixed = coeffs[0] * phi.astype(F32)
            for k in range(1, 4):
                mixed += coeffs[k] * turned[slot, k, lo:hi, :].astype(F32)
            mixed = mixed.astype(BF16)
            left[lo:hi, :G] = phi
            left[lo:hi, G:] = mixed
            right[lo:hi, :G] = mixed
            right[lo:hi, G:] = phi
        for t in range(4):
            lo, hi = 256 * t, 256 * (t + 1)
            assemble(jnp.minimum(slot + 1, SLOTS - 1), t)
            rows = dot_nt(left[lo:hi, :], right[lo:, :])
            for k in range(2):
                o1 = 2 * t + k
                for o2 in range(o1, KB):
                    c0 = o2 * BF - lo
                    block = rows[k * BF : (k + 1) * BF, c0 : c0 + BF]
                    if o2 == o1:
                        packed, line = pack_symmetric(block)
                        out[place_of(cls[o1], cls[o1]), span, :] = packed.astype(BF16)
                        lines[cls[o1]] = jnp.where(row == slot, line, lines[cls[o1]])
                    else:
                        out[place_of(cls[o1], cls[o2]), span, :] = block[:HB].astype(BF16)
                        out[place_of(cls[o2], cls[o1]), span, :] = block[HB:].astype(BF16)
        return total

    total = jnp.full((16, BF), lax.fori_loop(0, count, work, jnp.float32(0.0)), F32)
    first = total.astype(BF16).astype(F32)
    second = (total - first).astype(BF16).astype(F32)
    third = total - first - second
    spread = jnp.where(lane == 0, first, jnp.where(lane == 1, second, third))
    energy = jnp.where((row == 0) & (lane < 3), spread, 0.0)
    for peer in range(PEERS):
        if peer % (KB + 1) == 0:
            out[PLACE[peer], EXT:, :] = (lines[peer // (KB + 1)] + energy).astype(BF16)
        else:
            out[PLACE[peer], EXT:, :] = energy.astype(BF16)


def batches(table, weights, flipped, window):
    return pl.pallas_call(
        batch_kernel,
        out_shape=jax.ShapeDtypeStruct((PEERS, ROWS, BF), BF16),
        grid_spec=scalars(
            1,
            [VMEM, HBM, VMEM],
            VMEM,
            [
                pltpu.VMEM((SLOTS, 4, KF, G), BF16),
                pltpu.VMEM((KF, KF), BF16),
                pltpu.VMEM((KF, G), F32),
                pltpu.VMEM((KF, 2 * G), BF16),
                pltpu.VMEM((KF, 2 * G), BF16),
                pltpu.VMEM((KB, 16, BF), F32),
                pltpu.SemaphoreType.DMA((SLOTS, 4)),
            ],
        ),
        compiler_params=limit(44),
        name="batches",
    )(table, weights, flipped, window)


STEP = math.log(2.0) / 128.0
FULL = 32767.0


def integer(values):
    return values.astype(jnp.int32).astype(jnp.int16)


def encode(values):
    top = jnp.max(jnp.max(jnp.abs(values), axis=0, keepdims=True), axis=1, keepdims=True)
    code = jnp.ceil(jnp.log(jnp.maximum(top, 2.0**-110)) * (1.0 / STEP))
    scaled = values * jnp.exp(math.log(FULL) - code * STEP)
    return jnp.clip(scaled, -FULL, FULL), code


def decode(words, code):
    return words.astype(F32) * jnp.exp(code.astype(F32) * STEP - math.log(FULL))


def collect_kernel(which, table, arrived, *refs):
    row_id, col_id, _ = position()
    on_diagonal = ((col_id - row_id) & (KB - 1)) == 0
    row, lane = lanes((16, BF))
    eight, _ = lanes((8, BF))
    if which:
        out, acc = refs
    else:
        acc, blank, zeros, sems = refs
        zeros[...] = jnp.zeros(zeros.shape, F32)
        fills = [pltpu.make_async_copy(zeros, blank.at[t], sems.at[t]) for t in range(TURNS)]
        for fill in fills:
            fill.start()
    acc[...] = jnp.zeros(acc.shape, F32)
    high = first_of(table, which, PEERS // CHUNK)

    def add(peer, span, at, slot):
        acc[pl.ds(at, HB), :] += arrived[peer, pl.ds(span, HB), :].astype(F32)

    def add_line(peer, span, at, slot):
        line = jnp.where(lane >= HB, arrived[peer, EXT:, :].astype(F32), 0.0)
        acc[BAND:, :] += jnp.where(eight == at // HB, pick_row(line, slot), 0.0)

    walk(table, which, 0, high, add)
    pl.when(on_diagonal)(lambda: walk(table, which, 0, high, add_line))
    if not which:
        for fill in fills:
            fill.wait()
        return

    words, code = encode(acc[BAND:, :])
    ext = jnp.concatenate([words, words], axis=0)
    ext = jnp.where(row == 7, code, ext)
    total = jnp.sum(arrived[:, EXT:, :].astype(F32), axis=0)
    total = jnp.where((row == 0) & (lane < 3), total, 0.0)
    total = jnp.sum(jnp.sum(total, axis=0, keepdims=True), axis=1, keepdims=True)
    words, code = encode(total)
    first = jnp.floor(words + 0.5)
    ext = jnp.where(row == 4, first, ext)
    ext = jnp.where(row == 5, (words - first) * FULL, ext)
    ext = jnp.where(row == 6, code, ext)
    for k in range(2 * TURNS):
        words, code = encode(acc[k * HB : (k + 1) * HB, :])
        out[k * HB : (k + 1) * HB, :] = integer(jnp.floor(words + 0.5))
        ext = jnp.where(row == 8 + k, code, ext)
    out[BAND:, :] = integer(jnp.floor(ext + 0.5))


def collect(which, table, arrived):
    acc = jax.ShapeDtypeStruct((BAND + 8, BF), F32)
    if which:
        out_shape = jax.ShapeDtypeStruct((BAND + 16, BF), jnp.int16)
        out_specs = VMEM
        scratch = [pltpu.VMEM((BAND + 8, BF), F32)]
    else:
        out_shape = [acc, jax.ShapeDtypeStruct((TURNS, N_COL, BF, BF), F32)]
        out_specs = [VMEM, HBM]
        scratch = [pltpu.VMEM((N_COL, BF, BF), F32), pltpu.SemaphoreType.DMA((TURNS,))]
    return pl.pallas_call(
        functools.partial(collect_kernel, which),
        out_shape=out_shape,
        grid_spec=scalars(1, [VMEM], out_specs, scratch),
        compiler_params=limit(8),
        cost_estimate=pl.CostEstimate(flops=10**6, bytes_accessed=4 * MIB, transcendentals=0),
        name=("collect_own", "collect_other")[which],
    )(table, arrived)


def merge_kernel(mine, sent, theirs, upper, lower, rest, near, far):
    eight, _ = lanes((8, BF))
    row, _ = lanes((16, BF))
    got = theirs[BAND:, :].astype(F32)
    own = sent[BAND:, :].astype(F32)

    def line(rows, index):
        return rows[index : index + 1, :]

    def energy(rows):
        return decode(line(rows, 4) + line(rows, 5) * (1.0 / FULL), line(rows, 6))

    more = jnp.where(eight < TURNS, decode(got[:8, :], line(got, 7)), 0.0)
    rest[...] = jnp.where(eight == TURNS, energy(own) + energy(got), mine[BAND:, :] + more)
    row_id, col_id, _ = position()
    ahead = (row_id & (KB - 1)) < col_id
    codes = [jnp.zeros((16, BF), F32)] * 2
    for t in range(TURNS):
        span = slice(t * HB, (t + 1) * HB)
        words = []
        for low, full in ((0, upper), (1, lower)):
            k = low * TURNS + t
            whole = slice(k * HB, (k + 1) * HB)
            total = mine[whole, :] + decode(theirs[whole, :].astype(F32), line(got, 8 + k))
            full[span, :] = total
            scaled, code = encode(total)
            words.append(scaled)
            codes[low] = jnp.where(row == t, code, codes[low])
        near[span, :] = integer(jnp.floor(jnp.where(ahead, words[0], words[1]) + 0.5))
        far[span, :] = integer(jnp.floor(jnp.where(ahead, words[1], words[0]) + 0.5))
    near[TURNS * HB :, :] = integer(jnp.floor(jnp.where(ahead, codes[0], codes[1]) + 0.5))
    far[TURNS * HB :, :] = integer(jnp.floor(jnp.where(ahead, codes[1], codes[0]) + 0.5))


def merge(mine, sent, theirs):
    half = jax.ShapeDtypeStruct((TURNS * HB, BF), F32)
    words = jax.ShapeDtypeStruct((TURNS * HB + 16, BF), jnp.int16)
    return pl.pallas_call(
        merge_kernel,
        out_shape=[half, half, jax.ShapeDtypeStruct((8, BF), F32), words, words],
        in_specs=[VMEM] * 3,
        out_specs=[VMEM] * 5,
        compiler_params=limit(4),
        name="merge",
    )(mine, sent, theirs)


def place_kernel(upper, lower, rest, near, far, blank, out, blocks, sems):
    del blank
    row_id, col_id, _ = position()
    shift = (col_id - row_id) & (N_COL - 1)

    def part(ref, turn):
        return ref[pl.ds(pl.multiple_of(turn * HB, HB), HB), :]

    ahead = (row_id & (KB - 1)) < col_id

    def coded(from_near, turn):
        code = jnp.where(from_near, near[TURNS * HB :, :].astype(F32), far[TURNS * HB :, :].astype(F32))
        words = jnp.where(from_near, part(near, turn).astype(F32), part(far, turn).astype(F32))
        return decode(words, pick_row(code, turn))

    def write(t, low, at):
        slot = TURNS * low + t
        return pltpu.make_async_copy(blocks.at[slot], out.at[t, at], sems.at[slot])

    for finish in (False, True):
        for t in range(TURNS):
            at = (row_id + N_ROW * t + shift) >> 3

            @pl.when((shift > 0) & (at < N_COL))
            def _():
                if finish:
                    write(t, 0, at).wait()
                else:
                    turn = t + jnp.where(row_id + shift >= N_ROW, 1, 0)
                    blocks[t, :HB, :] = part(upper, t)
                    blocks[t, HB:, :] = coded(ahead, jnp.minimum(turn, TURNS - 1))
                    write(t, 0, at).start()

            @pl.when((shift > 0) & (at > 0))
            def _():
                if finish:
                    write(t, 1, at - 1).wait()
                else:
                    turn = t - jnp.where(row_id + shift < N_COL, 1, 0)
                    top = coded(jnp.logical_not(ahead), jnp.maximum(turn, 0))
                    blocks[TURNS + t] = jnp.concatenate([top, part(lower, t)], axis=0).T
                    write(t, 1, at - 1).start()

            @pl.when(shift == 0)
            def _():
                if finish:
                    write(t, 0, at).wait()
                else:
                    blocks[t] = unpack_symmetric(part(upper, t), rest[t : t + 1, :])
                    write(t, 0, at).start()


def place(upper, lower, rest, near, far, blank):
    return pl.pallas_call(
        place_kernel,
        out_shape=jax.ShapeDtypeStruct((TURNS, N_COL, BF, BF), F32),
        in_specs=[VMEM] * 5 + [HBM],
        out_specs=HBM,
        scratch_shapes=[
            pltpu.VMEM((2 * TURNS, BF, BF), F32),
            pltpu.SemaphoreType.DMA((2 * TURNS,)),
        ],
        input_output_aliases={5: 0},
        compiler_params=limit(4),
        name="place",
    )(upper, lower, rest, near, far, blank)


def mirror_pairs(across):
    pairs = []
    for row in range(N_ROW):
        for col in range(N_COL):
            half = (row // KB) ^ across
            pairs.append((row * N_COL + col, (half * KB + col) * N_COL + row % KB))
    return pairs


def exchange(parts):
    return lax.all_to_all(parts, ALL, 0, 0, axis_index_groups=GROUPS, tiled=True)


def shards(density, basis, weights, batch_start, batch_count):
    swap = [(0, 1), (1, 0)]
    held, sent = share(density)
    theirs = lax.ppermute(sent, "h", swap)
    table = route(batch_start, batch_count)
    packed = pack(table, held, theirs)
    window = exchange(packed)

    outgoing = batches(table, weights, turn(table, basis), window)
    arrived = exchange(outgoing)

    sent = collect(1, table, arrived)
    theirs = lax.ppermute(sent, "h", swap)
    mine, blank = collect(0, table, arrived)
    upper, lower, rest, near, far = merge(mine, sent, theirs)
    near = lax.ppermute(near, ALL, mirror_pairs(0))
    far = lax.ppermute(far, ALL, mirror_pairs(1))
    potential = place(upper, lower, rest, near, far, blank)
    return potential, rest[TURNS, 0] / (NBLK * BF)


def solution(mesh):
    fine = Mesh(np.asarray(mesh.devices).reshape(2, 2, 4, 4, 2), ALL)
    in_specs = (P(ROW, COL), P(ALL), P(ALL), P(), P())
    out_specs = (P(ROW, COL), P())
    return jax.shard_map(shards, mesh=fine, in_specs=in_specs, out_specs=out_specs, check_vma=False)
```
